32 devices in a mesh: narrow: 8 (over y, x, core), wide: 4 (over z).
Axes of the slice: x: 2, y: 2, z: 4, core: 2. Of those that a mesh axis runs over, the one named last changes fastest.
Arguments:
- feat_p2: float32 [4, 256, 64, 64], P('wide', 'narrow'), may hold values from -6 to 6
- feat_p3: float32 [4, 256, 32, 32], P('wide', 'narrow'), may hold values from -6 to 6
- feat_p4: float32 [4, 256, 16, 16], P('wide', 'narrow'), may hold values from -6 to 6
- feat_p5: float32 [4, 256, 8, 8], P('wide', 'narrow'), may hold values from -6 to 6
- rois: int32 [2, 4, 512, 4], P(None, 'wide'), may hold values from 0 to 256, as said below
- levels: int32 [2, 4, 512], P(None, 'wide'), may hold values from 0 to 3
- labels: int32 [2, 4, 512], P(None, 'wide'), may hold values from 0 to 80
- sampled: int32 [2, 4, 512], P(None, 'wide'), may hold values from 0 to 1
- targets: float32 [2, 4, 512, 4], P(None, 'wide'), may hold values from -6 to 6
- fc1_w: float32 [2, 12544, 1024], P(None, 'narrow'), may hold values from -0.078125 to 0.078125
- fc1_m: float32 [2, 12544, 1024], P(None, 'narrow'), may hold values from -0.09375 to 0.09375
- fc1_v: float32 [2, 12544, 1024], P(None, 'narrow'), may hold values from 2.4414063e-05 to 0.0001953125
- fc2_w: float32 [2, 1024, 1024], P(None, 'narrow'), may hold values from -0.1875 to 0.1875
- fc2_m: float32 [2, 1024, 1024], P(None, 'narrow'), may hold values from -0.09375 to 0.09375
- fc2_v: float32 [2, 1024, 1024], P(None, 'narrow'), may hold values from 2.4414063e-05 to 0.0001953125
- head_w: float32 [2, 1024, 401], P(None, 'narrow'), may hold values from -0.5 to 0.5
- head_m: float32 [2, 1024, 401], P(None, 'narrow'), may hold values from -0.09375 to 0.09375
- head_v: float32 [2, 1024, 401], P(None, 'narrow'), may hold values from 2.4414063e-05 to 0.0001953125
Outputs:
- loss_parts: float32 [2], replicated
- fc1_new: float32 [2, 12544, 1024], P(None, 'narrow')
- fc1_moment: float32 [2, 12544, 1024], P(None, 'narrow')
- fc1_second: float32 [2, 12544, 1024], P(None, 'narrow')
- fc2_new: float32 [2, 1024, 1024], P(None, 'narrow')
- fc2_moment: float32 [2, 1024, 1024], P(None, 'narrow')
- fc2_second: float32 [2, 1024, 1024], P(None, 'narrow')
- head_new: float32 [2, 1024, 401], P(None, 'narrow')
- head_moment: float32 [2, 1024, 401], P(None, 'narrow')
- head_second: float32 [2, 1024, 401], P(None, 'narrow')
The draws below stay inside these ranges and needn't reach their ends.
Inputs may be any that keep to these rules, and one draw needn't show every extreme that they name: `rois`: integer boxes inside an image of 256 pixels, at least 4 cells wide on their level.
All inputs are finite; a program needn't handle non-finite values.
Results may differ from the reference program's by a relative error of at most 0.0008.
Values may be sent and summed in bfloat16 or wider, within the bound.
A program may use at most 448 MiB of HBM per device.

```python
import math
import jax
import jax.numpy as jnp
from jax import lax

CHANNELS = 256
HIDDEN_SIZE = 1024
CLASSES = 81
HEAD = 401
FC1_IN = 12544
MAP = 64
STEP = 5
IMG_DEV = 1
ROI_IMG = 512
IMAGES = 4


def level_draw(key):
    raw = jax.random.randint(jax.random.fold_in(key, 11), (2, IMAGES, ROI_IMG), 0, 10)
    return ((raw >= 6).astype(jnp.int32) + (raw >= 8).astype(jnp.int32) + (raw >= 9).astype(jnp.int32)).astype(jnp.int32)


def draw_levels(key, part):
    return level_draw(key)


def draw_rois(key, part):
    levels = level_draw(key)
    image_side = 4 * MAP
    lowest = MAP // 4 * jnp.power(2, levels).astype(jnp.int32)
    highest = jnp.minimum(3 * lowest, image_side)
    bits = jax.random.randint(jax.random.fold_in(key, 12), (4, 2, IMAGES, ROI_IMG), 0, 2 ** 20)
    width = lowest + bits[0] % (highest - lowest + 1)
    height = lowest + bits[1] % (highest - lowest + 1)
    left = bits[2] % (image_side - width + 1)
    top = bits[3] % (image_side - height + 1)
    return jnp.stack([left, top, left + width, top + height], axis=-1).astype(jnp.int32)


def draw_sampled(key, part):
    rows = jnp.arange(IMAGES * ROI_IMG, dtype=jnp.int32)
    block_rows = IMG_DEV * ROI_IMG
    blocks = IMAGES // IMG_DEV
    chance = 150 + 350 * (rows // block_rows) // max(blocks - 1, 1) + 350 * (rows % block_rows) // block_rows
    draws = jax.random.randint(key, (2, IMAGES * ROI_IMG), 0, 1000)
    return (draws < chance[None, :]).astype(jnp.int32).reshape(2, IMAGES, ROI_IMG)


def place_ends(values, own_key, smallest, top_value):
    longest = values.shape.index(max(values.shape))
    spots = []
    for shift in (0, 1):
        where = [jax.random.randint(jax.random.fold_in(own_key, axis), (), 0, length) for axis, length in enumerate(values.shape)]
        where[longest] = (where[longest] + shift) % values.shape[longest]
        spots.append(tuple(where))
    return values.at[spots[0]].set(smallest).at[spots[1]].set(top_value)


def level_of(key, shape, cuts, smallest, high):
    gain, own = 1.0, jax.random.fold_in(key, 6)
    for axis_at, shards_of in cuts:
        steps = jnp.exp(jax.random.uniform(jax.random.fold_in(own, axis_at), (shards_of,), jnp.float32, smallest / len(cuts), high / len(cuts)))
        gain = gain * jnp.repeat(steps, shape[axis_at] // shards_of).reshape([-1 if axis == axis_at else 1 for axis in range(len(shape))])
    return gain


def noise(stream_key, shape, scale, reach, split=(), held_as=jnp.bfloat16):
    entries = scale * jax.random.normal(stream_key, shape, jnp.float32)
    if split:
        entries = entries * level_of(stream_key, shape, split, -0.22, 0.18)
    return jnp.clip(entries, -reach, reach).astype(held_as)


def setup_inputs(seed: int = 0) -> dict:
    seeds = jax.random.split(jax.random.key(seed), 19)
    feat_p2 = noise(seeds[0], (IMAGES, CHANNELS, MAP, MAP), 1.0, 6.0, ((0, 4), (1, 8)), jnp.float32)
    feat_p3 = noise(seeds[1], (IMAGES, CHANNELS, MAP // 2, MAP // 2), 1.0, 6.0, ((0, 4), (1, 8)), jnp.float32)
    feat_p4 = noise(seeds[2], (IMAGES, CHANNELS, MAP // 4, MAP // 4), 1.0, 6.0, ((0, 4), (1, 8)), jnp.float32)
    feat_p5 = noise(seeds[3], (IMAGES, CHANNELS, MAP // 8, MAP // 8), 1.0, 6.0, ((0, 4), (1, 8)), jnp.float32)
    rois = draw_rois(jax.random.fold_in(seeds[18], 71), 0)
    levels = draw_levels(jax.random.fold_in(seeds[18], 71), 0)
    labels = place_ends(jax.random.randint(seeds[6], (2, IMAGES, ROI_IMG), 0, CLASSES), jax.random.fold_in(seeds[6], 1), 0, CLASSES - 1).astype(jnp.int32)
    sampled = draw_sampled(jax.random.fold_in(seeds[18], 71), 0)
    targets = noise(seeds[8], (2, IMAGES, ROI_IMG, 4), 1.0, 6.0, ((1, 4),), jnp.float32)
    fc1_w = noise(seeds[9], (2, FC1_IN, HIDDEN_SIZE), (FC1_IN // 2) ** -0.5, 0.078125, ((1, 8),), jnp.float32)
    fc1_m = noise(seeds[10], (2, FC1_IN, HIDDEN_SIZE), (0.3 * (IMAGES * ROI_IMG) ** -0.5), 0.09375, ((1, 8),), jnp.float32)
    fc1_v = jnp.clip(jnp.exp(math.log(0.0001953125) - 2.0794415 * jax.random.uniform(seeds[11], (2, FC1_IN, HIDDEN_SIZE), jnp.float32) ** level_of(seeds[11], (2, FC1_IN, HIDDEN_SIZE), ((1, 8),), -0.2, 0.2)), 2.441406286379788e-05, 0.0001953125)
    fc2_w = noise(seeds[12], (2, HIDDEN_SIZE, HIDDEN_SIZE), HIDDEN_SIZE ** -0.5, 0.1875, ((1, 8),), jnp.float32)
    fc2_m = noise(seeds[13], (2, HIDDEN_SIZE, HIDDEN_SIZE), (0.3 * (IMAGES * ROI_IMG) ** -0.5), 0.09375, ((1, 8),), jnp.float32)
    fc2_v = jnp.clip(jnp.exp(math.log(0.0001953125) - 2.0794415 * jax.random.uniform(seeds[14], (2, HIDDEN_SIZE, HIDDEN_SIZE), jnp.float32) ** level_of(seeds[14], (2, HIDDEN_SIZE, HIDDEN_SIZE), ((1, 8),), -0.2, 0.2)), 2.441406286379788e-05, 0.0001953125)
    head_w = noise(seeds[15], (2, HIDDEN_SIZE, HEAD), (HIDDEN_SIZE // 8) ** -0.5, 0.5, ((1, 8),), jnp.float32)
    head_m = noise(seeds[16], (2, HIDDEN_SIZE, HEAD), (0.3 * (IMAGES * ROI_IMG) ** -0.5), 0.09375, ((1, 8),), jnp.float32)
    head_v = jnp.clip(jnp.exp(math.log(0.0001953125) - 2.0794415 * jax.random.uniform(seeds[17], (2, HIDDEN_SIZE, HEAD), jnp.float32) ** level_of(seeds[17], (2, HIDDEN_SIZE, HEAD), ((1, 8),), -0.2, 0.2)), 2.441406286379788e-05, 0.0001953125)
    return dict(feat_p2=feat_p2, feat_p3=feat_p3, feat_p4=feat_p4, feat_p5=feat_p5, rois=rois, levels=levels, labels=labels, sampled=sampled, targets=targets, fc1_w=fc1_w, fc1_m=fc1_m, fc1_v=fc1_v, fc2_w=fc2_w, fc2_m=fc2_m, fc2_v=fc2_v, head_w=head_w, head_m=head_m, head_v=head_v)


BETA_ONE = 0.5
BETA_TWO = 0.5
RATE = 0.02
DECAY = 0.01
EPSILON = 1e-08
HIGH = lax.Precision.HIGHEST

@jax.custom_vjp
def low(v):
    return lax.optimization_barrier(v.astype(jnp.bfloat16)).astype(jnp.float32)

@jax.custom_vjp
def low_back(v):
    return v

def low_keep(v):
    return (low(v), None)

def low_pass(kept, grad):
    return (grad,)

def back_keep(v):
    return (v, None)

def back_low(kept, grad):
    return (low(grad),)
low.defvjp(low_keep, low_pass)
low_back.defvjp(back_keep, back_low)

def tent_rows(start, length, side):
    bins = jnp.arange(7, dtype=jnp.float32)
    offsets = jnp.array([0.25, 0.75], jnp.float32)
    where = start[:, None, None] + (bins[None, :, None] + offsets[None, None, :]) * (length / 7.0)[:, None, None]
    where = jnp.clip(where, 0.0, side - 1.0)
    cells = jnp.arange(side, dtype=jnp.float32)
    weight = jnp.maximum(0.0, 1.0 - jnp.abs(where[..., None] - cells))
    return lax.optimization_barrier(jnp.mean(weight, axis=2))

def roi_pool(maps, boxes, levels):
    total = None
    corners = boxes.astype(jnp.float32)
    for level in range(4):
        fmap = maps[level]
        side = fmap.shape[1]
        scale = 1.0 / (4.0 * 2 ** level)
        pick = (levels == level).astype(jnp.float32)
        row_weights = tent_rows(corners[:, 1] * scale - 0.5, (corners[:, 3] - corners[:, 1]) * scale, side) * pick[:, None, None]
        col_weights = tent_rows(corners[:, 0] * scale - 0.5, (corners[:, 2] - corners[:, 0]) * scale, side)
        part = jnp.einsum('rih,chw->rciw', row_weights, fmap, precision=HIGH)
        part = jnp.einsum('rciw,rjw->rcij', part, col_weights, precision=HIGH)
        total = part if total is None else total + part
    return total.reshape(total.shape[0], -1)

def row_loss(logits, labels, sampled, targets):
    cls = logits[:, :CLASSES]
    box = logits[:, CLASSES:].reshape(logits.shape[0], CLASSES - 1, 4)
    top = lax.optimization_barrier(jnp.max(cls, axis=1, keepdims=True))
    lse = top[:, 0] + jnp.log(lax.optimization_barrier(jnp.sum(jnp.exp(cls - top), axis=1)))
    onehot = (labels[:, None] == jnp.arange(CLASSES)[None, :]).astype(jnp.float32)
    picked = lax.optimization_barrier(jnp.sum(cls * onehot, axis=1))
    weight = sampled.astype(jnp.float32)
    fore = onehot[:, 1:] * weight[:, None]
    chosen = jnp.einsum('rk,rkj->rj', fore, box, precision=HIGH)
    differ = chosen - targets * lax.optimization_barrier(jnp.sum(fore, axis=1, keepdims=True))
    huber = jnp.where(jnp.abs(differ) < 1.0, 0.5 * differ * differ, jnp.abs(differ) - 0.5)
    return jnp.sum(weight * (lse - picked)) + jnp.sum(huber)

def pass_total(w_one, w_two, w_head, maps, boxes, levels, labels, sampled, targets):
    w1b, w2b, whb = (low(w_one), low(w_two), low(w_head))

    def one_image(total, items):
        fmaps, box, lev, lab, samp, tgt = items
        pooled = low(roi_pool(fmaps, box, lev))
        pre1 = low_back(jnp.dot(pooled, w1b, precision=HIGH))
        hid1 = low(jax.nn.silu(pre1))
        pre2 = low_back(jnp.dot(hid1, w2b, precision=HIGH))
        hid2 = low(jax.nn.silu(pre2))
        logits = low_back(jnp.dot(hid2, whb, precision=HIGH))
        return (total + row_loss(logits, lab, samp, tgt), None)
    start = jnp.zeros((), jnp.float32)
    total, _ = lax.scan(jax.checkpoint(one_image), start, (maps, boxes, levels, labels, sampled, targets))
    return total

def adamw(weight, moment, second, grad):
    moment = BETA_ONE * moment + (1.0 - BETA_ONE) * grad
    second = BETA_TWO * second + (1.0 - BETA_TWO) * grad * grad
    fixed_m = moment / (1.0 - BETA_ONE ** STEP)
    fixed_v = second / (1.0 - BETA_TWO ** STEP)
    weight = weight - RATE * (fixed_m / (jnp.sqrt(fixed_v) + EPSILON) + DECAY * weight)
    return (weight, moment, second)

def reference(feat_p2, feat_p3, feat_p4, feat_p5, rois, levels, labels, sampled, targets, fc1_w, fc1_m, fc1_v, fc2_w, fc2_m, fc2_v, head_w, head_m, head_v):
    maps = (feat_p2, feat_p3, feat_p4, feat_p5)
    count = jnp.sum(sampled).astype(jnp.float32)

    def loss_of(weights):
        w_one, w_two, w_head = weights
        total = jnp.zeros((), jnp.float32)
        for index in range(2):
            total = total + pass_total(w_one[index], w_two[index], w_head[index], maps, rois[index], levels[index], labels[index], sampled[index], targets[index])
        return total
    total, pull = jax.vjp(loss_of, (fc1_w, fc2_w, head_w))
    grads = pull(jnp.ones((), jnp.float32) / count)[0]
    new1 = adamw(fc1_w, fc1_m, fc1_v, grads[0])
    new2 = adamw(fc2_w, fc2_m, fc2_v, grads[1])
    newh = adamw(head_w, head_m, head_v, grads[2])
    return (jnp.stack([total, count]), new1[0], new1[1], new1[2], new2[0], new2[1], new2[2], newh[0], newh[1], newh[2])
```

```python
from functools import partial

import jax
import jax.numpy as jnp
from jax import lax
from jax.experimental import pallas as pl
from jax.experimental.pallas import tpu as pltpu
from jax.sharding import PartitionSpec as P

CLASSES = 81
STEP = 5
BETA_ONE = 0.5
BETA_TWO = 0.5
RATE = 0.02
DECAY = 0.01
EPSILON = 1e-08
BINS = 7
CHUNK = 8
LANES = 128
MIB = 2**20


def tent(where, cells):
    return 0.5 * sum(jnp.maximum(0.0, 1.0 - jnp.abs(w - cells)) for w in where)


def pool_kernel(channels, side, span_ref, feat_ref, param_ref, out_ref, cols_ref, rows_ref, acc_ref, line_ref):
    step_id = pl.program_id(0)
    half = LANES // 2
    for group in range(2):
        y_start, y_step, top, base, x_start, x_step = (
            param_ref[group, k : k + 1, :] for k in range(6)
        )
        cells = lax.broadcasted_iota(jnp.int32, (side, LANES), 0).astype(jnp.float32)
        for j in range(BINS):
            where = [jnp.clip(x_start + (j + off) * x_step, 0.0, top) for off in (0.25, 0.75)]
            weight = tent(where, cells)
            high = weight.astype(jnp.bfloat16)
            low = (weight - high.astype(jnp.float32)).astype(jnp.bfloat16)
            lanes = pl.ds(j * LANES, LANES)
            cols_ref[0:side, lanes] = high
            cols_ref[side : 2 * side, lanes] = high
            cols_ref[2 * side : 3 * side, lanes] = low
            cols_ref[3 * side : 4 * side, lanes] = low
        acc_ref[...] = jnp.zeros_like(acc_ref)
        bins = lax.broadcasted_iota(jnp.int32, (8, LANES), 0).astype(jnp.float32)
        y_where = [jnp.clip(y_start + (bins + off) * y_step, 0.0, top) for off in (0.25, 0.75)]
        first = span_ref[(step_id * 2 + group) * 2]
        chunks = span_ref[(step_id * 2 + group) * 2 + 1]

        @pl.loop(0, chunks)
        def _(t):
            row = first + t * CHUNK
            for h in range(CHUNK):
                rows_ref[h] = tent(y_where, (row + h).astype(jnp.float32) - base)
            left = feat_ref[0, pl.ds(pl.multiple_of(row * channels, channels), CHUNK * channels), :]
            left = jnp.concatenate([left, left], axis=1)
            for j0 in range(0, BINS, 2):
                width = min(2, BINS - j0)
                part = jnp.dot(
                    left,
                    cols_ref[:, j0 * LANES : (j0 + width) * LANES],
                    preferred_element_type=jnp.float32,
                )
                for j in range(j0, j0 + width):
                    mine = part[:, (j - j0) * LANES : (j - j0 + 1) * LANES]
                    for i in range(BINS):
                        total = acc_ref[i * BINS + j]
                        for h in range(CHUNK):
                            total = total + rows_ref[h, i : i + 1, :] * mine[h * channels : (h + 1) * channels]
                        acc_ref[i * BINS + j] = total

        for ij in range(BINS * BINS):
            line_ref[group, pl.ds(ij, channels, stride=BINS * BINS), :] = acc_ref[ij]
    a, b = line_ref[0], line_ref[1]
    lanes = lax.broadcasted_iota(jnp.int32, a.shape, 1)
    out_ref[0] = jnp.where(lanes < half, a, pltpu.roll(b, half, 1)).astype(jnp.bfloat16)
    out_ref[1] = jnp.where(lanes < half, pltpu.roll(a, half, 1), b).astype(jnp.bfloat16)


def pool(feat, table, spans, shift, images, channels):
    total, height, depth = feat.shape
    blocks = table.shape[1]
    wide = channels * BINS * BINS
    side = depth // 2

    def kernel(order_ref, span_ref, *refs):
        pool_kernel(channels, side, span_ref, *refs)

    order = lax.rem(shift + jnp.arange(images, dtype=jnp.int32), total)
    spans = jnp.take(spans.reshape(total, -1), order, axis=0).reshape(-1)
    steps = images * blocks
    return pl.pallas_call(
        kernel,
        out_shape=jax.ShapeDtypeStruct((2, wide, steps * LANES), jnp.bfloat16),
        grid_spec=pltpu.PrefetchScalarGridSpec(
            num_scalar_prefetch=2,
            grid=(steps,),
            in_specs=[
                pl.BlockSpec((1, height, depth), lambda s, order, spans: (order[s // blocks], 0, 0)),
                pl.BlockSpec(
                    (None, None, 2, 8, LANES),
                    lambda s, order, spans: (order[s // blocks], lax.rem(s, blocks), 0, 0, 0),
                ),
            ],
            out_specs=pl.BlockSpec((2, wide, LANES), lambda s, order, spans: (0, 0, s)),
            scratch_shapes=[
                pltpu.VMEM((2 * depth, BINS * LANES), jnp.bfloat16),
                pltpu.VMEM((CHUNK, 8, LANES), jnp.float32),
                pltpu.VMEM((BINS * BINS, channels, LANES), jnp.float32),
                pltpu.VMEM((2, wide, LANES), jnp.float32),
            ],
        ),
        compiler_params=pltpu.CompilerParams(vmem_limit_bytes=40 * MIB),
        cost_estimate=pl.CostEstimate(
            flops=steps * 2 * 30 * channels * BINS * LANES * 4 * depth,
            bytes_accessed=steps * wide * LANES * 4,
            transcendentals=0,
        ),
        name="pool_rois",
    )(order, spans, feat, table)


def feature_rows(maps):
    side = maps[0].shape[-1]
    parts = [
        jnp.pad(m.transpose(0, 2, 1, 3), ((0, 0), (0, 0), (0, 0), (0, side - m.shape[-1])))
        for m in maps
    ]
    full = jnp.concatenate(parts, axis=1)
    high = lax.reduce_precision(full, 8, 7)
    low = (full - high).astype(jnp.bfloat16)
    full = jnp.concatenate([high.astype(jnp.bfloat16), low], axis=-1)
    return full.reshape(full.shape[0], -1, 2 * side)


def box_order(boxes, levels, side):
    base = 2 * side - 2 * (side >> levels)
    key = ((boxes[..., 1] + boxes[..., 3]) >> levels) + base * 8
    key = key * key.shape[-1] + jnp.arange(key.shape[-1], dtype=jnp.int32)
    return jnp.sum((key[..., :, None] > key[..., None, :]).astype(jnp.int32), axis=-1)


def box_table(boxes, levels, rank, side):
    count = boxes.shape[1]
    hot = (rank[:, None, :] == jnp.arange(count, dtype=jnp.int32)[:, None]).astype(jnp.bfloat16)
    both = jnp.concatenate([boxes, levels[..., None]], axis=-1).astype(jnp.bfloat16)
    both = jnp.einsum("psr,prk->kps", hot, both, preferred_element_type=jnp.float32)
    level = both[4]
    scale = jnp.where(level < 0.5, 0.25, jnp.where(level < 1.5, 0.125, jnp.where(level < 2.5, 0.0625, 0.03125)))
    height = scale * (4 * side)
    base = 2.0 * side - 2.0 * height
    top = height - 1.0
    rows = sum(side >> k for k in range(4))

    def axis(low, high):
        return low * scale - 0.5, ((high - low) * scale) / 7.0

    x_start, x_step = axis(both[0], both[2])
    y_start, y_step = axis(both[1], both[3])
    low = base + jnp.floor(jnp.clip(y_start, 0.0, top))
    high = base + jnp.floor(jnp.clip(y_start + 7.0 * y_step, 0.0, top)) + 1.0
    half = LANES // 2

    def split(v):
        return v.reshape(2, count // half, half)

    low = jnp.min(split(low), axis=(0, 2), keepdims=True)
    high = jnp.minimum(jnp.max(split(high), axis=(0, 2), keepdims=True), rows - 1.0)
    chunks = jnp.floor((high - low + CHUNK) / CHUNK)
    first = jnp.maximum(jnp.minimum(low, rows - chunks * CHUNK), 0.0)
    parts = [split(v) for v in (y_start, y_step, top, base, x_start, x_step)]
    parts += [jnp.broadcast_to(v, parts[0].shape) for v in (first, chunks)]
    return jnp.stack(parts).transpose(2, 0, 1, 3).reshape(count // LANES, 2, 8, LANES)


def adamw(weight, moment, second, grad):
    moment = BETA_ONE * moment + (1.0 - BETA_ONE) * grad
    second = BETA_TWO * second + (1.0 - BETA_TWO) * grad * grad
    fixed_m = moment / (1.0 - BETA_ONE**STEP)
    fixed_v = second / (1.0 - BETA_TWO**STEP)
    weight = weight - RATE * (fixed_m / (jnp.sqrt(fixed_v) + EPSILON) + DECAY * weight)
    return (weight, moment, second)


def update_kernel(images, boxes, me_ref, own_ref, other_ref, back_ref, w_ref, m_ref, v_ref, *outs):
    me = me_ref[0]

    def rows(k):
        image = lax.rem(me + k, images)
        return back_ref[pl.ds(pl.multiple_of(image * boxes, boxes), boxes), :]

    grad = jnp.dot(own_ref[...], rows(0), preferred_element_type=jnp.float32)
    for k in range(1, images):
        grad += jnp.dot(
            other_ref[:, (k - 1) * boxes : k * boxes], rows(k), preferred_element_type=jnp.float32
        )
    new = adamw(w_ref[...], m_ref[...], v_ref[...], grad)
    for ref, value in zip(outs, new):
        ref[...] = value


def update_first(me, own, other, back, weight, moment, second):
    passes, wide, hidden = weight.shape
    boxes = own.shape[2]
    images = back.shape[1] // boxes
    block = wide // BINS
    big = pl.BlockSpec((None, block, hidden), lambda p, b, me: (p, b, 0))
    return pl.pallas_call(
        partial(update_kernel, images, boxes),
        out_shape=[jax.ShapeDtypeStruct(weight.shape, jnp.float32)] * 3,
        grid_spec=pltpu.PrefetchScalarGridSpec(
            num_scalar_prefetch=1,
            grid=(passes, BINS),
            in_specs=[
                pl.BlockSpec((None, block, boxes), lambda p, b, me: (p, b, 0)),
                pl.BlockSpec((None, block, (images - 1) * boxes), lambda p, b, me: (p, b, 0)),
                pl.BlockSpec(
                    (None, images * boxes, hidden), lambda p, b, me: (p, 0, 0), pipeline_mode=pl.Buffered(1)
                ),
                big,
                big,
                big,
            ],
            out_specs=[big] * 3,
        ),
        compiler_params=pltpu.CompilerParams(vmem_limit_bytes=56 * MIB),
        cost_estimate=pl.CostEstimate(
            flops=2 * passes * wide * hidden * images * boxes,
            bytes_accessed=passes * wide * hidden * 24 + passes * images * boxes * (wide + hidden) * 2,
            transcendentals=passes * wide * hidden,
        ),
        name="update_first",
    )(me, own, other, back, weight, moment, second)


def silu_slope(value):
    sig = jax.nn.sigmoid(value)
    return sig * (1.0 + value * (1.0 - sig))


def loss_and_slope(logits, labels, sampled, targets, count):
    place = lax.broadcasted_iota(jnp.int32, logits.shape, 1)
    is_class = place < CLASSES
    weight = sampled.astype(jnp.float32)[:, None]
    label = labels[:, None]
    top = jnp.max(jnp.where(is_class, logits, -jnp.inf), axis=1, keepdims=True)
    grown = jnp.where(is_class, jnp.exp(jnp.where(is_class, logits - top, 0.0)), 0.0)
    norm = jnp.sum(grown, axis=1, keepdims=True)
    hot = place == label
    picked = jnp.sum(jnp.where(hot, logits, 0.0), axis=1, keepdims=True)
    fore = jnp.where(label > 0, weight, 0.0)
    total = jnp.sum(weight * (top + jnp.log(norm) - picked))
    slope = weight * (grown / norm - hot.astype(jnp.float32))
    for k in range(4):
        mask = place == CLASSES + 4 * (label - 1) + k
        mask = mask & (label > 0)
        chosen = fore * jnp.sum(jnp.where(mask, logits, 0.0), axis=1, keepdims=True)
        differ = chosen - fore * targets[:, k : k + 1]
        total += jnp.sum(jnp.where(jnp.abs(differ) < 1.0, 0.5 * differ * differ, jnp.abs(differ) - 0.5) * fore)
        slope = jnp.where(mask, fore * jnp.clip(differ, -1.0, 1.0), slope)
    return total, slope * (1.0 / count)


def per_device(
    feat_p2, feat_p3, feat_p4, feat_p5, rois, levels, labels, sampled, targets,
    fc1_w, fc1_m, fc1_v, fc2_w, fc2_m, fc2_v, head_w, head_m, head_v,
):
    side = feat_p2.shape[-1]
    channels = feat_p2.shape[1]
    boxes = rois.shape[2]
    images = lax.axis_size("wide")
    mine = boxes // lax.axis_size("narrow")
    first = lax.axis_index("narrow") * mine
    me = lax.axis_index("wide").astype(jnp.int32)
    feat = feature_rows((feat_p2, feat_p3, feat_p4, feat_p5))
    rank = box_order(rois[:, 0], levels[:, 0], side)
    table = box_table(rois[:, 0], levels[:, 0], rank, side)
    feats = lax.all_gather(feat, "wide", axis=0, tiled=True)
    tables = lax.all_gather(table, "wide", axis=0)
    w2 = lax.all_gather(fc2_w.astype(jnp.bfloat16), "narrow", axis=1, tiled=True)
    wh = lax.all_gather(head_w.astype(jnp.bfloat16), "narrow", axis=1, tiled=True)
    count = lax.psum(jnp.sum(sampled).astype(jnp.float32), "wide")

    def spans_of(t):
        return t[..., 6:8, 0].reshape(-1).astype(jnp.int32)

    zero = jnp.zeros((), jnp.int32)
    own = pool(feat, table[None], spans_of(table), zero, 1, channels)
    w1 = fc1_w.astype(jnp.bfloat16)
    part = lax.dot_general(own, w1, (((1,), (1,)), ((0,), (0,))), preferred_element_type=jnp.float32)
    pre1 = lax.psum_scatter(part, "narrow", scatter_dimension=1, tiled=True)
    other = pool(feats, tables, spans_of(tables), me + 1, images - 1, channels)

    hot = rank[:, None, :] == first + jnp.arange(mine, dtype=jnp.int32)[:, None]

    def pick(values):
        return jnp.sum(jnp.where(hot, values[:, 0][:, None, :], 0), axis=-1).reshape(-1)

    lab, samp = pick(labels), pick(sampled)
    tgt = jnp.stack([pick(targets[..., k]) for k in range(4)], axis=-1)

    def rows_by(left, right, dims):
        return lax.dot_general(left, right, (dims, ((0,), (0,))), preferred_element_type=jnp.float32)

    hid1 = jax.nn.silu(pre1).astype(jnp.bfloat16)
    pre2 = rows_by(hid1, w2, ((2,), (1,)))
    hid2 = jax.nn.silu(pre2).astype(jnp.bfloat16)
    logits = rows_by(hid2, wh, ((2,), (1,)))
    total, slope = loss_and_slope(logits.reshape(-1, logits.shape[-1]), lab, samp, tgt, count)
    back_z = slope.reshape(logits.shape).astype(jnp.bfloat16)
    back_h2 = rows_by(back_z, wh, ((2,), (2,)))
    back_p2 = (back_h2 * silu_slope(pre2)).astype(jnp.bfloat16)
    back_h1 = rows_by(back_p2, w2, ((2,), (2,)))
    back_p1 = (back_h1 * silu_slope(pre1)).astype(jnp.bfloat16)
    back = lax.all_gather(back_p1, ("wide", "narrow"), axis=1, tiled=True)
    grad_head = rows_by(hid2, back_z, ((1,), (1,)))
    grad_two = rows_by(hid1, back_p2, ((1,), (1,)))
    grad_two = lax.psum_scatter(grad_two, "narrow", scatter_dimension=1, tiled=True)
    grad_head = lax.psum_scatter(grad_head, "narrow", scatter_dimension=1, tiled=True)
    grad_two, grad_head = lax.psum((grad_two, grad_head), "wide")
    total = lax.psum(total, ("narrow", "wide"))
    new1 = update_first(me[None], own, other, back, fc1_w, fc1_m, fc1_v)
    new2 = adamw(fc2_w, fc2_m, fc2_v, grad_two)
    newh = adamw(head_w, head_m, head_v, grad_head)
    return (jnp.stack([total, count]),) + tuple(new1) + tuple(new2) + tuple(newh)


def solution(mesh):
    maps = P("wide", "narrow", None, None)
    rows = P(None, "narrow", None)
    box = P(None, "wide", None)
    coords = P(None, "wide", None, None)
    return jax.shard_map(
        per_device,
        mesh=mesh,
        in_specs=(maps,) * 4 + (coords, box, box, box, coords) + (rows,) * 9,
        out_specs=(P(),) + (rows,) * 9,
        check_vma=False,
    )
```

```python
from functools import partial

import jax
import jax.numpy as jnp
from jax import lax
from jax.experimental import pallas as pl
from jax.experimental.pallas import tpu as pltpu
from jax.sharding import PartitionSpec as P

CLASSES = 81
STEP = 5
BETA_ONE = 0.5
BETA_TWO = 0.5
RATE = 0.02
DECAY = 0.01
EPSILON = 1e-08
BINS = 7
CHUNK = 8
LANES = 128
MIB = 2**20


def tent(where, cells):
    return 0.5 * sum(jnp.maximum(0.0, 1.0 - jnp.abs(w - cells)) for w in where)


def pool_kernel(channels, side, span_ref, feat_ref, param_ref, out_ref, cols_ref, rows_ref, acc_ref, line_ref):
    step_id = pl.program_id(0)
    half = LANES // 2
    for group in range(2):
        y_start, y_step, top, base, x_start, x_step = (
            param_ref[group, k : k + 1, :] for k in range(6)
        )
        cells = lax.broadcasted_iota(jnp.int32, (side, LANES), 0).astype(jnp.float32)
        for j in range(BINS):
            where = [jnp.clip(x_start + (j + off) * x_step, 0.0, top) for off in (0.25, 0.75)]
            weight = tent(where, cells)
            high = weight.astype(jnp.bfloat16)
            low = (weight - high.astype(jnp.float32)).astype(jnp.bfloat16)
            lanes = pl.ds(j * LANES, LANES)
            cols_ref[0:side, lanes] = high
            cols_ref[side : 2 * side, lanes] = high
            cols_ref[2 * side : 3 * side, lanes] = low
            cols_ref[3 * side : 4 * side, lanes] = low
        acc_ref[...] = jnp.zeros_like(acc_ref)
        bins = lax.broadcasted_iota(jnp.int32, (8, LANES), 0).astype(jnp.float32)
        y_where = [jnp.clip(y_start + (bins + off) * y_step, 0.0, top) for off in (0.25, 0.75)]
        first = span_ref[(step_id * 2 + group) * 2]
        chunks = span_ref[(step_id * 2 + group) * 2 + 1]

        @pl.loop(0, chunks)
        def _(t):
            row = first + t * CHUNK
            for h in range(CHUNK):
                rows_ref[h] = tent(y_where, (row + h).astype(jnp.float32) - base)
            left = feat_ref[0, pl.ds(pl.multiple_of(row * channels, channels), CHUNK * channels), :]
            left = jnp.concatenate([left, left], axis=1)
            for j0 in range(0, BINS, 2):
                width = min(2, BINS - j0)
                part = jnp.dot(
                    left,
                    cols_ref[:, j0 * LANES : (j0 + width) * LANES],
                    preferred_element_type=jnp.float32,
                )
                for j in range(j0, j0 + width):
                    mine = part[:, (j - j0) * LANES : (j - j0 + 1) * LANES]
                    for i in range(BINS):
                        total = acc_ref[i * BINS + j]
                        for h in range(CHUNK):
                            total = total + rows_ref[h, i : i + 1, :] * mine[h * channels : (h + 1) * channels]
                        acc_ref[i * BINS + j] = total

        for ij in range(BINS * BINS):
            line_ref[group, pl.ds(ij, channels, stride=BINS * BINS), :] = acc_ref[ij]
    a, b = line_ref[0], line_ref[1]
    lanes = lax.broadcasted_iota(jnp.int32, a.shape, 1)
    out_ref[0] = jnp.where(lanes < half, a, pltpu.roll(b, half, 1)).astype(jnp.bfloat16)
    out_ref[1] = jnp.where(lanes < half, pltpu.roll(a, half, 1), b).astype(jnp.bfloat16)


def pool(feat, table, spans, shift, images, channels):
    total, height, depth = feat.shape
    blocks = table.shape[1]
    wide = channels * BINS * BINS
    side = depth // 2

    def kernel(order_ref, span_ref, *refs):
        pool_kernel(channels, side, span_ref, *refs)

    order = lax.rem(shift + jnp.arange(images, dtype=jnp.int32), total)
    spans = jnp.take(spans.reshape(total, -1), order, axis=0).reshape(-1)
    steps = images * blocks
    return pl.pallas_call(
        kernel,
        out_shape=jax.ShapeDtypeStruct((2, wide, steps * LANES), jnp.bfloat16),
        grid_spec=pltpu.PrefetchScalarGridSpec(
            num_scalar_prefetch=2,
            grid=(steps,),
            in_specs=[
                pl.BlockSpec((1, height, depth), lambda s, order, spans: (order[s // blocks], 0, 0)),
                pl.BlockSpec(
                    (None, None, 2, 8, LANES),
                    lambda s, order, spans: (order[s // blocks], lax.rem(s, blocks), 0, 0, 0),
                ),
            ],
            out_specs=pl.BlockSpec((2, wide, LANES), lambda s, order, spans: (0, 0, s)),
            scratch_shapes=[
                pltpu.VMEM((2 * depth, BINS * LANES), jnp.bfloat16),
                pltpu.VMEM((CHUNK, 8, LANES), jnp.float32),
                pltpu.VMEM((BINS * BINS, channels, LANES), jnp.float32),
                pltpu.VMEM((2, wide, LANES), jnp.float32),
            ],
        ),
        compiler_params=pltpu.CompilerParams(vmem_limit_bytes=40 * MIB),
        cost_estimate=pl.CostEstimate(
            flops=steps * 2 * 30 * channels * BINS * LANES * 4 * depth,
            bytes_accessed=steps * wide * LANES * 4,
            transcendentals=0,
        ),
        name="pool_rois",
    )(order, spans, feat, table)


def feature_rows(maps):
    side = maps[0].shape[-1]
    parts = [
        jnp.pad(m.transpose(0, 2, 1, 3), ((0, 0), (0, 0), (0, 0), (0, side - m.shape[-1])))
        for m in maps
    ]
    full = jnp.concatenate(parts, axis=1)
    high = lax.reduce_precision(full, 8, 7)
    low = (full - high).astype(jnp.bfloat16)
    full = jnp.concatenate([high.astype(jnp.bfloat16), low], axis=-1)
    return full.reshape(full.shape[0], -1, 2 * side)


def box_order(boxes, levels, side):
    base = 2 * side - 2 * (side >> levels)
    key = ((boxes[..., 1] + boxes[..., 3]) >> levels) + base * 8
    key = key * key.shape[-1] + jnp.arange(key.shape[-1], dtype=jnp.int32)
    return jnp.sum((key[..., :, None] > key[..., None, :]).astype(jnp.int32), axis=-1)


def box_table(boxes, levels, rank, side, sampled):
    count = boxes.shape[1]
    hot = (rank[:, None, :] == jnp.arange(count, dtype=jnp.int32)[:, None]).astype(jnp.bfloat16)
    both = jnp.concatenate([boxes, levels[..., None]], axis=-1).astype(jnp.bfloat16)
    both = jnp.einsum("psr,prk->kps", hot, both, preferred_element_type=jnp.float32)
    level = both[4]
    scale = jnp.where(level < 0.5, 0.25, jnp.where(level < 1.5, 0.125, jnp.where(level < 2.5, 0.0625, 0.03125)))
    height = scale * (4 * side)
    base = 2.0 * side - 2.0 * height
    top = height - 1.0
    rows = sum(side >> k for k in range(4))

    def axis(low, high):
        return low * scale - 0.5, ((high - low) * scale) / 7.0

    x_start, x_step = axis(both[0], both[2])
    y_start, y_step = axis(both[1], both[3])
    low = base + jnp.floor(jnp.clip(y_start, 0.0, top))
    high = base + jnp.floor(jnp.clip(y_start + 7.0 * y_step, 0.0, top)) + 1.0
    half = LANES // 2

    def split(v):
        return v.reshape(2, count // half, half)

    low = jnp.min(split(low), axis=(0, 2), keepdims=True)
    high = jnp.minimum(jnp.max(split(high), axis=(0, 2), keepdims=True), rows - 1.0)
    chunks = jnp.floor((high - low + CHUNK) / CHUNK)
    first = jnp.maximum(jnp.minimum(low, rows - chunks * CHUNK), 0.0)
    parts = [split(v) for v in (y_start, y_step, top, base, x_start, x_step)]
    lane = jnp.arange(half, dtype=jnp.int32)
    first = jnp.where(lane == 1, jnp.sum(sampled).astype(jnp.float32), first)
    parts += [jnp.broadcast_to(v, parts[0].shape) for v in (first, chunks)]
    return jnp.stack(parts).transpose(2, 0, 1, 3).reshape(count // LANES, 2, 8, LANES)


def adamw(weight, moment, second, grad):
    moment = BETA_ONE * moment + (1.0 - BETA_ONE) * grad
    second = BETA_TWO * second + (1.0 - BETA_TWO) * grad * grad
    fixed_m = moment / (1.0 - BETA_ONE**STEP)
    fixed_v = second / (1.0 - BETA_TWO**STEP)
    weight = weight - RATE * (fixed_m / (jnp.sqrt(fixed_v) + EPSILON) + DECAY * weight)
    return (weight, moment, second)


def update_kernel(images, boxes, me_ref, own_ref, other_ref, back_ref, w_ref, m_ref, v_ref, *outs):
    me = me_ref[0]

    def rows(k):
        image = lax.rem(me + k, images)
        return back_ref[pl.ds(pl.multiple_of(image * boxes, boxes), boxes), :]

    grad = jnp.dot(own_ref[...], rows(0), preferred_element_type=jnp.float32)
    for k in range(1, images):
        grad += jnp.dot(
            other_ref[:, (k - 1) * boxes : k * boxes], rows(k), preferred_element_type=jnp.float32
        )
    new = adamw(w_ref[...], m_ref[...], v_ref[...], grad)
    for ref, value in zip(outs, new):
        ref[...] = value


def update_first(me, own, other, back, weight, moment, second):
    passes, wide, hidden = weight.shape
    boxes = own.shape[2]
    images = back.shape[1] // boxes
    block = wide // BINS
    big = pl.BlockSpec((None, block, hidden), lambda p, b, me: (p, b, 0))
    return pl.pallas_call(
        partial(update_kernel, images, boxes),
        out_shape=[jax.ShapeDtypeStruct(weight.shape, jnp.float32)] * 3,
        grid_spec=pltpu.PrefetchScalarGridSpec(
            num_scalar_prefetch=1,
            grid=(passes, BINS),
            in_specs=[
                pl.BlockSpec((None, block, boxes), lambda p, b, me: (p, b, 0)),
                pl.BlockSpec((None, block, (images - 1) * boxes), lambda p, b, me: (p, b, 0)),
                pl.BlockSpec(
                    (None, images * boxes, hidden), lambda p, b, me: (p, 0, 0), pipeline_mode=pl.Buffered(1)
                ),
                big,
                big,
                big,
            ],
            out_specs=[big] * 3,
        ),
        compiler_params=pltpu.CompilerParams(vmem_limit_bytes=56 * MIB),
        cost_estimate=pl.CostEstimate(
            flops=2 * passes * wide * hidden * images * boxes,
            bytes_accessed=passes * wide * hidden * 24 + passes * images * boxes * (wide + hidden) * 2,
            transcendentals=passes * wide * hidden,
        ),
        name="update_first",
    )(me, own, other, back, weight, moment, second)


def loss_and_slope(logits, box, count):
    place = lax.broadcasted_iota(jnp.int32, logits.shape, 1)
    is_class = place < CLASSES
    label = box[:, 0:1].astype(jnp.int32)
    weight = box[:, 1:2]
    top = jnp.max(jnp.where(is_class, logits, -jnp.inf), axis=1, keepdims=True)
    grown = jnp.where(is_class, jnp.exp(jnp.where(is_class, logits - top, 0.0)), 0.0)
    norm = jnp.sum(grown, axis=1, keepdims=True)
    hot = place == label
    picked = jnp.sum(jnp.where(hot, logits, 0.0), axis=1, keepdims=True)
    fore = jnp.where(label > 0, weight, 0.0)
    rows = weight * (top + jnp.log(norm) - picked)
    slope = weight * (grown / norm - jnp.where(hot, 1.0, 0.0))
    offset = place - (CLASSES + 4 * (label - 1))
    for k in range(4):
        mask = (offset == k) & (place >= CLASSES)
        chosen = jnp.sum(jnp.where(mask, logits, 0.0), axis=1, keepdims=True)
        differ = fore * (chosen - box[:, 2 + k : 3 + k])
        near = jnp.abs(differ)
        rows += jnp.where(near < 1.0, 0.5 * differ * differ, near - 0.5) * fore
        slope = jnp.where(mask, fore * jnp.clip(differ, -1.0, 1.0), slope)
    return rows, slope / count


def sigmoid(value):
    return 1.0 / (1.0 + jnp.exp(-value))


def head_kernel(
    images, parts, mine,
    part_ref, w2_ref, wh_ref, box_ref, count_ref,
    back_ref, hid1_ref, hid2_ref, slope2_ref, slopez_ref, loss_ref,
    sums, landed, own, rs_send, rs_recv, ag_send, ag_recv, up_send, up_recv, down_send, down_recv, own_sem,
):
    me = lax.axis_index("narrow")
    level = lax.axis_index("wide")
    bits = parts.bit_length() - 1
    turn = [(1 - 2 * ((me // 2**k) % 2)) * 2**k for k in range(bits)]

    def peer(mask):
        return me + sum((turn[k] for k in range(bits) if mask >> k & 1), 0)

    links = list(range(1, bits))
    orders = [links, links[::-1]]

    barrier = pltpu.get_barrier_semaphore()
    for k in range(bits):
        pl.semaphore_signal(barrier, inc=1, device_id={"narrow": peer(1 << k)})

    @pl.when(level > 0)
    def _():
        pl.semaphore_signal(barrier, inc=1, device_id={"wide": level - 1})

    @pl.when(level < images - 1)
    def _():
        pl.semaphore_signal(barrier, inc=1, device_id={"wide": level + 1})

    ends = jnp.where(level > 0, 1, 0) + jnp.where(level < images - 1, 1, 0)
    pl.semaphore_wait(barrier, bits + ends)

    def scatter(p, mask, bit, source):
        return pltpu.make_async_remote_copy(
            src_ref=source,
            dst_ref=landed.at[p, mask],
            send_sem=rs_send.at[p, mask],
            recv_sem=rs_recv.at[p, mask],
            device_id={"narrow": peer(1 << bit)},
        )

    def part_at(p, mask):
        return part_ref.at[p, pl.ds(pl.multiple_of(peer(mask) * mine, mine), mine), :]

    copies = {}
    for p in range(2):
        for mask in range(1, parts, 2):
            copies[p, mask] = scatter(p, mask, 0, part_at(p, mask))
            copies[p, mask].start()

    def stage(p, at):
        order = [0] + orders[p]
        bit = order[at - 1]
        seen = sum(1 << b for b in order[:at])
        for mask in range(parts):
            if mask & seen:
                continue
            copies[p, mask | 1 << bit].wait_recv()
            if at == 1:
                have = part_ref[p, pl.ds(pl.multiple_of(peer(mask) * mine, mine), mine), :]
            else:
                have = sums[p, mask]
            sums[p, mask] = have + landed[p, mask | 1 << bit]
            if at < bits and mask >> order[at] & 1:
                copies[p, mask] = scatter(p, mask, order[at], sums.at[p, mask])
                copies[p, mask].start()

    for at in range(1, bits):
        for p in range(2):
            stage(p, at)

    def rows(p, image, mask):
        place = (image * parts + peer(mask)) * mine
        return back_ref.at[p, pl.ds(pl.multiple_of(place, mine), mine), :]

    def spread(p, image, mask, bit, source=None):
        spot = rows(p, image, mask)
        there = mask | 1 << bit
        return pltpu.make_async_remote_copy(
            src_ref=spot if source is None else source,
            dst_ref=spot,
            send_sem=ag_send.at[p, image, there],
            recv_sem=ag_recv.at[p, image, there],
            device_id={"narrow": peer(1 << bit)},
        )

    def arrive(p, image, mask):
        spot = rows(p, image, mask)
        pltpu.make_async_remote_copy(
            src_ref=spot, dst_ref=spot, send_sem=ag_send.at[p, image, mask],
            recv_sem=ag_recv.at[p, image, mask], device_id={"narrow": peer(1)},
        ).wait_recv()

    def hop(p, d, up, source=None):
        image = level - d if up else level + d
        spot = rows(p, image, 0)
        return pltpu.make_async_remote_copy(
            src_ref=spot if source is None else source,
            dst_ref=spot,
            send_sem=(up_send if up else down_send).at[p, d],
            recv_sem=(up_recv if up else down_recv).at[p, d],
            device_id={"wide": level + 1 if up else level - 1},
        )

    def came(p, d, up):
        image = level - d if up else level + d
        spot = rows(p, image, 0)
        pltpu.make_async_remote_copy(
            src_ref=spot, dst_ref=spot, send_sem=(up_send if up else down_send).at[p, d],
            recv_sem=(up_recv if up else down_recv).at[p, d - 1],
            device_id={"wide": level - 1 if up else level + 1},
        ).wait_recv()

    steps = [orders[p] + [0] for p in range(2)]

    def masks_before(p, at):
        seen = sum(1 << b for b in steps[p][:at])
        return [m for m in range(parts) if not m & ~seen]

    def advance(p, image, at, source=None):
        bit = steps[p][at]
        if at:
            last = steps[p][at - 1]
            for m in masks_before(p, at - 1):
                arrive(p, image, m | 1 << last)
        for m in masks_before(p, at):
            spread(p, image, m, bit, source if m == 0 else None).start()

    def finish(p, image):
        last = steps[p][-1]
        for m in masks_before(p, bits - 1):
            arrive(p, image, m | 1 << last)
        for at in range(bits):
            for m in masks_before(p, at):
                spread(p, image, m, steps[p][at]).wait_send()

    count = count_ref[0:1, 0:1]
    for p in range(2):
        stage(p, bits)
        pre1 = sums[p, 0]
        sig1 = sigmoid(pre1)
        hid1 = (pre1 * sig1).astype(jnp.bfloat16)
        pre2 = jnp.dot(hid1, w2_ref[p], preferred_element_type=jnp.float32)
        sig2 = sigmoid(pre2)
        hid2 = (pre2 * sig2).astype(jnp.bfloat16)
        logits = jnp.dot(hid2, wh_ref[p], preferred_element_type=jnp.float32)
        loss, slope = loss_and_slope(logits, box_ref[p], count)
        loss_ref[p] = jnp.broadcast_to(loss, loss_ref.shape[1:])
        back_z = slope.astype(jnp.bfloat16)
        turned = (((1,), (1,)), ((), ()))
        back_h2 = lax.dot_general(back_z, wh_ref[p], turned, preferred_element_type=jnp.float32)
        back_p2 = (back_h2 * (sig2 * (1.0 + pre2 * (1.0 - sig2)))).astype(jnp.bfloat16)
        back_h1 = lax.dot_general(back_p2, w2_ref[p], turned, preferred_element_type=jnp.float32)
        own[p] = (back_h1 * (sig1 * (1.0 + pre1 * (1.0 - sig1)))).astype(jnp.bfloat16)

        @pl.when(level < images - 1)
        def _():
            hop(p, 0, True, own.at[p]).start()

        @pl.when(level > 0)
        def _():
            hop(p, 0, False, own.at[p]).start()

        advance(p, level, 0, own.at[p])
        pltpu.make_async_copy(own.at[p], rows(p, level, 0), own_sem.at[p]).start()
        hid1_ref[p] = hid1
        hid2_ref[p] = hid2
        slope2_ref[p] = back_p2
        slopez_ref[p] = back_z
    for p in range(2):
        pltpu.make_async_copy(own.at[p], rows(p, level, 0), own_sem.at[p]).wait()

    def each_side(d, do):
        @pl.when(level >= d)
        def _():
            do(level - d, True)

        @pl.when(level + d < images)
        def _():
            do(level + d, False)

    def enter(d):
        def do(image, up):
            for p in range(2):
                came(p, d, up)

                @pl.when((level < images - 1) if up else (level > 0))
                def _():
                    hop(p, d, up).start()

                advance(p, image, 0)

        each_side(d, do)

    def go_on(d, at):
        if d == 0:
            for p in range(2):
                advance(p, level, at)
        else:

            def do(image, up):
                for p in range(2):
                    advance(p, image, at)

            each_side(d, do)

    for tick in range(1, images + bits - 1):
        for d in range(images):
            at = tick - d
            if at == 0:
                enter(d)
            elif 0 < at < bits:
                go_on(d, at)

    for p in range(2):
        finish(p, level)

        @pl.when(level < images - 1)
        def _():
            hop(p, 0, True).wait_send()

        @pl.when(level > 0)
        def _():
            hop(p, 0, False).wait_send()

    for d in range(1, images):

        def do(image, up):
            for p in range(2):
                finish(p, image)

                @pl.when((level < images - 1) if up else (level > 0))
                def _():
                    hop(p, d, up).wait_send()

        each_side(d, do)
    for p in range(2):
        for mask in range(1, parts):
            copies[p, mask].wait_send()


def head_step(part, w2, wh, box, count, images, parts):
    passes, boxes, hidden = part.shape
    mine = boxes // parts
    outs = wh.shape[2]
    low = jnp.bfloat16
    vmem = pl.BlockSpec(memory_space=pltpu.VMEM)
    dma = pltpu.SemaphoreType.DMA
    return pl.pallas_call(
        partial(head_kernel, images, parts, mine),
        out_shape=[
            jax.ShapeDtypeStruct((passes, images * boxes, hidden), low),
            jax.ShapeDtypeStruct((passes, mine, hidden), low),
            jax.ShapeDtypeStruct((passes, mine, hidden), low),
            jax.ShapeDtypeStruct((passes, mine, hidden), low),
            jax.ShapeDtypeStruct((passes, mine, outs), low),
            jax.ShapeDtypeStruct((passes, mine, LANES), jnp.float32),
        ],
        in_specs=[vmem] * 5,
        out_specs=[pl.BlockSpec(memory_space=pl.ANY)] + [vmem] * 5,
        scratch_shapes=[
            pltpu.VMEM((passes, parts, mine, hidden), jnp.float32),
            pltpu.VMEM((passes, parts, mine, hidden), jnp.float32),
            pltpu.VMEM((passes, mine, hidden), low),
            dma((passes, parts)),
            dma((passes, parts)),
            dma((passes, images, parts)),
            dma((passes, images, parts)),
            dma((passes, images)),
            dma((passes, images)),
            dma((passes, images)),
            dma((passes, images)),
            dma((passes,)),
        ],
        compiler_params=pltpu.CompilerParams(
            vmem_limit_bytes=48 * MIB, collective_id=0, has_side_effects=True
        ),
        cost_estimate=pl.CostEstimate(
            flops=8 * passes * mine * hidden * (hidden + outs),
            bytes_accessed=100 * MIB,
            transcendentals=4 * passes * mine * hidden,
        ),
        name="head_step",
    )(part, w2, wh, box, count)


def per_device(
    feat_p2, feat_p3, feat_p4, feat_p5, rois, levels, labels, sampled, targets,
    fc1_w, fc1_m, fc1_v, fc2_w, fc2_m, fc2_v, head_w, head_m, head_v,
):
    side = feat_p2.shape[-1]
    channels = feat_p2.shape[1]
    boxes = rois.shape[2]
    images = lax.axis_size("wide")
    mine = boxes // lax.axis_size("narrow")
    first = lax.axis_index("narrow") * mine
    me = lax.axis_index("wide").astype(jnp.int32)
    feat = feature_rows((feat_p2, feat_p3, feat_p4, feat_p5))
    rank = box_order(rois[:, 0], levels[:, 0], side)
    table = box_table(rois[:, 0], levels[:, 0], rank, side, sampled)
    feats = lax.all_gather(feat, "wide", axis=0, tiled=True)
    tables = lax.all_gather(table, "wide", axis=0)
    outs = head_w.shape[2]
    w2 = lax.all_gather(fc2_w.astype(jnp.bfloat16), "narrow", axis=1, tiled=True)
    wide_head = jnp.pad(head_w, ((0, 0), (0, 0), (0, -outs % LANES))).astype(jnp.bfloat16)
    wh = lax.all_gather(wide_head, "narrow", axis=1, tiled=True)
    count = jnp.sum(tables[:, 0, 0, 6, 1])

    def spans_of(t):
        return t[..., 6:8, 0].reshape(-1).astype(jnp.int32)

    zero = jnp.zeros((), jnp.int32)
    own = pool(feat, table[None], spans_of(table), zero, 1, channels)
    w1 = fc1_w.astype(jnp.bfloat16)
    part = lax.dot_general(own, w1, (((1,), (1,)), ((0,), (0,))), preferred_element_type=jnp.float32)
    hot = rank[:, None, :] == first + jnp.arange(mine, dtype=jnp.int32)[:, None]

    def pick(values):
        return jnp.sum(jnp.where(hot, values[:, 0].astype(jnp.float32)[:, None, :], 0), axis=-1)

    box = [pick(labels), pick(sampled)] + [pick(targets[..., k]) for k in range(4)]
    box = jnp.pad(jnp.stack(box, axis=-1), ((0, 0), (0, 0), (0, LANES - 6)))
    back, hid1, hid2, back_p2, back_z, loss = head_step(
        part, w2, wh, box, jnp.full((8, LANES), count), images, boxes // mine
    )
    other = pool(feats, tables, spans_of(tables), me + 1, images - 1, channels)

    def rows_by(left, right):
        return lax.dot_general(left, right, (((1,), (1,)), ((0,), (0,))), preferred_element_type=jnp.float32)

    def over_all(grad):
        grad = lax.psum_scatter(grad, "narrow", scatter_dimension=1, tiled=True)
        grad = lax.psum_scatter(grad, "wide", scatter_dimension=1, tiled=True)
        return lax.all_gather(grad, "wide", axis=1, tiled=True)

    grad_two = over_all(rows_by(hid1, back_p2))
    grad_head = over_all(rows_by(hid2, back_z))[..., :outs]
    total = jnp.sum(lax.all_gather(jnp.sum(loss[:, :, 0]).reshape(1, 1), ("wide", "narrow"), axis=0, tiled=True))
    new1 = update_first(me[None], own, other, back, fc1_w, fc1_m, fc1_v)
    new2 = adamw(fc2_w, fc2_m, fc2_v, grad_two)
    newh = adamw(head_w, head_m, head_v, grad_head)
    return (jnp.stack([total, count]),) + tuple(new1) + tuple(new2) + tuple(newh)


def solution(mesh):
    maps = P("wide", "narrow", None, None)
    rows = P(None, "narrow", None)
    box = P(None, "wide", None)
    coords = P(None, "wide", None, None)
    return jax.shard_map(
        per_device,
        mesh=mesh,
        in_specs=(maps,) * 4 + (coords, box, box, box, coords) + (rows,) * 9,
        out_specs=(P(),) + (rows,) * 9,
        check_vma=False,
    )
```

```python
from functools import partial

import jax
import jax.numpy as jnp
from jax import lax
from jax.experimental import pallas as pl
from jax.experimental.pallas import tpu as pltpu
from jax.sharding import PartitionSpec as P

CLASSES = 81
STEP = 5
BETA_ONE = 0.5
BETA_TWO = 0.5
RATE = 0.02
DECAY = 0.01
EPSILON = 1e-08
BINS = 7
CHUNK = 8
STATIC = 5
WINDOW = 24
MORE = 4
SPANS = 17
LANES = 128
MIB = 2**20


def tent(where, cells):
    return 0.5 * sum(jnp.maximum(0.0, 1.0 - jnp.abs(w - cells)) for w in where)


def pool_kernel(channels, side, groups, copies, pick_ref, span_ref, feat_ref, table_ref, *refs):
    out_refs = refs[-7 - copies : -7]
    cols, rows, parts = refs[-7:-5], refs[-5:-3], refs[-3:-1]
    line_ref = refs[-1]
    image = pick_ref[0]
    half = LANES // 2
    offsets = (0.25, 0.75)
    cells = lax.broadcasted_iota(jnp.int32, (side, LANES), 0).astype(jnp.float32)
    bins = lax.broadcasted_iota(jnp.int32, (8, LANES), 0).astype(jnp.float32)

    def at(group):
        return (image * groups + group) * SPANS

    def param(group, k):
        return table_ref[group, k : k + 1, :]

    def weights(group, slot):
        top, x_start, x_step = param(group, 2), param(group, 4), param(group, 5)
        for j in range(BINS):
            where = [jnp.clip(x_start + (j + off) * x_step, 0.0, top) for off in offsets]
            weight = tent(where, cells)
            high = weight.astype(jnp.bfloat16)
            low = (weight - high.astype(jnp.float32)).astype(jnp.bfloat16)
            lanes = pl.ds(j * LANES, LANES)
            cols[slot][0:side, lanes] = high
            cols[slot][side : 2 * side, lanes] = high
            cols[slot][2 * side : 3 * side, lanes] = low
            cols[slot][3 * side : 4 * side, lanes] = low

    def fill(group, slot, row):
        y_start, y_step, top, base = (param(group, k) for k in range(4))
        where = [jnp.clip(y_start + (bins + off) * y_step, 0.0, top) for off in offsets]
        for h in range(CHUNK):
            rows[slot][row + h] = tent(where, (row + h).astype(jnp.float32) - base)
        place = pl.ds(pl.multiple_of(row * channels, channels), CHUNK * channels)
        left = feat_ref[place, :]
        left = jnp.concatenate([left, left], axis=1)
        parts[slot][place, :] = jnp.dot(left, cols[slot][...], preferred_element_type=jnp.float32)

    def rest(group, slot):
        first = span_ref[at(group)] + STATIC * CHUNK

        @pl.loop(0, span_ref[at(group) + 1])
        def _(t):
            fill(group, slot, first + t * CHUNK)

    def block(slot, i, low_row, count):
        accs = None
        for h in range(count):
            start = pl.multiple_of((low_row + h) * channels, channels)
            weight = jnp.broadcast_to(rows[slot][low_row + h, i : i + 1, :], (channels, LANES))
            new = [
                weight * parts[slot][pl.ds(start, channels), j * LANES : (j + 1) * LANES] for j in range(BINS)
            ]
            accs = new if accs is None else [x + y for x, y in zip(accs, new)]
        return accs

    def spot(i, j):
        return pl.ds(i * BINS + j, channels, stride=BINS * BINS)

    def work(group, slot, following):
        for i in range(BINS):
            accs = block(slot, i, span_ref[at(group) + 3 + i], WINDOW)
            for j in range(BINS):
                line_ref[slot, spot(i, j), :] = accs[j]
            if i < STATIC:
                fill(following, 1 - slot, span_ref[at(following)] + i * CHUNK)

        @pl.when(span_ref[at(group) + 2] > 0)
        def _():
            for i in range(BINS):
                low_row = span_ref[at(group) + 3 + i] + WINDOW

                @pl.loop(0, span_ref[at(group) + 3 + BINS + i])
                def _(t):
                    more = block(slot, i, low_row + t * MORE, MORE)
                    for j in range(BINS):
                        line_ref[slot, spot(i, j), :] = line_ref[slot, spot(i, j), :] + more[j]

    step = pl.program_id(0)

    @pl.when(step == 0)
    def _():
        weights(0, 0)
        for i in range(STATIC):
            fill(0, 0, span_ref[at(0)] + i * CHUNK)
        rest(0, 0)

    group = 2 * step
    weights(group + 1, 1)
    work(group, 0, group + 1)
    rest(group + 1, 1)
    following = jnp.minimum(group + 2, groups - 1)
    weights(following, 0)
    work(group + 1, 1, following)
    rest(following, 0)
    a, b = line_ref[0], line_ref[1]
    lanes = lax.broadcasted_iota(jnp.int32, a.shape, 1)
    new = [jnp.where(lanes < half, a, pltpu.roll(b, half, 1)), jnp.where(lanes < half, pltpu.roll(a, half, 1), b)]
    for out_ref in out_refs:
        for p in range(2):
            out_ref[p] = new[p].astype(jnp.bfloat16)


def pool(feat, table, spans, source, image, images, channels, buffer=None):
    depth = feat.shape[2]
    groups = table.shape[1]
    wide = channels * BINS * BINS
    side = depth // 2
    rows = sum(side >> k for k in range(4))
    boxes = groups * LANES // 2
    blocks = groups // 2
    pick = jnp.stack([source, image])
    out_shape = [jax.ShapeDtypeStruct((2, wide, images * boxes), jnp.bfloat16)]
    out_specs = [pl.BlockSpec((2, wide, LANES), lambda s, pick, spans: (0, 0, pick[1] * blocks + s))]
    in_specs = [
        pl.BlockSpec((None, rows * channels, depth), lambda s, pick, spans: (pick[0], 0, 0)),
        pl.BlockSpec((None, groups, 8, LANES), lambda s, pick, spans: (pick[0], 0, 0, 0)),
    ]
    operands = (pick, spans, feat, table)
    aliases = {}
    if buffer is None:
        out_shape.append(jax.ShapeDtypeStruct((2, wide, boxes), jnp.bfloat16))
        out_specs.append(pl.BlockSpec((2, wide, LANES), lambda s, pick, spans: (0, 0, s)))
    else:
        in_specs.append(pl.BlockSpec(memory_space=pl.ANY))
        operands += (buffer,)
        aliases = {4: 0}
    return pl.pallas_call(
        partial(pool_kernel, channels, side, groups, len(out_shape)),
        out_shape=out_shape,
        grid_spec=pltpu.PrefetchScalarGridSpec(
            num_scalar_prefetch=2,
            grid=(blocks,),
            in_specs=in_specs,
            out_specs=out_specs,
            scratch_shapes=[
                pltpu.VMEM((4 * side, BINS * LANES), jnp.bfloat16),
                pltpu.VMEM((4 * side, BINS * LANES), jnp.bfloat16),
                pltpu.VMEM((rows, 8, LANES), jnp.float32),
                pltpu.VMEM((rows, 8, LANES), jnp.float32),
                pltpu.VMEM((rows * channels, BINS * LANES), jnp.float32),
                pltpu.VMEM((rows * channels, BINS * LANES), jnp.float32),
                pltpu.VMEM((2, wide, LANES), jnp.float32),
            ],
        ),
        input_output_aliases=aliases,
        compiler_params=pltpu.CompilerParams(vmem_limit_bytes=44 * MIB),
        cost_estimate=pl.CostEstimate(
            flops=groups * 40 * channels * BINS * LANES * 8 * depth,
            bytes_accessed=80 * MIB,
            transcendentals=0,
        ),
        name="pool_rois",
    )(*operands)


def feature_rows(maps):
    side = maps[0].shape[-1]
    parts = [
        jnp.pad(m.transpose(0, 2, 1, 3), ((0, 0), (0, 0), (0, 0), (0, side - m.shape[-1])))
        for m in maps
    ]
    full = jnp.concatenate(parts, axis=1)
    high = lax.reduce_precision(full, 8, 7)
    low = (full - high).astype(jnp.bfloat16)
    full = jnp.concatenate([high.astype(jnp.bfloat16), low], axis=-1)
    return full.reshape(-1, 2 * side)


def box_order(boxes, levels, side):
    base = 2 * side - 2 * (side >> levels)
    key = ((boxes[..., 1] + boxes[..., 3]) >> levels) + base * 8
    key = key * key.shape[-1] + jnp.arange(key.shape[-1], dtype=jnp.int32)
    return jnp.sum((key[..., :, None] > key[..., None, :]).astype(jnp.int32), axis=-1)


def sort_boxes(boxes, levels, rank):
    count = boxes.shape[1]
    hot = (rank[:, None, :] == jnp.arange(count, dtype=jnp.int32)[:, None]).astype(jnp.bfloat16)
    both = jnp.concatenate([boxes, levels[..., None]], axis=-1).astype(jnp.bfloat16)
    return jnp.einsum("psr,prk->kps", hot, both, preferred_element_type=jnp.float32).astype(jnp.bfloat16)


def box_table(boxes, side):
    images, _, _, count = boxes.shape
    x0, y0, x1, y1, level = (boxes[:, k].astype(jnp.float32) for k in range(5))
    rows = sum(side >> k for k in range(4))
    scale = jnp.where(level < 0.5, 0.25, jnp.where(level < 1.5, 0.125, jnp.where(level < 2.5, 0.0625, 0.03125)))
    height = scale * (4 * side)
    base = 2.0 * side - 2.0 * height
    top = height - 1.0

    def axis(low, high):
        return low * scale - 0.5, ((high - low) * scale) / 7.0

    x_start, x_step = axis(x0, x1)
    y_start, y_step = axis(y0, y1)
    half = LANES // 2
    groups = count // half

    def split(v):
        return v.reshape(v.shape[:-1] + (groups, half))

    lows, highs = [], []
    for i in range(BINS):
        low = base + jnp.floor(jnp.clip(y_start + (i + 0.25) * y_step, 0.0, top))
        high = base + jnp.floor(jnp.clip(y_start + (i + 0.75) * y_step, 0.0, top)) + 1.0
        lows.append(jnp.min(split(low), axis=(1, 3)))
        highs.append(jnp.max(split(jnp.minimum(high, rows - 1.0)), axis=(1, 3)))
    low = jnp.stack(lows, axis=-1).astype(jnp.int32)
    high = jnp.stack(highs, axis=-1).astype(jnp.int32)
    least = jnp.min(low, axis=-1)
    chunks = jnp.maximum((jnp.max(high, axis=-1) - least + CHUNK) // CHUNK, STATIC)
    first = jnp.clip(rows - chunks * CHUNK, 0, least)
    extra = jnp.maximum(high - low + MORE - WINDOW, 0) // MORE
    low = jnp.minimum(low, (first + chunks * CHUNK)[..., None] - WINDOW - MORE * extra)
    heads = jnp.stack([first, chunks - STATIC, jnp.max(extra, axis=-1)], axis=-1)
    spans = jnp.concatenate([heads, low, extra], axis=-1).reshape(-1)
    zero = jnp.zeros_like(base)
    table = jnp.stack([split(v) for v in (y_start, y_step, top, base, x_start, x_step, zero, zero)])
    return table.transpose(1, 3, 0, 2, 4).reshape(images, groups, 8, LANES), spans


def adamw(weight, moment, second, grad):
    moment = BETA_ONE * moment + (1.0 - BETA_ONE) * grad
    second = BETA_TWO * second + (1.0 - BETA_TWO) * grad * grad
    fixed_m = moment / (1.0 - BETA_ONE**STEP)
    fixed_v = second / (1.0 - BETA_TWO**STEP)
    weight = weight - RATE * (fixed_m / (jnp.sqrt(fixed_v) + EPSILON) + DECAY * weight)
    return (weight, moment, second)


def update_kernel(pooled_ref, back_ref, w_ref, m_ref, v_ref, *outs):
    grad = jnp.dot(pooled_ref[...], back_ref[...], preferred_element_type=jnp.float32)
    new = adamw(w_ref[...], m_ref[...], v_ref[...], grad)
    for ref, value in zip(outs, new):
        ref[...] = value


def update_first(pooled, back, weight, moment, second):
    passes, wide, hidden = weight.shape
    boxes = pooled.shape[2]
    block = wide // BINS
    big = pl.BlockSpec((None, block, hidden), lambda p, b: (p, b, 0))
    return pl.pallas_call(
        update_kernel,
        out_shape=[jax.ShapeDtypeStruct(weight.shape, jnp.float32)] * 3,
        grid=(passes, BINS),
        in_specs=[
            pl.BlockSpec((None, block, boxes), lambda p, b: (p, b, 0)),
            pl.BlockSpec((None, boxes, hidden), lambda p, b: (p, 0, 0)),
            big,
            big,
            big,
        ],
        out_specs=[big] * 3,
        compiler_params=pltpu.CompilerParams(vmem_limit_bytes=56 * MIB),
        cost_estimate=pl.CostEstimate(
            flops=2 * passes * wide * hidden * boxes,
            bytes_accessed=passes * wide * hidden * 24 + passes * boxes * (wide + hidden) * 2,
            transcendentals=passes * wide * hidden,
        ),
        name="update_first",
    )(pooled, back, weight, moment, second)


def loss_and_slope(logits, box, count):
    place = lax.broadcasted_iota(jnp.int32, logits.shape, 1)
    is_class = place < CLASSES
    label = box[:, 0:1].astype(jnp.int32)
    weight = box[:, 1:2]
    top = jnp.max(jnp.where(is_class, logits, -jnp.inf), axis=1, keepdims=True)
    grown = jnp.where(is_class, jnp.exp(jnp.where(is_class, logits - top, 0.0)), 0.0)
    norm = jnp.sum(grown, axis=1, keepdims=True)
    hot = place == label
    picked = jnp.sum(jnp.where(hot, logits, 0.0), axis=1, keepdims=True)
    fore = jnp.where(label > 0, weight, 0.0)
    rows = weight * (top + jnp.log(norm) - picked)
    slope = weight * (grown / norm - jnp.where(hot, 1.0, 0.0))
    offset = place - (CLASSES + 4 * (label - 1))
    for k in range(4):
        mask = (offset == k) & (place >= CLASSES)
        chosen = jnp.sum(jnp.where(mask, logits, 0.0), axis=1, keepdims=True)
        differ = fore * (chosen - box[:, 2 + k : 3 + k])
        near = jnp.abs(differ)
        rows += jnp.where(near < 1.0, 0.5 * differ * differ, near - 0.5) * fore
        slope = jnp.where(mask, fore * jnp.clip(differ, -1.0, 1.0), slope)
    return rows, slope / count


def sigmoid(value):
    return 1.0 / (1.0 + jnp.exp(-value))


def head_kernel(
    images, parts, mine,
    part_ref, weight_ref, box_ref, count_ref,
    back_ref, kept_ref,
    sums, landed, own, rs_send, rs_recv, ag_send, ag_recv, up_send, up_recv, down_send, down_recv, own_sem,
):
    me = lax.axis_index("narrow")
    level = lax.axis_index("wide")
    bits = parts.bit_length() - 1
    turn = [(1 - 2 * ((me // 2**k) % 2)) * 2**k for k in range(bits)]

    def peer(mask):
        return me + sum((turn[k] for k in range(bits) if mask >> k & 1), 0)

    links = list(range(1, bits))
    orders = [links, links[::-1]]

    barrier = pltpu.get_barrier_semaphore()
    for k in range(bits):
        pl.semaphore_signal(barrier, inc=1, device_id={"narrow": peer(1 << k)})

    @pl.when(level > 0)
    def _():
        pl.semaphore_signal(barrier, inc=1, device_id={"wide": level - 1})

    @pl.when(level < images - 1)
    def _():
        pl.semaphore_signal(barrier, inc=1, device_id={"wide": level + 1})

    ends = jnp.where(level > 0, 1, 0) + jnp.where(level < images - 1, 1, 0)
    pl.semaphore_wait(barrier, bits + ends)

    def scatter(p, mask, bit, source):
        return pltpu.make_async_remote_copy(
            src_ref=source,
            dst_ref=landed.at[p, mask],
            send_sem=rs_send.at[p, mask],
            recv_sem=rs_recv.at[p, mask],
            device_id={"narrow": peer(1 << bit)},
        )

    def part_at(p, mask):
        return part_ref.at[p, pl.ds(pl.multiple_of(peer(mask) * mine, mine), mine), :]

    copies = {}
    for p in range(2):
        for mask in range(1, parts, 2):
            copies[p, mask] = scatter(p, mask, 0, part_at(p, mask))
            copies[p, mask].start()

    def stage(p, at):
        order = [0] + orders[p]
        bit = order[at - 1]
        seen = sum(1 << b for b in order[:at])
        for mask in range(parts):
            if mask & seen:
                continue
            copies[p, mask | 1 << bit].wait_recv()
            if at == 1:
                have = part_ref[p, pl.ds(pl.multiple_of(peer(mask) * mine, mine), mine), :]
            else:
                have = sums[p, mask]
            sums[p, mask] = have + landed[p, mask | 1 << bit]
            if at < bits and mask >> order[at] & 1:
                copies[p, mask] = scatter(p, mask, order[at], sums.at[p, mask])
                copies[p, mask].start()

    for at in range(1, bits):
        for p in range(2):
            stage(p, at)

    def rows(p, image, mask):
        place = (image * parts + peer(mask)) * mine
        return back_ref.at[p, pl.ds(pl.multiple_of(place, mine), mine), :]

    def spread(p, image, mask, bit, source=None):
        spot = rows(p, image, mask)
        there = mask | 1 << bit
        return pltpu.make_async_remote_copy(
            src_ref=spot if source is None else source,
            dst_ref=spot,
            send_sem=ag_send.at[p, image, there],
            recv_sem=ag_recv.at[p, image, there],
            device_id={"narrow": peer(1 << bit)},
        )

    def arrive(p, image, mask):
        spot = rows(p, image, mask)
        pltpu.make_async_remote_copy(
            src_ref=spot, dst_ref=spot, send_sem=ag_send.at[p, image, mask],
            recv_sem=ag_recv.at[p, image, mask], device_id={"narrow": peer(1)},
        ).wait_recv()

    def hop(p, d, up, source=None):
        image = level - d if up else level + d
        spot = rows(p, image, 0)
        return pltpu.make_async_remote_copy(
            src_ref=spot if source is None else source,
            dst_ref=spot,
            send_sem=(up_send if up else down_send).at[p, d],
            recv_sem=(up_recv if up else down_recv).at[p, d],
            device_id={"wide": level + 1 if up else level - 1},
        )

    def came(p, d, up):
        image = level - d if up else level + d
        spot = rows(p, image, 0)
        pltpu.make_async_remote_copy(
            src_ref=spot, dst_ref=spot, send_sem=(up_send if up else down_send).at[p, d],
            recv_sem=(up_recv if up else down_recv).at[p, d - 1],
            device_id={"wide": level - 1 if up else level + 1},
        ).wait_recv()

    steps = [orders[p] + [0] for p in range(2)]

    def masks_before(p, at):
        seen = sum(1 << b for b in steps[p][:at])
        return [m for m in range(parts) if not m & ~seen]

    def advance(p, image, at, source=None):
        bit = steps[p][at]
        if at:
            last = steps[p][at - 1]
            for m in masks_before(p, at - 1):
                arrive(p, image, m | 1 << last)
        for m in masks_before(p, at):
            spread(p, image, m, bit, source if m == 0 else None).start()

    def finish(p, image):
        last = steps[p][-1]
        for m in masks_before(p, bits - 1):
            arrive(p, image, m | 1 << last)
        for at in range(bits):
            for m in masks_before(p, at):
                spread(p, image, m, steps[p][at]).wait_send()

    count = count_ref[0:1, 0:1]
    hidden = part_ref.shape[2]
    for p in range(2):
        stage(p, bits)
        pre1 = sums[p, 0]
        sig1 = sigmoid(pre1)
        hid1 = (pre1 * sig1).astype(jnp.bfloat16)
        pre2 = jnp.dot(hid1, weight_ref[p, :, :hidden], preferred_element_type=jnp.float32)
        sig2 = sigmoid(pre2)
        hid2 = (pre2 * sig2).astype(jnp.bfloat16)
        logits = jnp.dot(hid2, weight_ref[p, :, hidden:], preferred_element_type=jnp.float32)
        loss, slope = loss_and_slope(logits, box_ref[p], count)
        back_z = slope.astype(jnp.bfloat16)
        turned = (((1,), (1,)), ((), ()))
        back_h2 = lax.dot_general(back_z, weight_ref[p, :, hidden:], turned, preferred_element_type=jnp.float32)
        back_p2 = (back_h2 * (sig2 * (1.0 + pre2 * (1.0 - sig2)))).astype(jnp.bfloat16)
        back_h1 = lax.dot_general(back_p2, weight_ref[p, :, :hidden], turned, preferred_element_type=jnp.float32)
        own[p] = (back_h1 * (sig1 * (1.0 + pre1 * (1.0 - sig1)))).astype(jnp.bfloat16)

        @pl.when(level < images - 1)
        def _():
            hop(p, 0, True, own.at[p]).start()

        @pl.when(level > 0)
        def _():
            hop(p, 0, False, own.at[p]).start()

        advance(p, level, 0, own.at[p])
        pltpu.make_async_copy(own.at[p], rows(p, level, 0), own_sem.at[p]).start()
        place = lax.broadcasted_iota(jnp.int32, (mine, LANES), 1)
        losses = jnp.zeros((mine, LANES), jnp.float32)
        for k in range(3):
            near = loss.astype(jnp.bfloat16).astype(jnp.float32)
            losses = jnp.where(place == k, near, losses)
            loss = loss - near
        at = 0
        for value in (hid1, hid2, back_p2, back_z, losses.astype(jnp.bfloat16)):
            kept_ref[p, :, at : at + value.shape[1]] = value
            at += value.shape[1]
    for p in range(2):
        pltpu.make_async_copy(own.at[p], rows(p, level, 0), own_sem.at[p]).wait()

    def each_side(d, do):
        @pl.when(level >= d)
        def _():
            do(level - d, True)

        @pl.when(level + d < images)
        def _():
            do(level + d, False)

    def enter(d):
        def do(image, up):
            for p in range(2):
                came(p, d, up)

                @pl.when((level < images - 1) if up else (level > 0))
                def _():
                    hop(p, d, up).start()

                advance(p, image, 0)

        each_side(d, do)

    def go_on(d, at):
        if d == 0:
            for p in range(2):
                advance(p, level, at)
        else:

            def do(image, up):
                for p in range(2):
                    advance(p, image, at)

            each_side(d, do)

    for tick in range(1, images + bits - 1):
        for d in range(images):
            at = tick - d
            if at == 0:
                enter(d)
            elif 0 < at < bits:
                go_on(d, at)

    for p in range(2):
        finish(p, level)

        @pl.when(level < images - 1)
        def _():
            hop(p, 0, True).wait_send()

        @pl.when(level > 0)
        def _():
            hop(p, 0, False).wait_send()

    for d in range(1, images):

        def do(image, up):
            for p in range(2):
                finish(p, image)

                @pl.when((level < images - 1) if up else (level > 0))
                def _():
                    hop(p, d, up).wait_send()

        each_side(d, do)
    for p in range(2):
        for mask in range(1, parts):
            copies[p, mask].wait_send()


def head_step(part, weight, box, count, images, parts):
    passes, boxes, hidden = part.shape
    mine = boxes // parts
    outs = weight.shape[2] - hidden
    low = jnp.bfloat16
    vmem = pl.BlockSpec(memory_space=pltpu.VMEM)
    dma = pltpu.SemaphoreType.DMA
    return pl.pallas_call(
        partial(head_kernel, images, parts, mine),
        out_shape=[
            jax.ShapeDtypeStruct((passes, images * boxes, hidden), low),
            jax.ShapeDtypeStruct((passes, mine, 3 * hidden + outs + LANES), low),
        ],
        in_specs=[vmem] * 4,
        out_specs=[pl.BlockSpec(memory_space=pl.ANY), vmem],
        scratch_shapes=[
            pltpu.VMEM((passes, parts, mine, hidden), jnp.float32),
            pltpu.VMEM((passes, parts, mine, hidden), jnp.float32),
            pltpu.VMEM((passes, mine, hidden), low),
            dma((passes, parts)),
            dma((passes, parts)),
            dma((passes, images, parts)),
            dma((passes, images, parts)),
            dma((passes, images)),
            dma((passes, images)),
            dma((passes, images)),
            dma((passes, images)),
            dma((passes,)),
        ],
        compiler_params=pltpu.CompilerParams(
            vmem_limit_bytes=48 * MIB, collective_id=0, has_side_effects=True
        ),
        cost_estimate=pl.CostEstimate(
            flops=8 * passes * mine * hidden * (hidden + outs),
            bytes_accessed=100 * MIB,
            transcendentals=4 * passes * mine * hidden,
        ),
        name="head_step",
    )(part, weight, box, count)


def own_gradient(kept, hidden, outs):
    parts = lax.axis_size("narrow")
    span = hidden // parts
    at = lax.axis_index("narrow") * span
    end = kept.shape[2] - LANES

    def rows(start):
        return lax.dynamic_slice_in_dim(kept, start + at, span, 2)

    def by(left, right):
        return lax.dot_general(left, right, (((1,), (1,)), ((0,), (0,))), preferred_element_type=jnp.float32)

    two = by(rows(0), kept[..., 2 * hidden : 3 * hidden])
    head = by(rows(hidden), kept[..., 3 * hidden : end])
    loss = jnp.sum(kept[..., end : end + 3].astype(jnp.float32))
    grad = jnp.concatenate([two, head], axis=2)
    spot = [lax.broadcasted_iota(jnp.int32, grad.shape, k) for k in range(3)]
    spot = (spot[0] == 0) & (spot[1] == 0) & (spot[2] == grad.shape[2] - 1)
    return jnp.where(spot, loss, grad)


def per_device(
    feat_p2, feat_p3, feat_p4, feat_p5, rois, levels, labels, sampled, targets,
    fc1_w, fc1_m, fc1_v, fc2_w, fc2_m, fc2_v, head_w, head_m, head_v,
):
    side = feat_p2.shape[-1]
    channels = feat_p2.shape[1]
    boxes = rois.shape[2]
    images = lax.axis_size("wide")
    mine = boxes // lax.axis_size("narrow")
    first = lax.axis_index("narrow") * mine
    level = lax.axis_index("wide").astype(jnp.int32)
    parts = lax.axis_size("narrow")
    hidden = fc2_w.shape[2]
    outs = head_w.shape[2]
    zero = jnp.zeros((), jnp.int32)
    rank = box_order(rois[:, 0], levels[:, 0], side)
    ordered = sort_boxes(rois[:, 0], levels[:, 0], rank)
    feat = feature_rows((feat_p2, feat_p3, feat_p4, feat_p5))
    height = feat.shape[0]
    flags = sampled[:, 0].astype(jnp.bfloat16).reshape(1, 2, boxes)
    tail = jnp.concatenate([ordered, flags]).reshape(-1, LANES)
    weight = jnp.concatenate([fc2_w, jnp.pad(head_w, ((0, 0), (0, 0), (0, -outs % LANES)))], axis=2)
    weight = lax.all_gather(weight.astype(jnp.bfloat16), "narrow", axis=1, tiled=True)
    feats = lax.all_gather(jnp.concatenate([feat, tail]), "wide", axis=0)
    tails = feats[:, height:].reshape(images, 6, 2, boxes)
    count = jnp.sum(tails[:, 5].astype(jnp.float32))

    table, spans = box_table(ordered[None], side)
    pooled, own = pool(feat[None], table, spans, zero, level, images, channels)
    w1 = fc1_w.astype(jnp.bfloat16)
    part = lax.dot_general(own, w1, (((1,), (1,)), ((0,), (0,))), preferred_element_type=jnp.float32)
    hot = rank[:, None, :] == first + jnp.arange(mine, dtype=jnp.int32)[:, None]

    def pick(values):
        return jnp.sum(jnp.where(hot, values[:, 0].astype(jnp.float32)[:, None, :], 0), axis=-1)

    box = [pick(labels), pick(sampled)] + [pick(targets[..., k]) for k in range(4)]
    box = jnp.pad(jnp.stack(box, axis=-1), ((0, 0), (0, 0), (0, LANES - 6)))
    back, kept = head_step(part, weight, box, jnp.full((8, LANES), count), images, parts)

    tables, all_spans = box_table(tails[:, :5], side)
    kept = lax.all_gather(kept, "narrow", axis=1, tiled=True)
    turn = [lax.rem(level + k, images) for k in range(1, images)]
    held = max(images - 2, 1)
    for k in range(images - 1):
        if k == held:
            kept, pooled = lax.optimization_barrier((kept, pooled))
            grad = own_gradient(kept, hidden, outs)
            grad, pooled = lax.optimization_barrier((grad, pooled))
            grad = lax.psum_scatter(grad, "wide", scatter_dimension=1, tiled=True)
        pooled = pool(feats, tables, all_spans, turn[k], turn[k], images, channels, pooled)[0]
    grad, pooled = lax.optimization_barrier((grad, pooled))
    grad = lax.all_gather(grad, "wide", axis=1, tiled=True)
    new1 = update_first(pooled, back, fc1_w, fc1_m, fc1_v)
    grad, new1 = lax.optimization_barrier((grad, new1))
    total = grad[0, 0, -1]
    new2 = adamw(fc2_w, fc2_m, fc2_v, grad[..., :hidden])
    newh = adamw(head_w, head_m, head_v, grad[..., hidden : hidden + outs])
    return (jnp.stack([total, count]),) + tuple(new1) + tuple(new2) + tuple(newh)


def solution(mesh):
    maps = P("wide", "narrow", None, None)
    rows = P(None, "narrow", None)
    box = P(None, "wide", None)
    coords = P(None, "wide", None, None)
    return jax.shard_map(
        per_device,
        mesh=mesh,
        in_specs=(maps,) * 4 + (coords, box, box, box, coords) + (rows,) * 9,
        out_specs=(P(),) + (rows,) * 9,
        check_vma=False,
    )
```

```python
from functools import partial

import jax
import jax.numpy as jnp
from jax import lax
from jax.experimental import pallas as pl
from jax.experimental.pallas import tpu as pltpu
from jax.sharding import PartitionSpec as P

CLASSES = 81
STEP = 5
BETA_ONE = 0.5
BETA_TWO = 0.5
RATE = 0.02
DECAY = 0.01
EPSILON = 1e-08
BINS = 7
CHUNK = 8
STATIC = 5
WINDOW = 24
MORE = 4
SPANS = 17
LANES = 128
MIB = 2**20


def tent(where, cells):
    return 0.5 * sum(jnp.maximum(0.0, 1.0 - jnp.abs(w - cells)) for w in where)


def pool_kernel(channels, side, groups, copies, pick_ref, span_ref, feat_ref, table_ref, *refs):
    out_refs = refs[-7 - copies : -7]
    cols, rows, parts = refs[-7:-5], refs[-5:-3], refs[-3:-1]
    line_ref = refs[-1]
    image = pick_ref[0]
    half = LANES // 2
    offsets = (0.25, 0.75)
    cells = lax.broadcasted_iota(jnp.int32, (side, LANES), 0).astype(jnp.float32)
    bins = lax.broadcasted_iota(jnp.int32, (8, LANES), 0).astype(jnp.float32)

    def at(group):
        return (image * groups + group) * SPANS

    def param(group, k):
        return table_ref[group, k : k + 1, :]

    def weights(group, slot):
        top, x_start, x_step = param(group, 2), param(group, 4), param(group, 5)
        for j in range(BINS):
            where = [jnp.clip(x_start + (j + off) * x_step, 0.0, top) for off in offsets]
            weight = tent(where, cells)
            high = weight.astype(jnp.bfloat16)
            low = (weight - high.astype(jnp.float32)).astype(jnp.bfloat16)
            lanes = pl.ds(j * LANES, LANES)
            cols[slot][0:side, lanes] = high
            cols[slot][side : 2 * side, lanes] = high
            cols[slot][2 * side : 3 * side, lanes] = low
            cols[slot][3 * side : 4 * side, lanes] = low

    def fill(group, slot, row):
        y_start, y_step, top, base = (param(group, k) for k in range(4))
        where = [jnp.clip(y_start + (bins + off) * y_step, 0.0, top) for off in offsets]
        for h in range(CHUNK):
            rows[slot][row + h] = tent(where, (row + h).astype(jnp.float32) - base)
        place = pl.ds(pl.multiple_of(row * channels, channels), CHUNK * channels)
        left = feat_ref[place, :]
        left = jnp.concatenate([left, left], axis=1)
        parts[slot][place, :] = jnp.dot(left, cols[slot][...], preferred_element_type=jnp.float32)

    def rest(group, slot):
        first = span_ref[at(group)] + STATIC * CHUNK

        @pl.loop(0, span_ref[at(group) + 1])
        def _(t):
            fill(group, slot, first + t * CHUNK)

    def block(slot, i, low_row, count):
        accs = None
        for h in range(count):
            start = pl.multiple_of((low_row + h) * channels, channels)
            weight = jnp.broadcast_to(rows[slot][low_row + h, i : i + 1, :], (channels, LANES))
            new = [
                weight * parts[slot][pl.ds(start, channels), j * LANES : (j + 1) * LANES] for j in range(BINS)
            ]
            accs = new if accs is None else [x + y for x, y in zip(accs, new)]
        return accs

    def spot(i, j):
        return pl.ds(i * BINS + j, channels, stride=BINS * BINS)

    def work(group, slot, following):
        for i in range(BINS):
            accs = block(slot, i, span_ref[at(group) + 3 + i], WINDOW)
            for j in range(BINS):
                line_ref[slot, spot(i, j), :] = accs[j]
            if i < STATIC:
                fill(following, 1 - slot, span_ref[at(following)] + i * CHUNK)

        @pl.when(span_ref[at(group) + 2] > 0)
        def _():
            for i in range(BINS):
                low_row = span_ref[at(group) + 3 + i] + WINDOW

                @pl.loop(0, span_ref[at(group) + 3 + BINS + i])
                def _(t):
                    more = block(slot, i, low_row + t * MORE, MORE)
                    for j in range(BINS):
                        line_ref[slot, spot(i, j), :] = line_ref[slot, spot(i, j), :] + more[j]

    step = pl.program_id(0)

    @pl.when(step == 0)
    def _():
        weights(0, 0)
        for i in range(STATIC):
            fill(0, 0, span_ref[at(0)] + i * CHUNK)
        rest(0, 0)

    group = 2 * step
    weights(group + 1, 1)
    work(group, 0, group + 1)
    rest(group + 1, 1)
    following = jnp.minimum(group + 2, groups - 1)
    weights(following, 0)
    work(group + 1, 1, following)
    rest(following, 0)
    a, b = line_ref[0], line_ref[1]
    lanes = lax.broadcasted_iota(jnp.int32, a.shape, 1)
    new = [jnp.where(lanes < half, a, pltpu.roll(b, half, 1)), jnp.where(lanes < half, pltpu.roll(a, half, 1), b)]
    for out_ref in out_refs:
        for p in range(2):
            out_ref[p] = new[p].astype(jnp.bfloat16)


def pool(feat, table, spans, source, image, images, channels, buffer=None):
    depth = feat.shape[2]
    groups = table.shape[1]
    wide = channels * BINS * BINS
    side = depth // 2
    rows = sum(side >> k for k in range(4))
    boxes = groups * LANES // 2
    blocks = groups // 2
    pick = jnp.stack([source, image])
    out_shape = [jax.ShapeDtypeStruct((2, wide, images * boxes), jnp.bfloat16)]
    out_specs = [pl.BlockSpec((2, wide, LANES), lambda s, pick, spans: (0, 0, pick[1] * blocks + s))]
    in_specs = [
        pl.BlockSpec((None, rows * channels, depth), lambda s, pick, spans: (pick[0], 0, 0)),
        pl.BlockSpec((None, groups, 8, LANES), lambda s, pick, spans: (pick[0], 0, 0, 0)),
    ]
    operands = (pick, spans, feat, table)
    aliases = {}
    if buffer is None:
        out_shape.append(jax.ShapeDtypeStruct((2, wide, boxes), jnp.bfloat16))
        out_specs.append(pl.BlockSpec((2, wide, LANES), lambda s, pick, spans: (0, 0, s)))
    else:
        in_specs.append(pl.BlockSpec(memory_space=pl.ANY))
        operands += (buffer,)
        aliases = {4: 0}
    return pl.pallas_call(
        partial(pool_kernel, channels, side, groups, len(out_shape)),
        out_shape=out_shape,
        grid_spec=pltpu.PrefetchScalarGridSpec(
            num_scalar_prefetch=2,
            grid=(blocks,),
            in_specs=in_specs,
            out_specs=out_specs,
            scratch_shapes=[
                pltpu.VMEM((4 * side, BINS * LANES), jnp.bfloat16),
                pltpu.VMEM((4 * side, BINS * LANES), jnp.bfloat16),
                pltpu.VMEM((rows, 8, LANES), jnp.float32),
                pltpu.VMEM((rows, 8, LANES), jnp.float32),
                pltpu.VMEM((rows * channels, BINS * LANES), jnp.float32),
                pltpu.VMEM((rows * channels, BINS * LANES), jnp.float32),
                pltpu.VMEM((2, wide, LANES), jnp.float32),
            ],
        ),
        input_output_aliases=aliases,
        compiler_params=pltpu.CompilerParams(vmem_limit_bytes=44 * MIB),
        cost_estimate=pl.CostEstimate(
            flops=groups * 40 * channels * BINS * LANES * 8 * depth,
            bytes_accessed=80 * MIB,
            transcendentals=0,
        ),
        name="pool_rois",
    )(*operands)


def feature_rows(maps):
    side = maps[0].shape[-1]
    parts = [
        jnp.pad(m.transpose(0, 2, 1, 3), ((0, 0), (0, 0), (0, 0), (0, side - m.shape[-1])))
        for m in maps
    ]
    full = jnp.concatenate(parts, axis=1)
    high = lax.reduce_precision(full, 8, 7)
    low = (full - high).astype(jnp.bfloat16)
    full = jnp.concatenate([high.astype(jnp.bfloat16), low], axis=-1)
    return full.reshape(-1, 2 * side)


def box_order(boxes, levels, side):
    base = 2 * side - 2 * (side >> levels)
    key = ((boxes[..., 1] + boxes[..., 3]) >> levels) + base * 8
    key = key * key.shape[-1] + jnp.arange(key.shape[-1], dtype=jnp.int32)
    return jnp.sum((key[..., :, None] > key[..., None, :]).astype(jnp.int32), axis=-1)


def sort_boxes(boxes, levels, rank):
    count = boxes.shape[1]
    hot = (rank[:, None, :] == jnp.arange(count, dtype=jnp.int32)[:, None]).astype(jnp.bfloat16)
    both = jnp.concatenate([boxes, levels[..., None]], axis=-1).astype(jnp.bfloat16)
    return jnp.einsum("psr,prk->kps", hot, both, preferred_element_type=jnp.float32).astype(jnp.bfloat16)


def box_table(boxes, side):
    images, _, _, count = boxes.shape
    x0, y0, x1, y1, level = (boxes[:, k].astype(jnp.float32) for k in range(5))
    rows = sum(side >> k for k in range(4))
    scale = jnp.where(level < 0.5, 0.25, jnp.where(level < 1.5, 0.125, jnp.where(level < 2.5, 0.0625, 0.03125)))
    height = scale * (4 * side)
    base = 2.0 * side - 2.0 * height
    top = height - 1.0

    def axis(low, high):
        return low * scale - 0.5, ((high - low) * scale) / 7.0

    x_start, x_step = axis(x0, x1)
    y_start, y_step = axis(y0, y1)
    half = LANES // 2
    groups = count // half

    def split(v):
        return v.reshape(v.shape[:-1] + (groups, half))

    lows, highs = [], []
    for i in range(BINS):
        low = base + jnp.floor(jnp.clip(y_start + (i + 0.25) * y_step, 0.0, top))
        high = base + jnp.floor(jnp.clip(y_start + (i + 0.75) * y_step, 0.0, top)) + 1.0
        lows.append(jnp.min(split(low), axis=(1, 3)))
        highs.append(jnp.max(split(jnp.minimum(high, rows - 1.0)), axis=(1, 3)))
    low = jnp.stack(lows, axis=-1).astype(jnp.int32)
    high = jnp.stack(highs, axis=-1).astype(jnp.int32)
    least = jnp.min(low, axis=-1)
    chunks = jnp.maximum((jnp.max(high, axis=-1) - least + CHUNK) // CHUNK, STATIC)
    first = jnp.clip(rows - chunks * CHUNK, 0, least)
    extra = jnp.maximum(high - low + MORE - WINDOW, 0) // MORE
    low = jnp.minimum(low, (first + chunks * CHUNK)[..., None] - WINDOW - MORE * extra)
    heads = jnp.stack([first, chunks - STATIC, jnp.max(extra, axis=-1)], axis=-1)
    spans = jnp.concatenate([heads, low, extra], axis=-1).reshape(-1)
    zero = jnp.zeros_like(base)
    table = jnp.stack([split(v) for v in (y_start, y_step, top, base, x_start, x_step, zero, zero)])
    return table.transpose(1, 3, 0, 2, 4).reshape(images, groups, 8, LANES), spans


def adamw(weight, moment, second, grad):
    moment = BETA_ONE * moment + (1.0 - BETA_ONE) * grad
    second = BETA_TWO * second + (1.0 - BETA_TWO) * grad * grad
    fixed_m = moment / (1.0 - BETA_ONE**STEP)
    fixed_v = second / (1.0 - BETA_TWO**STEP)
    weight = weight - RATE * (fixed_m / (jnp.sqrt(fixed_v) + EPSILON) + DECAY * weight)
    return (weight, moment, second)


def update_kernel(pooled_ref, back_ref, w_ref, m_ref, v_ref, *outs):
    grad = jnp.dot(pooled_ref[...], back_ref[...], preferred_element_type=jnp.float32)
    new = adamw(w_ref[...], m_ref[...], v_ref[...], grad)
    for ref, value in zip(outs, new):
        ref[...] = value


def update_first(pooled, back, weight, moment, second):
    passes, wide, hidden = weight.shape
    boxes = pooled.shape[2]
    block = wide // BINS
    big = pl.BlockSpec((None, block, hidden), lambda p, b: (p, b, 0))
    return pl.pallas_call(
        update_kernel,
        out_shape=[jax.ShapeDtypeStruct(weight.shape, jnp.float32)] * 3,
        grid=(passes, BINS),
        in_specs=[
            pl.BlockSpec((None, block, boxes), lambda p, b: (p, b, 0)),
            pl.BlockSpec((None, boxes, hidden), lambda p, b: (p, 0, 0)),
            big,
            big,
            big,
        ],
        out_specs=[big] * 3,
        compiler_params=pltpu.CompilerParams(vmem_limit_bytes=56 * MIB),
        cost_estimate=pl.CostEstimate(
            flops=2 * passes * wide * hidden * boxes,
            bytes_accessed=passes * wide * hidden * 24 + passes * boxes * (wide + hidden) * 2,
            transcendentals=passes * wide * hidden,
        ),
        name="update_first",
    )(pooled, back, weight, moment, second)


def loss_and_slope(logits, box, count):
    place = lax.broadcasted_iota(jnp.int32, logits.shape, 1)
    is_class = place < CLASSES
    label = box[:, 0:1].astype(jnp.int32)
    weight = box[:, 1:2]
    top = jnp.max(jnp.where(is_class, logits, -jnp.inf), axis=1, keepdims=True)
    grown = jnp.where(is_class, jnp.exp(jnp.where(is_class, logits - top, 0.0)), 0.0)
    norm = jnp.sum(grown, axis=1, keepdims=True)
    hot = place == label
    picked = jnp.sum(jnp.where(hot, logits, 0.0), axis=1, keepdims=True)
    fore = jnp.where(label > 0, weight, 0.0)
    rows = weight * (top + jnp.log(norm) - picked)
    slope = weight * (grown / norm - jnp.where(hot, 1.0, 0.0))
    offset = place - (CLASSES + 4 * (label - 1))
    for k in range(4):
        mask = (offset == k) & (place >= CLASSES)
        chosen = jnp.sum(jnp.where(mask, logits, 0.0), axis=1, keepdims=True)
        differ = fore * (chosen - box[:, 2 + k : 3 + k])
        near = jnp.abs(differ)
        rows += jnp.where(near < 1.0, 0.5 * differ * differ, near - 0.5) * fore
        slope = jnp.where(mask, fore * jnp.clip(differ, -1.0, 1.0), slope)
    return rows, slope / count


def sigmoid(value):
    return 1.0 / (1.0 + jnp.exp(-value))


def head_kernel(
    images, parts, mine,
    part_ref, weight_ref, box_ref, count_ref,
    back_ref, grad_ref,
    sums, landed, own, counts, turned, cols, kept,
    rs_send, rs_recv, ag_send, ag_recv, up_send, up_recv, down_send, down_recv, own_sem,
    count_send, count_recv, col_send, col_recv, kept_send, kept_recv,
):
    me = lax.axis_index("narrow")
    level = lax.axis_index("wide")
    bits = parts.bit_length() - 1
    turn = [(1 - 2 * ((me // 2**k) % 2)) * 2**k for k in range(bits)]

    def peer(mask):
        return me + sum((turn[k] for k in range(bits) if mask >> k & 1), 0)

    links = list(range(1, bits))
    orders = [links, links[::-1]]

    barrier = pltpu.get_barrier_semaphore()
    for mask in range(1, parts):
        pl.semaphore_signal(barrier, inc=1, device_id={"narrow": peer(mask)})
    for k in range(1, images):
        pl.semaphore_signal(barrier, inc=1, device_id={"wide": lax.rem(level + k, images)})
    pl.semaphore_wait(barrier, parts + images - 2)

    counting = []
    for k in range(1, images):
        counting.append(
            pltpu.make_async_remote_copy(
                src_ref=count_ref,
                dst_ref=counts.at[k],
                send_sem=count_send.at[k],
                recv_sem=count_recv.at[k],
                device_id={"wide": lax.rem(level + k, images)},
            )
        )

    def scatter(p, mask, bit, source):
        return pltpu.make_async_remote_copy(
            src_ref=source,
            dst_ref=landed.at[p, mask],
            send_sem=rs_send.at[p, mask],
            recv_sem=rs_recv.at[p, mask],
            device_id={"narrow": peer(1 << bit)},
        )

    def part_at(p, mask):
        return part_ref.at[p, pl.ds(pl.multiple_of(peer(mask) * mine, mine), mine), :]

    copies = {}
    for p in range(2):
        for mask in range(1, parts, 2):
            copies[p, mask] = scatter(p, mask, 0, part_at(p, mask))
            copies[p, mask].start()

    def stage(p, at):
        order = [0] + orders[p]
        bit = order[at - 1]
        seen = sum(1 << b for b in order[:at])
        for mask in range(parts):
            if mask & seen:
                continue
            copies[p, mask | 1 << bit].wait_recv()
            if at == 1:
                have = part_ref[p, pl.ds(pl.multiple_of(peer(mask) * mine, mine), mine), :]
            else:
                have = sums[p, mask]
            sums[p, mask] = have + landed[p, mask | 1 << bit]
            if at < bits and mask >> order[at] & 1:
                copies[p, mask] = scatter(p, mask, order[at], sums.at[p, mask])
                copies[p, mask].start()

    for copy in counting:
        copy.start()
    for at in range(1, bits):
        for p in range(2):
            stage(p, at)

    def rows(p, image, mask):
        place = (image * parts + peer(mask)) * mine
        return back_ref.at[p, pl.ds(pl.multiple_of(place, mine), mine), :]

    def hop(p, d, up, source=None):
        image = level - d if up else level + d
        spot = rows(p, image, 0)
        return pltpu.make_async_remote_copy(
            src_ref=spot if source is None else source,
            dst_ref=spot,
            send_sem=(up_send if up else down_send).at[p, d],
            recv_sem=(up_recv if up else down_recv).at[p, d],
            device_id={"wide": level + 1 if up else level - 1},
        )

    def came(p, d, up):
        image = level - d if up else level + d
        spot = rows(p, image, 0)
        pltpu.make_async_remote_copy(
            src_ref=spot, dst_ref=spot, send_sem=(up_send if up else down_send).at[p, d],
            recv_sem=(up_recv if up else down_recv).at[p, d - 1],
            device_id={"wide": level - 1 if up else level + 1},
        ).wait_recv()

    steps = [orders[p] + [0] for p in range(2)]

    def masks_before(p, at):
        seen = sum(1 << b for b in steps[p][:at])
        return [m for m in range(parts) if not m & ~seen]

    def doubling(spot, send, recv):
        def spread(p, key, mask, bit, source=None):
            there = mask | 1 << bit
            return pltpu.make_async_remote_copy(
                src_ref=spot(p, key, mask) if source is None else source,
                dst_ref=spot(p, key, mask),
                send_sem=send.at[p, key, there],
                recv_sem=recv.at[p, key, there],
                device_id={"narrow": peer(1 << bit)},
            )

        def arrive(p, key, at):
            for m in masks_before(p, at):
                there = m | 1 << steps[p][at]
                pltpu.make_async_remote_copy(
                    src_ref=spot(p, key, there),
                    dst_ref=spot(p, key, there),
                    send_sem=send.at[p, key, there],
                    recv_sem=recv.at[p, key, there],
                    device_id={"narrow": peer(1)},
                ).wait_recv()

        def advance(p, key, at, source=None):
            if at:
                arrive(p, key, at - 1)
            for m in masks_before(p, at):
                spread(p, key, m, steps[p][at], source if m == 0 else None).start()

        def sent(p, key):
            for at in range(bits):
                for m in masks_before(p, at):
                    spread(p, key, m, steps[p][at]).wait_send()

        return advance, arrive, sent

    advance, arrive, sent = doubling(rows, ag_send, ag_recv)
    advance_kept, arrive_kept, sent_kept = doubling(
        lambda p, key, mask: kept.at[p, peer(mask)], kept_send, kept_recv
    )

    def finish(p, image):
        arrive(p, image, bits - 1)
        sent(p, image)

    span = grad_ref.shape[1]

    def columns(p, mask):
        return turned.at[p, :, pl.ds(pl.multiple_of(peer(mask) * span, span), span), :]

    def hand(p, mask):
        return pltpu.make_async_remote_copy(
            src_ref=columns(p, mask),
            dst_ref=cols.at[p, mask],
            send_sem=col_send.at[p, mask],
            recv_sem=col_recv.at[p, mask],
            device_id={"narrow": peer(mask)},
        )

    for copy in counting:
        copy.wait_recv()
    count = count_ref[0:1, 0:1] + sum(counts[k, 0:1, 0:1] for k in range(1, images))
    hidden = part_ref.shape[2]
    for p in range(2):
        stage(p, bits)
        pre1 = sums[p, 0]
        sig1 = sigmoid(pre1)
        hid1 = (pre1 * sig1).astype(jnp.bfloat16)
        pre2 = jnp.dot(hid1, weight_ref[p, :, :hidden], preferred_element_type=jnp.float32)
        sig2 = sigmoid(pre2)
        hid2 = (pre2 * sig2).astype(jnp.bfloat16)
        logits = jnp.dot(hid2, weight_ref[p, :, hidden:], preferred_element_type=jnp.float32)
        loss, slope = loss_and_slope(logits, box_ref[p], count)
        back_z = slope.astype(jnp.bfloat16)
        across = (((1,), (1,)), ((), ()))
        back_h2 = lax.dot_general(back_z, weight_ref[p, :, hidden:], across, preferred_element_type=jnp.float32)
        back_p2 = (back_h2 * (sig2 * (1.0 + pre2 * (1.0 - sig2)))).astype(jnp.bfloat16)
        back_h1 = lax.dot_general(back_p2, weight_ref[p, :, :hidden], across, preferred_element_type=jnp.float32)
        own[p] = (back_h1 * (sig1 * (1.0 + pre1 * (1.0 - sig1)))).astype(jnp.bfloat16)

        @pl.when(level < images - 1)
        def _():
            hop(p, 0, True, own.at[p]).start()

        @pl.when(level > 0)
        def _():
            hop(p, 0, False, own.at[p]).start()

        advance(p, level, 0, own.at[p])
        pltpu.make_async_copy(own.at[p], rows(p, level, 0), own_sem.at[p]).start()
        place = lax.broadcasted_iota(jnp.int32, (mine, LANES), 1)
        losses = jnp.zeros((mine, LANES), jnp.float32)
        for k in range(3):
            near = loss.astype(jnp.bfloat16).astype(jnp.float32)
            losses = jnp.where(place == k, near, losses)
            loss = loss - near
        at = 0
        for value in (back_p2, back_z, losses.astype(jnp.bfloat16)):
            kept[p, me, :, at : at + value.shape[1]] = value
            at += value.shape[1]
        advance_kept(p, 0, 0)
        turned[p, 0] = hid1.T
        turned[p, 1] = hid2.T
        for mask in range(1, parts):
            hand(p, mask).start()
    for p in range(2):
        pltpu.make_async_copy(own.at[p], rows(p, level, 0), own_sem.at[p]).wait()

    def each_side(d, do):
        @pl.when(level >= d)
        def _():
            do(level - d, True)

        @pl.when(level + d < images)
        def _():
            do(level + d, False)

    def enter(d):
        def do(image, up):
            for p in range(2):
                came(p, d, up)

                @pl.when((level < images - 1) if up else (level > 0))
                def _():
                    hop(p, d, up).start()

                advance(p, image, 0)

        each_side(d, do)

    def go_on(d, at):
        if d == 0:
            for p in range(2):
                advance(p, level, at)
                advance_kept(p, 0, at)
        else:

            def do(image, up):
                for p in range(2):
                    advance(p, image, at)

            each_side(d, do)

    for tick in range(1, images + bits - 1):
        for d in range(images):
            at = tick - d
            if at == 0:
                enter(d)
            elif 0 < at < bits:
                go_on(d, at)

    loss = jnp.zeros((1, 1), jnp.float32)
    for p in range(2):
        arrive_kept(p, 0, bits - 1)
        two, head = [], []
        for mask in range(parts):
            if mask:
                hand(p, mask).wait_recv()
            mine_ref = cols.at[p, mask] if mask else columns(p, 0)
            slopes = kept.at[p, peer(mask)]
            two.append(jnp.dot(mine_ref[0], slopes[:, :hidden], preferred_element_type=jnp.float32))
            head.append(jnp.dot(mine_ref[1], slopes[:, hidden:-LANES], preferred_element_type=jnp.float32))
            loss += jnp.sum(slopes[:, -LANES:].astype(jnp.float32), keepdims=True)
        grad_ref[p, :, :hidden] = sum(two)
        grad_ref[p, :, hidden:] = sum(head)
    corner = grad_ref[0, 0:8, grad_ref.shape[2] - LANES :]
    place = [lax.broadcasted_iota(jnp.int32, corner.shape, k) for k in range(2)]
    corner = jnp.where((place[0] == 0) & (place[1] == LANES - 1), loss, corner)
    grad_ref[0, 0:8, grad_ref.shape[2] - LANES :] = corner

    for p in range(2):
        finish(p, level)
        sent_kept(p, 0)
        for mask in range(1, parts):
            hand(p, mask).wait_send()

        @pl.when(level < images - 1)
        def _():
            hop(p, 0, True).wait_send()

        @pl.when(level > 0)
        def _():
            hop(p, 0, False).wait_send()

    for d in range(1, images):

        def do(image, up):
            for p in range(2):
                finish(p, image)

                @pl.when((level < images - 1) if up else (level > 0))
                def _():
                    hop(p, d, up).wait_send()

        each_side(d, do)
    for p in range(2):
        for mask in range(1, parts):
            copies[p, mask].wait_send()
    for copy in counting:
        copy.wait_send()


def head_step(part, weight, box, count, images, parts):
    passes, boxes, hidden = part.shape
    mine = boxes // parts
    outs = weight.shape[2] - hidden
    span = hidden // parts
    low = jnp.bfloat16
    vmem = pl.BlockSpec(memory_space=pltpu.VMEM)
    dma = pltpu.SemaphoreType.DMA
    return pl.pallas_call(
        partial(head_kernel, images, parts, mine),
        out_shape=[
            jax.ShapeDtypeStruct((passes, images * boxes, hidden), low),
            jax.ShapeDtypeStruct((passes, span, hidden + outs), jnp.float32),
        ],
        in_specs=[vmem] * 4,
        out_specs=[pl.BlockSpec(memory_space=pl.ANY), vmem],
        scratch_shapes=[
            pltpu.VMEM((passes, parts, mine, hidden), jnp.float32),
            pltpu.VMEM((passes, parts, mine, hidden), jnp.float32),
            pltpu.VMEM((passes, mine, hidden), low),
            pltpu.VMEM((images, 8, LANES), jnp.float32),
            pltpu.VMEM((passes, 2, hidden, mine), low),
            pltpu.VMEM((passes, parts, 2, span, mine), low),
            pltpu.VMEM((passes, parts, mine, hidden + outs + LANES), low),
            dma((passes, parts)),
            dma((passes, parts)),
            dma((passes, images, parts)),
            dma((passes, images, parts)),
            dma((passes, images)),
            dma((passes, images)),
            dma((passes, images)),
            dma((passes, images)),
            dma((passes,)),
            dma((images,)),
            dma((images,)),
            dma((passes, parts)),
            dma((passes, parts)),
            dma((passes, 1, parts)),
            dma((passes, 1, parts)),
        ],
        compiler_params=pltpu.CompilerParams(
            vmem_limit_bytes=48 * MIB, collective_id=0, has_side_effects=True
        ),
        cost_estimate=pl.CostEstimate(
            flops=8 * passes * mine * hidden * (hidden + outs),
            bytes_accessed=100 * MIB,
            transcendentals=4 * passes * mine * hidden,
        ),
        name="head_step",
    )(part, weight, box, count)


def small_kernel(grad_ref, *refs):
    at = 0
    for k in range(2):
        weight, moment, second = (r[...] for r in refs[3 * k : 3 * k + 3])
        new = adamw(weight, moment, second, grad_ref[:, at : at + weight.shape[1]])
        for ref, value in zip(refs[6 + 3 * k : 9 + 3 * k], new):
            ref[...] = value
        at += weight.shape[1]


def update_small(grad, *arrays):
    def spec(x):
        return pl.BlockSpec((None,) + x.shape[1:], lambda p: (p, 0, 0))

    return pl.pallas_call(
        small_kernel,
        out_shape=[jax.ShapeDtypeStruct(x.shape, jnp.float32) for x in arrays],
        grid=(grad.shape[0],),
        in_specs=[spec(x) for x in (grad,) + arrays],
        out_specs=[spec(x) for x in arrays],
        compiler_params=pltpu.CompilerParams(vmem_limit_bytes=24 * MIB),
        name="update_small",
    )(grad, *arrays)


def per_device(
    feat_p2, feat_p3, feat_p4, feat_p5, rois, levels, labels, sampled, targets,
    fc1_w, fc1_m, fc1_v, fc2_w, fc2_m, fc2_v, head_w, head_m, head_v,
):
    side = feat_p2.shape[-1]
    channels = feat_p2.shape[1]
    boxes = rois.shape[2]
    images = lax.axis_size("wide")
    mine = boxes // lax.axis_size("narrow")
    first = lax.axis_index("narrow") * mine
    level = lax.axis_index("wide").astype(jnp.int32)
    parts = lax.axis_size("narrow")
    hidden = fc2_w.shape[2]
    outs = head_w.shape[2]
    zero = jnp.zeros((), jnp.int32)
    rank = box_order(rois[:, 0], levels[:, 0], side)
    ordered = sort_boxes(rois[:, 0], levels[:, 0], rank)
    feat = feature_rows((feat_p2, feat_p3, feat_p4, feat_p5))
    height = feat.shape[0]
    flags = sampled[:, 0].astype(jnp.bfloat16).reshape(1, 2, boxes)
    both = jnp.concatenate([feat, jnp.concatenate([ordered, flags]).reshape(-1, LANES)])
    weight = jnp.concatenate([fc2_w, jnp.pad(head_w, ((0, 0), (0, 0), (0, -outs % LANES)))], axis=2)
    weight = lax.all_gather(weight.astype(jnp.bfloat16), "narrow", axis=1, tiled=True)
    counted = jnp.sum(sampled).astype(jnp.float32)
    table, spans = box_table(ordered[None], side)
    pooled, own = pool(feat[None], table, spans, zero, level, images, channels)
    both, own = lax.optimization_barrier((both, own))
    feats = lax.all_gather(both, "wide", axis=0)
    w1 = fc1_w.astype(jnp.bfloat16)
    part = lax.dot_general(own, w1, (((1,), (1,)), ((0,), (0,))), preferred_element_type=jnp.float32)
    hot = rank[:, None, :] == first + jnp.arange(mine, dtype=jnp.int32)[:, None]

    def pick(values):
        return jnp.sum(jnp.where(hot, values[:, 0].astype(jnp.float32)[:, None, :], 0), axis=-1)

    box = [pick(labels), pick(sampled)] + [pick(targets[..., k]) for k in range(4)]
    box = jnp.pad(jnp.stack(box, axis=-1), ((0, 0), (0, 0), (0, LANES - 6)))
    back, grad = head_step(part, weight, box, jnp.full((8, LANES), counted), images, parts)
    grad = lax.psum_scatter(grad, "wide", scatter_dimension=1, tiled=True)

    tails = feats[:, height:].reshape(images, 6, 2, boxes)
    count = jnp.sum(tails[:, 5].astype(jnp.float32))
    tables, all_spans = box_table(tails[:, :5], side)
    turn = [lax.rem(level + k, images) for k in range(1, images)]
    for k in range(images - 1):
        pooled = pool(feats, tables, all_spans, turn[k], turn[k], images, channels, pooled)[0]
        if k == max(images - 3, 0):
            grad, pooled = lax.optimization_barrier((grad, pooled))
            grad = lax.all_gather(grad, "wide", axis=1, tiled=True)
    new1 = update_first(pooled, back, fc1_w, fc1_m, fc1_v)
    grad, new1 = lax.optimization_barrier((grad, new1))
    total = grad[0, 0, -1]
    new = update_small(grad, fc2_w, fc2_m, fc2_v, head_w, head_m, head_v)
    return (jnp.stack([total, count]),) + tuple(new1) + tuple(new)


def solution(mesh):
    maps = P("wide", "narrow", None, None)
    rows = P(None, "narrow", None)
    box = P(None, "wide", None)
    coords = P(None, "wide", None, None)
    return jax.shard_map(
        per_device,
        mesh=mesh,
        in_specs=(maps,) * 4 + (coords, box, box, box, coords) + (rows,) * 9,
        out_specs=(P(),) + (rows,) * 9,
        check_vma=False,
    )
```

```python
from functools import partial

import jax
import jax.numpy as jnp
from jax import lax
from jax.experimental import pallas as pl
from jax.experimental.pallas import tpu as pltpu
from jax.sharding import PartitionSpec as P

CLASSES = 81
STEP = 5
BETA_ONE = 0.5
BETA_TWO = 0.5
RATE = 0.02
DECAY = 0.01
EPSILON = 1e-08
BINS = 7
CHUNK = 8
STATIC = 5
WINDOW = 24
MORE = 4
SPANS = 17
LANES = 128
MIB = 2**20


def tent(where, cells):
    return 0.5 * sum(jnp.maximum(0.0, 1.0 - jnp.abs(w - cells)) for w in where)


def pool_kernel(channels, side, groups, copies, pick_ref, span_ref, feat_ref, table_ref, *refs):
    out_refs = refs[-7 - copies : -7]
    cols, rows, parts = refs[-7:-5], refs[-5:-3], refs[-3:-1]
    line_ref = refs[-1]
    image = pick_ref[0]
    half = LANES // 2
    offsets = (0.25, 0.75)
    cells = lax.broadcasted_iota(jnp.int32, (side, LANES), 0).astype(jnp.float32)
    bins = lax.broadcasted_iota(jnp.int32, (8, LANES), 0).astype(jnp.float32)

    def at(group):
        return (image * groups + group) * SPANS

    def param(group, k):
        return table_ref[group, k : k + 1, :]

    def weights(group, slot):
        top, x_start, x_step = param(group, 2), param(group, 4), param(group, 5)
        for j in range(BINS):
            where = [jnp.clip(x_start + (j + off) * x_step, 0.0, top) for off in offsets]
            weight = tent(where, cells)
            high = weight.astype(jnp.bfloat16)
            low = (weight - high.astype(jnp.float32)).astype(jnp.bfloat16)
            lanes = pl.ds(j * LANES, LANES)
            cols[slot][0:side, lanes] = high
            cols[slot][side : 2 * side, lanes] = high
            cols[slot][2 * side : 3 * side, lanes] = low
            cols[slot][3 * side : 4 * side, lanes] = low

    def fill(group, slot, row):
        y_start, y_step, top, base = (param(group, k) for k in range(4))
        where = [jnp.clip(y_start + (bins + off) * y_step, 0.0, top) for off in offsets]
        for h in range(CHUNK):
            rows[slot][row + h] = tent(where, (row + h).astype(jnp.float32) - base)
        place = pl.ds(pl.multiple_of(row * channels, channels), CHUNK * channels)
        left = feat_ref[place, :]
        left = jnp.concatenate([left, left], axis=1)
        parts[slot][place, :] = jnp.dot(left, cols[slot][...], preferred_element_type=jnp.float32)

    def rest(group, slot):
        first = span_ref[at(group)] + STATIC * CHUNK

        @pl.loop(0, span_ref[at(group) + 1])
        def _(t):
            fill(group, slot, first + t * CHUNK)

    def block(slot, i, low_row, count):
        accs = None
        for h in range(count):
            start = pl.multiple_of((low_row + h) * channels, channels)
            weight = jnp.broadcast_to(rows[slot][low_row + h, i : i + 1, :], (channels, LANES))
            new = [
                weight * parts[slot][pl.ds(start, channels), j * LANES : (j + 1) * LANES] for j in range(BINS)
            ]
            accs = new if accs is None else [x + y for x, y in zip(accs, new)]
        return accs

    def spot(i, j):
        return pl.ds(i * BINS + j, channels, stride=BINS * BINS)

    def work(group, slot, following):
        for i in range(BINS):
            accs = block(slot, i, span_ref[at(group) + 3 + i], WINDOW)
            for j in range(BINS):
                line_ref[slot, spot(i, j), :] = accs[j]
            if i < STATIC:
                fill(following, 1 - slot, span_ref[at(following)] + i * CHUNK)

        @pl.when(span_ref[at(group) + 2] > 0)
        def _():
            for i in range(BINS):
                low_row = span_ref[at(group) + 3 + i] + WINDOW

                @pl.loop(0, span_ref[at(group) + 3 + BINS + i])
                def _(t):
                    more = block(slot, i, low_row + t * MORE, MORE)
                    for j in range(BINS):
                        line_ref[slot, spot(i, j), :] = line_ref[slot, spot(i, j), :] + more[j]

    step = pl.program_id(0)

    @pl.when(step == 0)
    def _():
        weights(0, 0)
        for i in range(STATIC):
            fill(0, 0, span_ref[at(0)] + i * CHUNK)
        rest(0, 0)

    group = 2 * step
    weights(group + 1, 1)
    work(group, 0, group + 1)
    rest(group + 1, 1)
    following = jnp.minimum(group + 2, groups - 1)
    weights(following, 0)
    work(group + 1, 1, following)
    rest(following, 0)
    a, b = line_ref[0], line_ref[1]
    lanes = lax.broadcasted_iota(jnp.int32, a.shape, 1)
    new = [jnp.where(lanes < half, a, pltpu.roll(b, half, 1)), jnp.where(lanes < half, pltpu.roll(a, half, 1), b)]
    for out_ref in out_refs:
        for p in range(2):
            out_ref[p] = new[p].astype(jnp.bfloat16)


def pool(feat, table, spans, source, image, images, channels, buffer=None):
    depth = feat.shape[2]
    groups = table.shape[1]
    wide = channels * BINS * BINS
    side = depth // 2
    rows = sum(side >> k for k in range(4))
    boxes = groups * LANES // 2
    blocks = groups // 2
    pick = jnp.stack([source, image])
    out_shape = [jax.ShapeDtypeStruct((2, wide, images * boxes), jnp.bfloat16)]
    out_specs = [pl.BlockSpec((2, wide, LANES), lambda s, pick, spans: (0, 0, pick[1] * blocks + s))]
    in_specs = [
        pl.BlockSpec((None, rows * channels, depth), lambda s, pick, spans: (pick[0], 0, 0)),
        pl.BlockSpec((None, groups, 8, LANES), lambda s, pick, spans: (pick[0], 0, 0, 0)),
    ]
    operands = (pick, spans, feat, table)
    aliases = {}
    if buffer is None:
        out_shape.append(jax.ShapeDtypeStruct((2, wide, boxes), jnp.bfloat16))
        out_specs.append(pl.BlockSpec((2, wide, LANES), lambda s, pick, spans: (0, 0, s)))
    else:
        in_specs.append(pl.BlockSpec(memory_space=pl.ANY))
        operands += (buffer,)
        aliases = {4: 0}
    return pl.pallas_call(
        partial(pool_kernel, channels, side, groups, len(out_shape)),
        out_shape=out_shape,
        grid_spec=pltpu.PrefetchScalarGridSpec(
            num_scalar_prefetch=2,
            grid=(blocks,),
            in_specs=in_specs,
            out_specs=out_specs,
            scratch_shapes=[
                pltpu.VMEM((4 * side, BINS * LANES), jnp.bfloat16),
                pltpu.VMEM((4 * side, BINS * LANES), jnp.bfloat16),
                pltpu.VMEM((rows, 8, LANES), jnp.float32),
                pltpu.VMEM((rows, 8, LANES), jnp.float32),
                pltpu.VMEM((rows * channels, BINS * LANES), jnp.float32),
                pltpu.VMEM((rows * channels, BINS * LANES), jnp.float32),
                pltpu.VMEM((2, wide, LANES), jnp.float32),
            ],
        ),
        input_output_aliases=aliases,
        compiler_params=pltpu.CompilerParams(vmem_limit_bytes=44 * MIB),
        cost_estimate=pl.CostEstimate(
            flops=groups * 40 * channels * BINS * LANES * 8 * depth,
            bytes_accessed=80 * MIB,
            transcendentals=0,
        ),
        name="pool_rois",
    )(*operands)


def feature_rows(maps):
    side = maps[0].shape[-1]
    parts = [
        jnp.pad(m.transpose(0, 2, 1, 3), ((0, 0), (0, 0), (0, 0), (0, side - m.shape[-1])))
        for m in maps
    ]
    full = jnp.concatenate(parts, axis=1)
    high = lax.reduce_precision(full, 8, 7)
    low = (full - high).astype(jnp.bfloat16)
    full = jnp.concatenate([high.astype(jnp.bfloat16), low], axis=-1)
    return full.reshape(-1, 2 * side)


def box_order(boxes, levels, side):
    base = 2 * side - 2 * (side >> levels)
    key = ((boxes[..., 1] + boxes[..., 3]) >> levels) + base * 8
    key = key * key.shape[-1] + jnp.arange(key.shape[-1], dtype=jnp.int32)
    return jnp.sum((key[..., :, None] > key[..., None, :]).astype(jnp.int32), axis=-1)


def sort_boxes(boxes, levels, rank):
    count = boxes.shape[1]
    hot = (rank[:, None, :] == jnp.arange(count, dtype=jnp.int32)[:, None]).astype(jnp.bfloat16)
    both = jnp.concatenate([boxes, levels[..., None]], axis=-1).astype(jnp.bfloat16)
    return jnp.einsum("psr,prk->kps", hot, both, preferred_element_type=jnp.float32).astype(jnp.bfloat16)


def box_table(boxes, side):
    images, _, _, count = boxes.shape
    x0, y0, x1, y1, level = (boxes[:, k].astype(jnp.float32) for k in range(5))
    rows = sum(side >> k for k in range(4))
    scale = jnp.where(level < 0.5, 0.25, jnp.where(level < 1.5, 0.125, jnp.where(level < 2.5, 0.0625, 0.03125)))
    height = scale * (4 * side)
    base = 2.0 * side - 2.0 * height
    top = height - 1.0

    def axis(low, high):
        return low * scale - 0.5, ((high - low) * scale) / 7.0

    x_start, x_step = axis(x0, x1)
    y_start, y_step = axis(y0, y1)
    half = LANES // 2
    groups = count // half

    def split(v):
        return v.reshape(v.shape[:-1] + (groups, half))

    lows, highs = [], []
    for i in range(BINS):
        low = base + jnp.floor(jnp.clip(y_start + (i + 0.25) * y_step, 0.0, top))
        high = base + jnp.floor(jnp.clip(y_start + (i + 0.75) * y_step, 0.0, top)) + 1.0
        lows.append(jnp.min(split(low), axis=(1, 3)))
        highs.append(jnp.max(split(jnp.minimum(high, rows - 1.0)), axis=(1, 3)))
    low = jnp.stack(lows, axis=-1).astype(jnp.int32)
    high = jnp.stack(highs, axis=-1).astype(jnp.int32)
    least = jnp.min(low, axis=-1)
    chunks = jnp.maximum((jnp.max(high, axis=-1) - least + CHUNK) // CHUNK, STATIC)
    first = jnp.clip(rows - chunks * CHUNK, 0, least)
    extra = jnp.maximum(high - low + MORE - WINDOW, 0) // MORE
    low = jnp.minimum(low, (first + chunks * CHUNK)[..., None] - WINDOW - MORE * extra)
    heads = jnp.stack([first, chunks - STATIC, jnp.max(extra, axis=-1)], axis=-1)
    spans = jnp.concatenate([heads, low, extra], axis=-1).reshape(-1)
    zero = jnp.zeros_like(base)
    table = jnp.stack([split(v) for v in (y_start, y_step, top, base, x_start, x_step, zero, zero)])
    return table.transpose(1, 3, 0, 2, 4).reshape(images, groups, 8, LANES), spans


def adamw(weight, moment, second, grad):
    moment = BETA_ONE * moment + (1.0 - BETA_ONE) * grad
    second = BETA_TWO * second + (1.0 - BETA_TWO) * grad * grad
    fixed_m = moment / (1.0 - BETA_ONE**STEP)
    fixed_v = second / (1.0 - BETA_TWO**STEP)
    weight = weight - RATE * (fixed_m / (jnp.sqrt(fixed_v) + EPSILON) + DECAY * weight)
    return (weight, moment, second)


def update_kernel(pooled_ref, back_ref, w_ref, m_ref, v_ref, *outs):
    grad = jnp.dot(pooled_ref[...], back_ref[...], preferred_element_type=jnp.float32)
    new = adamw(w_ref[...], m_ref[...], v_ref[...], grad)
    for ref, value in zip(outs, new):
        ref[...] = value


def update_first(pooled, back, weight, moment, second):
    passes, wide, hidden = weight.shape
    boxes = pooled.shape[2]
    block = wide // BINS
    big = pl.BlockSpec((None, block, hidden), lambda p, b: (p, b, 0))
    return pl.pallas_call(
        update_kernel,
        out_shape=[jax.ShapeDtypeStruct(weight.shape, jnp.float32)] * 3,
        grid=(passes, BINS),
        in_specs=[
            pl.BlockSpec((None, block, boxes), lambda p, b: (p, b, 0)),
            pl.BlockSpec((None, boxes, hidden), lambda p, b: (p, 0, 0)),
            big,
            big,
            big,
        ],
        out_specs=[big] * 3,
        compiler_params=pltpu.CompilerParams(vmem_limit_bytes=56 * MIB),
        cost_estimate=pl.CostEstimate(
            flops=2 * passes * wide * hidden * boxes,
            bytes_accessed=passes * wide * hidden * 24 + passes * boxes * (wide + hidden) * 2,
            transcendentals=passes * wide * hidden,
        ),
        name="update_first",
    )(pooled, back, weight, moment, second)


def loss_and_slope(logits, box, count):
    place = lax.broadcasted_iota(jnp.int32, logits.shape, 1)
    is_class = place < CLASSES
    label = box[:, 0:1].astype(jnp.int32)
    weight = box[:, 1:2]
    top = jnp.max(jnp.where(is_class, logits, -jnp.inf), axis=1, keepdims=True)
    grown = jnp.where(is_class, jnp.exp(jnp.where(is_class, logits - top, 0.0)), 0.0)
    norm = jnp.sum(grown, axis=1, keepdims=True)
    hot = place == label
    picked = jnp.sum(jnp.where(hot, logits, 0.0), axis=1, keepdims=True)
    fore = jnp.where(label > 0, weight, 0.0)
    rows = weight * (top + jnp.log(norm) - picked)
    slope = weight * (grown / norm - jnp.where(hot, 1.0, 0.0))
    offset = place - (CLASSES + 4 * (label - 1))
    for k in range(4):
        mask = (offset == k) & (place >= CLASSES)
        chosen = jnp.sum(jnp.where(mask, logits, 0.0), axis=1, keepdims=True)
        differ = fore * (chosen - box[:, 2 + k : 3 + k])
        near = jnp.abs(differ)
        rows += jnp.where(near < 1.0, 0.5 * differ * differ, near - 0.5) * fore
        slope = jnp.where(mask, fore * jnp.clip(differ, -1.0, 1.0), slope)
    return rows, slope / count


def sigmoid(value):
    return 1.0 / (1.0 + jnp.exp(-value))


def head_kernel(
    images, parts, mine,
    part_ref, weight_ref, box_ref, count_ref,
    back_ref, grad_ref,
    sums, landed, own, counts, turned, cols, kept,
    rs_send, rs_recv, ag_send, ag_recv, up_send, up_recv, down_send, down_recv, own_sem,
    count_send, count_recv, col_send, col_recv, kept_send, kept_recv,
):
    me = lax.axis_index("narrow")
    level = lax.axis_index("wide")
    bits = parts.bit_length() - 1
    turn = [(1 - 2 * ((me // 2**k) % 2)) * 2**k for k in range(bits)]

    def peer(mask):
        return me + sum((turn[k] for k in range(bits) if mask >> k & 1), 0)

    links = list(range(1, bits))
    orders = [links, links[::-1]]

    barrier = pltpu.get_barrier_semaphore()
    for mask in range(1, parts):
        pl.semaphore_signal(barrier, inc=1, device_id={"narrow": peer(mask)})
    for k in range(1, images):
        pl.semaphore_signal(barrier, inc=1, device_id={"wide": lax.rem(level + k, images)})
    pl.semaphore_wait(barrier, parts + images - 2)

    counting = []
    for k in range(1, images):
        counting.append(
            pltpu.make_async_remote_copy(
                src_ref=count_ref,
                dst_ref=counts.at[k],
                send_sem=count_send.at[k],
                recv_sem=count_recv.at[k],
                device_id={"wide": lax.rem(level + k, images)},
            )
        )

    def scatter(p, mask, bit, source):
        return pltpu.make_async_remote_copy(
            src_ref=source,
            dst_ref=landed.at[p, mask],
            send_sem=rs_send.at[p, mask],
            recv_sem=rs_recv.at[p, mask],
            device_id={"narrow": peer(1 << bit)},
        )

    def part_at(p, mask):
        return part_ref.at[p, pl.ds(pl.multiple_of(peer(mask) * mine, mine), mine), :]

    copies = {}
    for p in range(2):
        for mask in range(1, parts, 2):
            copies[p, mask] = scatter(p, mask, 0, part_at(p, mask))
            copies[p, mask].start()

    def stage(p, at):
        order = [0] + orders[p]
        bit = order[at - 1]
        seen = sum(1 << b for b in order[:at])
        for mask in range(parts):
            if mask & seen:
                continue
            copies[p, mask | 1 << bit].wait_recv()
            if at == 1:
                have = part_ref[p, pl.ds(pl.multiple_of(peer(mask) * mine, mine), mine), :]
            else:
                have = sums[p, mask]
            sums[p, mask] = have + landed[p, mask | 1 << bit]
            if at < bits and mask >> order[at] & 1:
                copies[p, mask] = scatter(p, mask, order[at], sums.at[p, mask])
                copies[p, mask].start()

    for copy in counting:
        copy.start()
    for at in range(1, bits):
        for p in range(2):
            stage(p, at)

    def rows(p, image, mask):
        place = (image * parts + peer(mask)) * mine
        return back_ref.at[p, pl.ds(pl.multiple_of(place, mine), mine), :]

    def hop(p, d, up, source=None):
        image = level - d if up else level + d
        spot = rows(p, image, 0)
        return pltpu.make_async_remote_copy(
            src_ref=spot if source is None else source,
            dst_ref=spot,
            send_sem=(up_send if up else down_send).at[p, d],
            recv_sem=(up_recv if up else down_recv).at[p, d],
            device_id={"wide": level + 1 if up else level - 1},
        )

    def came(p, d, up):
        image = level - d if up else level + d
        spot = rows(p, image, 0)
        pltpu.make_async_remote_copy(
            src_ref=spot, dst_ref=spot, send_sem=(up_send if up else down_send).at[p, d],
            recv_sem=(up_recv if up else down_recv).at[p, d - 1],
            device_id={"wide": level - 1 if up else level + 1},
        ).wait_recv()

    steps = [orders[p] + [0] for p in range(2)]

    def masks_before(p, at):
        seen = sum(1 << b for b in steps[p][:at])
        return [m for m in range(parts) if not m & ~seen]

    def doubling(spot, send, recv):
        def spread(p, key, mask, bit, source=None):
            there = mask | 1 << bit
            return pltpu.make_async_remote_copy(
                src_ref=spot(p, key, mask) if source is None else source,
                dst_ref=spot(p, key, mask),
                send_sem=send.at[p, key, there],
                recv_sem=recv.at[p, key, there],
                device_id={"narrow": peer(1 << bit)},
            )

        def arrive(p, key, at):
            for m in masks_before(p, at):
                there = m | 1 << steps[p][at]
                pltpu.make_async_remote_copy(
                    src_ref=spot(p, key, there),
                    dst_ref=spot(p, key, there),
                    send_sem=send.at[p, key, there],
                    recv_sem=recv.at[p, key, there],
                    device_id={"narrow": peer(1)},
                ).wait_recv()

        def advance(p, key, at, source=None):
            if at:
                arrive(p, key, at - 1)
            for m in masks_before(p, at):
                spread(p, key, m, steps[p][at], source if m == 0 else None).start()

        def sent(p, key):
            for at in range(bits):
                for m in masks_before(p, at):
                    spread(p, key, m, steps[p][at]).wait_send()

        return advance, arrive, sent

    advance, arrive, sent = doubling(rows, ag_send, ag_recv)
    advance_kept, arrive_kept, sent_kept = doubling(
        lambda p, key, mask: kept.at[p, peer(mask)], kept_send, kept_recv
    )

    def finish(p, image):
        arrive(p, image, bits - 1)
        sent(p, image)

    span = grad_ref.shape[1]

    def columns(p, mask):
        return turned.at[p, :, pl.ds(pl.multiple_of(peer(mask) * span, span), span), :]

    def hand(p, mask):
        return pltpu.make_async_remote_copy(
            src_ref=columns(p, mask),
            dst_ref=cols.at[p, mask],
            send_sem=col_send.at[p, mask],
            recv_sem=col_recv.at[p, mask],
            device_id={"narrow": peer(mask)},
        )

    for copy in counting:
        copy.wait_recv()
    count = count_ref[0:1, 0:1] + sum(counts[k, 0:1, 0:1] for k in range(1, images))
    hidden = part_ref.shape[2]
    for p in range(2):
        stage(p, bits)
        pre1 = sums[p, 0]
        sig1 = sigmoid(pre1)
        hid1 = (pre1 * sig1).astype(jnp.bfloat16)
        pre2 = jnp.dot(hid1, weight_ref[p, :, :hidden], preferred_element_type=jnp.float32)
        sig2 = sigmoid(pre2)
        hid2 = (pre2 * sig2).astype(jnp.bfloat16)
        logits = jnp.dot(hid2, weight_ref[p, :, hidden:], preferred_element_type=jnp.float32)
        loss, slope = loss_and_slope(logits, box_ref[p], count)
        back_z = slope.astype(jnp.bfloat16)
        across = (((1,), (1,)), ((), ()))
        back_h2 = lax.dot_general(back_z, weight_ref[p, :, hidden:], across, preferred_element_type=jnp.float32)
        back_p2 = (back_h2 * (sig2 * (1.0 + pre2 * (1.0 - sig2)))).astype(jnp.bfloat16)
        back_h1 = lax.dot_general(back_p2, weight_ref[p, :, :hidden], across, preferred_element_type=jnp.float32)
        own[p] = (back_h1 * (sig1 * (1.0 + pre1 * (1.0 - sig1)))).astype(jnp.bfloat16)

        @pl.when(level < images - 1)
        def _():
            hop(p, 0, True, own.at[p]).start()

        @pl.when(level > 0)
        def _():
            hop(p, 0, False, own.at[p]).start()

        advance(p, level, 0, own.at[p])
        pltpu.make_async_copy(own.at[p], rows(p, level, 0), own_sem.at[p]).start()
        place = lax.broadcasted_iota(jnp.int32, (mine, LANES), 1)
        losses = jnp.zeros((mine, LANES), jnp.float32)
        for k in range(3):
            near = loss.astype(jnp.bfloat16).astype(jnp.float32)
            losses = jnp.where(place == k, near, losses)
            loss = loss - near
        at = 0
        for value in (back_p2, back_z, losses.astype(jnp.bfloat16)):
            kept[p, me, :, at : at + value.shape[1]] = value
            at += value.shape[1]
        advance_kept(p, 0, 0)
        turned[p, 0] = hid1.T
        turned[p, 1] = hid2.T
        for mask in range(1, parts):
            hand(p, mask).start()
    for p in range(2):
        pltpu.make_async_copy(own.at[p], rows(p, level, 0), own_sem.at[p]).wait()

    def each_side(d, do):
        @pl.when(level >= d)
        def _():
            do(level - d, True)

        @pl.when(level + d < images)
        def _():
            do(level + d, False)

    def enter(d):
        def do(image, up):
            for p in range(2):
                came(p, d, up)

                @pl.when((level < images - 1) if up else (level > 0))
                def _():
                    hop(p, d, up).start()

                advance(p, image, 0)

        each_side(d, do)

    def go_on(d, at):
        if d == 0:
            for p in range(2):
                advance(p, level, at)
                advance_kept(p, 0, at)
        else:

            def do(image, up):
                for p in range(2):
                    advance(p, image, at)

            each_side(d, do)

    for tick in range(1, images + bits - 1):
        for d in range(images):
            at = tick - d
            if at == 0:
                enter(d)
            elif 0 < at < bits:
                go_on(d, at)

    loss = jnp.zeros((1, 1), jnp.float32)
    for p in range(2):
        arrive_kept(p, 0, bits - 1)
        two, head = [], []
        for mask in range(parts):
            if mask:
                hand(p, mask).wait_recv()
            mine_ref = cols.at[p, mask] if mask else columns(p, 0)
            slopes = kept.at[p, peer(mask)]
            two.append(jnp.dot(mine_ref[0], slopes[:, :hidden], preferred_element_type=jnp.float32))
            head.append(jnp.dot(mine_ref[1], slopes[:, hidden:-LANES], preferred_element_type=jnp.float32))
            loss += jnp.sum(slopes[:, -LANES:].astype(jnp.float32), keepdims=True)
        grad_ref[p, :, :hidden] = sum(two)
        grad_ref[p, :, hidden:] = sum(head)
    corner = grad_ref[0, 0:8, grad_ref.shape[2] - LANES :]
    place = [lax.broadcasted_iota(jnp.int32, corner.shape, k) for k in range(2)]
    corner = jnp.where((place[0] == 0) & (place[1] == LANES - 1), loss, corner)
    grad_ref[0, 0:8, grad_ref.shape[2] - LANES :] = corner

    for p in range(2):
        finish(p, level)
        sent_kept(p, 0)
        for mask in range(1, parts):
            hand(p, mask).wait_send()

        @pl.when(level < images - 1)
        def _():
            hop(p, 0, True).wait_send()

        @pl.when(level > 0)
        def _():
            hop(p, 0, False).wait_send()

    for d in range(1, images):

        def do(image, up):
            for p in range(2):
                finish(p, image)

                @pl.when((level < images - 1) if up else (level > 0))
                def _():
                    hop(p, d, up).wait_send()

        each_side(d, do)
    for p in range(2):
        for mask in range(1, parts):
            copies[p, mask].wait_send()
    for copy in counting:
        copy.wait_send()


def head_step(part, weight, box, count, images, parts):
    passes, boxes, hidden = part.shape
    mine = boxes // parts
    outs = weight.shape[2] - hidden
    span = hidden // parts
    low = jnp.bfloat16
    vmem = pl.BlockSpec(memory_space=pltpu.VMEM)
    dma = pltpu.SemaphoreType.DMA
    return pl.pallas_call(
        partial(head_kernel, images, parts, mine),
        out_shape=[
            jax.ShapeDtypeStruct((passes, images * boxes, hidden), low),
            jax.ShapeDtypeStruct((passes, span, hidden + outs), jnp.float32),
        ],
        in_specs=[vmem] * 4,
        out_specs=[pl.BlockSpec(memory_space=pl.ANY), vmem],
        scratch_shapes=[
            pltpu.VMEM((passes, parts, mine, hidden), jnp.float32),
            pltpu.VMEM((passes, parts, mine, hidden), jnp.float32),
            pltpu.VMEM((passes, mine, hidden), low),
            pltpu.VMEM((images, 8, LANES), jnp.float32),
            pltpu.VMEM((passes, 2, hidden, mine), low),
            pltpu.VMEM((passes, parts, 2, span, mine), low),
            pltpu.VMEM((passes, parts, mine, hidden + outs + LANES), low),
            dma((passes, parts)),
            dma((passes, parts)),
            dma((passes, images, parts)),
            dma((passes, images, parts)),
            dma((passes, images)),
            dma((passes, images)),
            dma((passes, images)),
            dma((passes, images)),
            dma((passes,)),
            dma((images,)),
            dma((images,)),
            dma((passes, parts)),
            dma((passes, parts)),
            dma((passes, 1, parts)),
            dma((passes, 1, parts)),
        ],
        compiler_params=pltpu.CompilerParams(
            vmem_limit_bytes=48 * MIB, collective_id=0, has_side_effects=True
        ),
        cost_estimate=pl.CostEstimate(
            flops=8 * passes * mine * hidden * (hidden + outs),
            bytes_accessed=100 * MIB,
            transcendentals=4 * passes * mine * hidden,
        ),
        name="head_step",
    )(part, weight, box, count)


def small_kernel(grad_ref, *refs):
    at = 0
    for k in range(2):
        weight, moment, second = (r[...] for r in refs[3 * k : 3 * k + 3])
        new = adamw(weight, moment, second, grad_ref[:, at : at + weight.shape[1]])
        for ref, value in zip(refs[6 + 3 * k : 9 + 3 * k], new):
            ref[...] = value
        at += weight.shape[1]


def update_small(grad, *arrays):
    def spec(x):
        return pl.BlockSpec((None,) + x.shape[1:], lambda p: (p, 0, 0))

    return pl.pallas_call(
        small_kernel,
        out_shape=[jax.ShapeDtypeStruct(x.shape, jnp.float32) for x in arrays],
        grid=(grad.shape[0],),
        in_specs=[spec(x) for x in (grad,) + arrays],
        out_specs=[spec(x) for x in arrays],
        compiler_params=pltpu.CompilerParams(vmem_limit_bytes=24 * MIB),
        name="update_small",
    )(grad, *arrays)


def per_device(
    feat_p2, feat_p3, feat_p4, feat_p5, rois, levels, labels, sampled, targets,
    fc1_w, fc1_m, fc1_v, fc2_w, fc2_m, fc2_v, head_w, head_m, head_v,
):
    side = feat_p2.shape[-1]
    channels = feat_p2.shape[1]
    boxes = rois.shape[2]
    images = lax.axis_size("wide")
    mine = boxes // lax.axis_size("narrow")
    first = lax.axis_index("narrow") * mine
    level = lax.axis_index("wide").astype(jnp.int32)
    parts = lax.axis_size("narrow")
    hidden = fc2_w.shape[2]
    outs = head_w.shape[2]
    zero = jnp.zeros((), jnp.int32)
    rank = box_order(rois[:, 0], levels[:, 0], side)
    ordered = sort_boxes(rois[:, 0], levels[:, 0], rank)
    feat = feature_rows((feat_p2, feat_p3, feat_p4, feat_p5))
    height = feat.shape[0]
    flags = sampled[:, 0].astype(jnp.bfloat16).reshape(1, 2, boxes)
    both = jnp.concatenate([feat, jnp.concatenate([ordered, flags]).reshape(-1, LANES)])
    weight = jnp.concatenate([fc2_w, jnp.pad(head_w, ((0, 0), (0, 0), (0, -outs % LANES)))], axis=2)
    weight = lax.all_gather(weight.astype(jnp.bfloat16), "narrow", axis=1, tiled=True)
    counted = jnp.sum(sampled).astype(jnp.float32)
    table, spans = box_table(ordered[None], side)
    pooled, own = pool(feat[None], table, spans, zero, level, images, channels)
    w1 = fc1_w.astype(jnp.bfloat16)
    part = lax.dot_general(own, w1, (((1,), (1,)), ((0,), (0,))), preferred_element_type=jnp.float32)
    both, weight, part = lax.optimization_barrier((both, weight, part))
    feats = lax.all_gather(both, "wide", axis=0)
    hot = rank[:, None, :] == first + jnp.arange(mine, dtype=jnp.int32)[:, None]

    def pick(values):
        return jnp.sum(jnp.where(hot, values[:, 0].astype(jnp.float32)[:, None, :], 0), axis=-1)

    box = [pick(labels), pick(sampled)] + [pick(targets[..., k]) for k in range(4)]
    box = jnp.pad(jnp.stack(box, axis=-1), ((0, 0), (0, 0), (0, LANES - 6)))
    back, grad = head_step(part, weight, box, jnp.full((8, LANES), counted), images, parts)
    grad = lax.psum_scatter(grad, "wide", scatter_dimension=1, tiled=True)

    tails = feats[:, height:].reshape(images, 6, 2, boxes)
    count = jnp.sum(tails[:, 5].astype(jnp.float32))
    tables, all_spans = box_table(tails[:, :5], side)
    turn = [lax.rem(level + k, images) for k in range(1, images)]
    for k in range(images - 1):
        pooled = pool(feats, tables, all_spans, turn[k], turn[k], images, channels, pooled)[0]
        if k == max(images - 3, 0):
            grad, pooled = lax.optimization_barrier((grad, pooled))
            grad = lax.all_gather(grad, "wide", axis=1, tiled=True)
    new1 = update_first(pooled, back, fc1_w, fc1_m, fc1_v)
    grad, new1 = lax.optimization_barrier((grad, new1))
    total = grad[0, 0, -1]
    new = update_small(grad, fc2_w, fc2_m, fc2_v, head_w, head_m, head_v)
    return (jnp.stack([total, count]),) + tuple(new1) + tuple(new)


def solution(mesh):
    maps = P("wide", "narrow", None, None)
    rows = P(None, "narrow", None)
    box = P(None, "wide", None)
    coords = P(None, "wide", None, None)
    return jax.shard_map(
        per_device,
        mesh=mesh,
        in_specs=(maps,) * 4 + (coords, box, box, box, coords) + (rows,) * 9,
        out_specs=(P(),) + (rows,) * 9,
        check_vma=False,
    )
```

```python
from functools import partial

import jax
import jax.numpy as jnp
from jax import lax
from jax.experimental import pallas as pl
from jax.experimental.pallas import tpu as pltpu
from jax.sharding import PartitionSpec as P

CLASSES = 81
STEP = 5
BETA_ONE = 0.5
BETA_TWO = 0.5
RATE = 0.02
DECAY = 0.01
EPSILON = 1e-08
BINS = 7
CHUNK = 8
STATIC = 5
WINDOW = 24
MORE = 4
SPANS = 17
LANES = 128
MIB = 2**20


def tent(where, cells):
    return 0.5 * sum(jnp.maximum(0.0, 1.0 - jnp.abs(w - cells)) for w in where)


def pool_kernel(channels, side, groups, copies, pick_ref, span_ref, feat_ref, table_ref, *refs):
    out_refs = refs[-7 - copies : -7]
    cols, rows, parts = refs[-7:-5], refs[-5:-3], refs[-3:-1]
    line_ref = refs[-1]
    image = pick_ref[0]
    half = LANES // 2
    offsets = (0.25, 0.75)
    cells = lax.broadcasted_iota(jnp.int32, (side, LANES), 0).astype(jnp.float32)
    bins = lax.broadcasted_iota(jnp.int32, (8, LANES), 0).astype(jnp.float32)

    def at(group):
        return (image * groups + group) * SPANS

    def param(group, k):
        return table_ref[group, k : k + 1, :]

    def weights(group, slot):
        top, x_start, x_step = param(group, 2), param(group, 4), param(group, 5)
        for j in range(BINS):
            where = [jnp.clip(x_start + (j + off) * x_step, 0.0, top) for off in offsets]
            weight = tent(where, cells)
            high = weight.astype(jnp.bfloat16)
            low = (weight - high.astype(jnp.float32)).astype(jnp.bfloat16)
            lanes = pl.ds(j * LANES, LANES)
            cols[slot][0:side, lanes] = high
            cols[slot][side : 2 * side, lanes] = high
            cols[slot][2 * side : 3 * side, lanes] = low
            cols[slot][3 * side : 4 * side, lanes] = low

    def fill(group, slot, row):
        y_start, y_step, top, base = (param(group, k) for k in range(4))
        where = [jnp.clip(y_start + (bins + off) * y_step, 0.0, top) for off in offsets]
        for h in range(CHUNK):
            rows[slot][row + h] = tent(where, (row + h).astype(jnp.float32) - base)
        place = pl.ds(pl.multiple_of(row * channels, channels), CHUNK * channels)
        left = feat_ref[place, :]
        left = jnp.concatenate([left, left], axis=1)
        parts[slot][place, :] = jnp.dot(left, cols[slot][...], preferred_element_type=jnp.float32)

    def rest(group, slot):
        first = span_ref[at(group)] + STATIC * CHUNK

        @pl.loop(0, span_ref[at(group) + 1])
        def _(t):
            fill(group, slot, first + t * CHUNK)

    def block(slot, i, low_row, count):
        accs = None
        for h in range(count):
            start = pl.multiple_of((low_row + h) * channels, channels)
            weight = jnp.broadcast_to(rows[slot][low_row + h, i : i + 1, :], (channels, LANES))
            new = [
                weight * parts[slot][pl.ds(start, channels), j * LANES : (j + 1) * LANES] for j in range(BINS)
            ]
            accs = new if accs is None else [x + y for x, y in zip(accs, new)]
        return accs

    def spot(i, j):
        return pl.ds(i * BINS + j, channels, stride=BINS * BINS)

    def work(group, slot, following):
        for i in range(BINS):
            accs = block(slot, i, span_ref[at(group) + 3 + i], WINDOW)
            for j in range(BINS):
                line_ref[slot, spot(i, j), :] = accs[j]
            if i < STATIC:
                fill(following, 1 - slot, span_ref[at(following)] + i * CHUNK)

        @pl.when(span_ref[at(group) + 2] > 0)
        def _():
            for i in range(BINS):
                low_row = span_ref[at(group) + 3 + i] + WINDOW

                @pl.loop(0, span_ref[at(group) + 3 + BINS + i])
                def _(t):
                    more = block(slot, i, low_row + t * MORE, MORE)
                    for j in range(BINS):
                        line_ref[slot, spot(i, j), :] = line_ref[slot, spot(i, j), :] + more[j]

    step = pl.program_id(0)

    @pl.when(step == 0)
    def _():
        weights(0, 0)
        for i in range(STATIC):
            fill(0, 0, span_ref[at(0)] + i * CHUNK)
        rest(0, 0)

    group = 2 * step
    weights(group + 1, 1)
    work(group, 0, group + 1)
    rest(group + 1, 1)
    following = jnp.minimum(group + 2, groups - 1)
    weights(following, 0)
    work(group + 1, 1, following)
    rest(following, 0)
    a, b = line_ref[0], line_ref[1]
    lanes = lax.broadcasted_iota(jnp.int32, a.shape, 1)
    new = [jnp.where(lanes < half, a, pltpu.roll(b, half, 1)), jnp.where(lanes < half, pltpu.roll(a, half, 1), b)]
    for out_ref in out_refs:
        for p in range(2):
            out_ref[p] = new[p].astype(jnp.bfloat16)


def pool(feat, table, spans, source, image, images, channels, buffer=None):
    depth = feat.shape[2]
    groups = table.shape[1]
    wide = channels * BINS * BINS
    side = depth // 2
    rows = sum(side >> k for k in range(4))
    boxes = groups * LANES // 2
    blocks = groups // 2
    pick = jnp.stack([source, image])
    out_shape = [jax.ShapeDtypeStruct((2, wide, images * boxes), jnp.bfloat16)]
    out_specs = [pl.BlockSpec((2, wide, LANES), lambda s, pick, spans: (0, 0, pick[1] * blocks + s))]
    in_specs = [
        pl.BlockSpec((None, rows * channels, depth), lambda s, pick, spans: (pick[0], 0, 0)),
        pl.BlockSpec((None, groups, 8, LANES), lambda s, pick, spans: (pick[0], 0, 0, 0)),
    ]
    operands = (pick, spans, feat, table)
    aliases = {}
    if buffer is None:
        out_shape.append(jax.ShapeDtypeStruct((2, wide, boxes), jnp.bfloat16))
        out_specs.append(pl.BlockSpec((2, wide, LANES), lambda s, pick, spans: (0, 0, s)))
    else:
        in_specs.append(pl.BlockSpec(memory_space=pl.ANY))
        operands += (buffer,)
        aliases = {4: 0}
    return pl.pallas_call(
        partial(pool_kernel, channels, side, groups, len(out_shape)),
        out_shape=out_shape,
        grid_spec=pltpu.PrefetchScalarGridSpec(
            num_scalar_prefetch=2,
            grid=(blocks,),
            in_specs=in_specs,
            out_specs=out_specs,
            scratch_shapes=[
                pltpu.VMEM((4 * side, BINS * LANES), jnp.bfloat16),
                pltpu.VMEM((4 * side, BINS * LANES), jnp.bfloat16),
                pltpu.VMEM((rows, 8, LANES), jnp.float32),
                pltpu.VMEM((rows, 8, LANES), jnp.float32),
                pltpu.VMEM((rows * channels, BINS * LANES), jnp.float32),
                pltpu.VMEM((rows * channels, BINS * LANES), jnp.float32),
                pltpu.VMEM((2, wide, LANES), jnp.float32),
            ],
        ),
        input_output_aliases=aliases,
        compiler_params=pltpu.CompilerParams(vmem_limit_bytes=60 * MIB),
        cost_estimate=pl.CostEstimate(
            flops=groups * 40 * channels * BINS * LANES * 8 * depth,
            bytes_accessed=80 * MIB,
            transcendentals=0,
        ),
        name="pool_rois",
    )(*operands)


def feature_rows(maps):
    side = maps[0].shape[-1]
    parts = [
        jnp.pad(m.transpose(0, 2, 1, 3), ((0, 0), (0, 0), (0, 0), (0, side - m.shape[-1])))
        for m in maps
    ]
    full = jnp.concatenate(parts, axis=1)
    high = lax.reduce_precision(full, 8, 7)
    low = (full - high).astype(jnp.bfloat16)
    full = jnp.concatenate([high.astype(jnp.bfloat16), low], axis=-1)
    return full.reshape(-1, 2 * side)


def box_order(boxes, levels, side):
    base = 2 * side - 2 * (side >> levels)
    key = ((boxes[..., 1] + boxes[..., 3]) >> levels) + base * 8
    key = key * key.shape[-1] + jnp.arange(key.shape[-1], dtype=jnp.int32)
    return jnp.sum((key[..., :, None] > key[..., None, :]).astype(jnp.int32), axis=-1)


def sort_boxes(boxes, levels, rank):
    count = boxes.shape[1]
    hot = (rank[:, None, :] == jnp.arange(count, dtype=jnp.int32)[:, None]).astype(jnp.bfloat16)
    both = jnp.concatenate([boxes, levels[..., None]], axis=-1).astype(jnp.bfloat16)
    return jnp.einsum("psr,prk->kps", hot, both, preferred_element_type=jnp.float32).astype(jnp.bfloat16)


def box_table(boxes, side):
    images, _, _, count = boxes.shape
    x0, y0, x1, y1, level = (boxes[:, k].astype(jnp.float32) for k in range(5))
    rows = sum(side >> k for k in range(4))
    scale = jnp.where(level < 0.5, 0.25, jnp.where(level < 1.5, 0.125, jnp.where(level < 2.5, 0.0625, 0.03125)))
    height = scale * (4 * side)
    base = 2.0 * side - 2.0 * height
    top = height - 1.0

    def axis(low, high):
        return low * scale - 0.5, ((high - low) * scale) / 7.0

    x_start, x_step = axis(x0, x1)
    y_start, y_step = axis(y0, y1)
    half = LANES // 2
    groups = count // half

    def split(v):
        return v.reshape(v.shape[:-1] + (groups, half))

    lows, highs = [], []
    for i in range(BINS):
        low = base + jnp.floor(jnp.clip(y_start + (i + 0.25) * y_step, 0.0, top))
        high = base + jnp.floor(jnp.clip(y_start + (i + 0.75) * y_step, 0.0, top)) + 1.0
        lows.append(jnp.min(split(low), axis=(1, 3)))
        highs.append(jnp.max(split(jnp.minimum(high, rows - 1.0)), axis=(1, 3)))
    low = jnp.stack(lows, axis=-1).astype(jnp.int32)
    high = jnp.stack(highs, axis=-1).astype(jnp.int32)
    least = jnp.min(low, axis=-1)
    chunks = jnp.maximum((jnp.max(high, axis=-1) - least + CHUNK) // CHUNK, STATIC)
    first = jnp.clip(rows - chunks * CHUNK, 0, least)
    extra = jnp.maximum(high - low + MORE - WINDOW, 0) // MORE
    low = jnp.minimum(low, (first + chunks * CHUNK)[..., None] - WINDOW - MORE * extra)
    heads = jnp.stack([first, chunks - STATIC, jnp.max(extra, axis=-1)], axis=-1)
    spans = jnp.concatenate([heads, low, extra], axis=-1).reshape(-1)
    zero = jnp.zeros_like(base)
    table = jnp.stack([split(v) for v in (y_start, y_step, top, base, x_start, x_step, zero, zero)])
    return table.transpose(1, 3, 0, 2, 4).reshape(images, groups, 8, LANES), spans


def adamw(weight, moment, second, grad):
    moment = BETA_ONE * moment + (1.0 - BETA_ONE) * grad
    second = BETA_TWO * second + (1.0 - BETA_TWO) * grad * grad
    fixed_m = moment / (1.0 - BETA_ONE**STEP)
    fixed_v = second / (1.0 - BETA_TWO**STEP)
    weight = weight - RATE * (fixed_m / (jnp.sqrt(fixed_v) + EPSILON) + DECAY * weight)
    return (weight, moment, second)


def update_kernel(pooled_ref, back_ref, w_ref, m_ref, v_ref, *outs):
    grad = jnp.dot(pooled_ref[...], back_ref[...], preferred_element_type=jnp.float32)
    new = adamw(w_ref[...], m_ref[...], v_ref[...], grad)
    for ref, value in zip(outs, new):
        ref[...] = value


def update_first(pooled, back, weight, moment, second):
    passes, wide, hidden = weight.shape
    boxes = pooled.shape[2]
    block = wide // BINS
    big = pl.BlockSpec((None, block, hidden), lambda p, b: (p, b, 0))
    return pl.pallas_call(
        update_kernel,
        out_shape=[jax.ShapeDtypeStruct(weight.shape, jnp.float32)] * 3,
        grid=(passes, BINS),
        in_specs=[
            pl.BlockSpec((None, block, boxes), lambda p, b: (p, b, 0)),
            pl.BlockSpec((None, boxes, hidden), lambda p, b: (p, 0, 0)),
            big,
            big,
            big,
        ],
        out_specs=[big] * 3,
        compiler_params=pltpu.CompilerParams(vmem_limit_bytes=60 * MIB),
        cost_estimate=pl.CostEstimate(
            flops=2 * passes * wide * hidden * boxes,
            bytes_accessed=passes * wide * hidden * 24 + passes * boxes * (wide + hidden) * 2,
            transcendentals=passes * wide * hidden,
        ),
        name="update_first",
    )(pooled, back, weight, moment, second)


def loss_and_slope(logits, box, count):
    place = lax.broadcasted_iota(jnp.int32, logits.shape, 1)
    is_class = place < CLASSES
    label = box[:, 0:1].astype(jnp.int32)
    weight = box[:, 1:2]
    top = jnp.max(jnp.where(is_class, logits, -jnp.inf), axis=1, keepdims=True)
    grown = jnp.where(is_class, jnp.exp(jnp.where(is_class, logits - top, 0.0)), 0.0)
    norm = jnp.sum(grown, axis=1, keepdims=True)
    hot = place == label
    picked = jnp.sum(jnp.where(hot, logits, 0.0), axis=1, keepdims=True)
    fore = jnp.where(label > 0, weight, 0.0)
    rows = weight * (top + jnp.log(norm) - picked)
    slope = weight * (grown / norm - jnp.where(hot, 1.0, 0.0))
    offset = place - (CLASSES + 4 * (label - 1))
    for k in range(4):
        mask = (offset == k) & (place >= CLASSES)
        chosen = jnp.sum(jnp.where(mask, logits, 0.0), axis=1, keepdims=True)
        differ = fore * (chosen - box[:, 2 + k : 3 + k])
        near = jnp.abs(differ)
        rows += jnp.where(near < 1.0, 0.5 * differ * differ, near - 0.5) * fore
        slope = jnp.where(mask, fore * jnp.clip(differ, -1.0, 1.0), slope)
    return rows, slope / count


def sigmoid(value):
    return 1.0 / (1.0 + jnp.exp(-value))


def head_kernel(
    images, parts, mine,
    part_ref, weight_ref, box_ref, count_ref,
    back_ref, grad_ref,
    sums, landed, own, counts, split, cols, kept,
    rs_send, rs_recv, ag_send, ag_recv, up_send, up_recv, down_send, down_recv, own_sem,
    count_send, count_recv, col_send, col_recv, kept_send, kept_recv,
):
    me = lax.axis_index("narrow")
    level = lax.axis_index("wide")
    bits = parts.bit_length() - 1
    turn = [(1 - 2 * ((me // 2**k) % 2)) * 2**k for k in range(bits)]

    def peer(mask):
        return me + sum((turn[k] for k in range(bits) if mask >> k & 1), 0)

    links = list(range(1, bits))
    orders = [links, links[::-1]]

    barrier = pltpu.get_barrier_semaphore()
    for mask in range(1, parts):
        pl.semaphore_signal(barrier, inc=1, device_id={"narrow": peer(mask)})
    for k in range(1, images):
        pl.semaphore_signal(barrier, inc=1, device_id={"wide": lax.rem(level + k, images)})
    pl.semaphore_wait(barrier, parts + images - 2)

    counting = []
    for k in range(1, images):
        counting.append(
            pltpu.make_async_remote_copy(
                src_ref=count_ref,
                dst_ref=counts.at[k],
                send_sem=count_send.at[k],
                recv_sem=count_recv.at[k],
                device_id={"wide": lax.rem(level + k, images)},
            )
        )

    def scatter(p, mask, bit, source):
        return pltpu.make_async_remote_copy(
            src_ref=source,
            dst_ref=landed.at[p, mask],
            send_sem=rs_send.at[p, mask],
            recv_sem=rs_recv.at[p, mask],
            device_id={"narrow": peer(1 << bit)},
        )

    def part_at(p, mask):
        return part_ref.at[p, pl.ds(pl.multiple_of(peer(mask) * mine, mine), mine), :]

    copies = {}
    for p in range(2):
        for mask in range(1, parts, 2):
            copies[p, mask] = scatter(p, mask, 0, part_at(p, mask))
            copies[p, mask].start()

    def stage(p, at):
        order = [0] + orders[p]
        bit = order[at - 1]
        seen = sum(1 << b for b in order[:at])
        for mask in range(parts):
            if mask & seen:
                continue
            copies[p, mask | 1 << bit].wait_recv()
            if at == 1:
                have = part_ref[p, pl.ds(pl.multiple_of(peer(mask) * mine, mine), mine), :]
            else:
                have = sums[p, mask]
            sums[p, mask] = have + landed[p, mask | 1 << bit]
            if at < bits and mask >> order[at] & 1:
                copies[p, mask] = scatter(p, mask, order[at], sums.at[p, mask])
                copies[p, mask].start()

    for copy in counting:
        copy.start()
    for at in range(1, bits):
        for p in range(2):
            stage(p, at)

    def rows(p, image, mask):
        place = (image * parts + peer(mask)) * mine
        return back_ref.at[p, pl.ds(pl.multiple_of(place, mine), mine), :]

    def hop(p, d, up, source=None):
        image = level - d if up else level + d
        spot = rows(p, image, 0)
        return pltpu.make_async_remote_copy(
            src_ref=spot if source is None else source,
            dst_ref=spot,
            send_sem=(up_send if up else down_send).at[p, d],
            recv_sem=(up_recv if up else down_recv).at[p, d],
            device_id={"wide": level + 1 if up else level - 1},
        )

    def came(p, d, up):
        image = level - d if up else level + d
        spot = rows(p, image, 0)
        pltpu.make_async_remote_copy(
            src_ref=spot, dst_ref=spot, send_sem=(up_send if up else down_send).at[p, d],
            recv_sem=(up_recv if up else down_recv).at[p, d - 1],
            device_id={"wide": level - 1 if up else level + 1},
        ).wait_recv()

    steps = [orders[p] + [0] for p in range(2)]

    def masks_before(p, at):
        seen = sum(1 << b for b in steps[p][:at])
        return [m for m in range(parts) if not m & ~seen]

    def doubling(spot, send, recv):
        def spread(p, key, mask, bit, source=None):
            there = mask | 1 << bit
            return pltpu.make_async_remote_copy(
                src_ref=spot(p, key, mask) if source is None else source,
                dst_ref=spot(p, key, mask),
                send_sem=send.at[p, key, there],
                recv_sem=recv.at[p, key, there],
                device_id={"narrow": peer(1 << bit)},
            )

        def arrive(p, key, at):
            for m in masks_before(p, at):
                there = m | 1 << steps[p][at]
                pltpu.make_async_remote_copy(
                    src_ref=spot(p, key, there),
                    dst_ref=spot(p, key, there),
                    send_sem=send.at[p, key, there],
                    recv_sem=recv.at[p, key, there],
                    device_id={"narrow": peer(1)},
                ).wait_recv()

        def advance(p, key, at, source=None):
            if at:
                arrive(p, key, at - 1)
            for m in masks_before(p, at):
                spread(p, key, m, steps[p][at], source if m == 0 else None).start()

        def sent(p, key):
            for at in range(bits):
                for m in masks_before(p, at):
                    spread(p, key, m, steps[p][at]).wait_send()

        return advance, arrive, sent

    advance, arrive, sent = doubling(rows, ag_send, ag_recv)
    advance_kept, arrive_kept, sent_kept = doubling(
        lambda p, key, mask: kept.at[p, peer(mask)], kept_send, kept_recv
    )

    def finish(p, image):
        arrive(p, image, bits - 1)
        sent(p, image)

    span = grad_ref.shape[1]

    def hand(p, mask):
        return pltpu.make_async_remote_copy(
            src_ref=split.at[p, :, peer(mask)],
            dst_ref=cols.at[p, :, me],
            send_sem=col_send.at[p, mask],
            recv_sem=col_recv.at[p, mask],
            device_id={"narrow": peer(mask)},
        )

    def handed(p, mask):
        spot = cols.at[p, :, peer(mask)]
        pltpu.make_async_remote_copy(
            src_ref=spot, dst_ref=spot, send_sem=col_send.at[p, mask], recv_sem=col_recv.at[p, mask],
            device_id={"narrow": peer(mask)},
        ).wait_recv()

    for copy in counting:
        copy.wait_recv()
    count = count_ref[0:1, 0:1] + sum(counts[k, 0:1, 0:1] for k in range(1, images))
    hidden = part_ref.shape[2]
    for p in range(2):
        stage(p, bits)
        pre1 = sums[p, 0]
        sig1 = sigmoid(pre1)
        hid1 = (pre1 * sig1).astype(jnp.bfloat16)
        pre2 = jnp.dot(hid1, weight_ref[p, :, :hidden], preferred_element_type=jnp.float32)
        sig2 = sigmoid(pre2)
        hid2 = (pre2 * sig2).astype(jnp.bfloat16)
        logits = jnp.dot(hid2, weight_ref[p, :, hidden:], preferred_element_type=jnp.float32)
        loss, slope = loss_and_slope(logits, box_ref[p], count)
        back_z = slope.astype(jnp.bfloat16)
        across = (((1,), (1,)), ((), ()))
        back_h2 = lax.dot_general(back_z, weight_ref[p, :, hidden:], across, preferred_element_type=jnp.float32)
        back_p2 = (back_h2 * (sig2 * (1.0 + pre2 * (1.0 - sig2)))).astype(jnp.bfloat16)
        back_h1 = lax.dot_general(back_p2, weight_ref[p, :, :hidden], across, preferred_element_type=jnp.float32)
        own[p] = (back_h1 * (sig1 * (1.0 + pre1 * (1.0 - sig1)))).astype(jnp.bfloat16)

        @pl.when(level < images - 1)
        def _():
            hop(p, 0, True, own.at[p]).start()

        @pl.when(level > 0)
        def _():
            hop(p, 0, False, own.at[p]).start()

        advance(p, level, 0, own.at[p])
        pltpu.make_async_copy(own.at[p], rows(p, level, 0), own_sem.at[p]).start()
        place = lax.broadcasted_iota(jnp.int32, (mine, LANES), 1)
        losses = jnp.zeros((mine, LANES), jnp.float32)
        for k in range(3):
            near = loss.astype(jnp.bfloat16).astype(jnp.float32)
            losses = jnp.where(place == k, near, losses)
            loss = loss - near
        at = 0
        for value in (back_p2, back_z, losses.astype(jnp.bfloat16)):
            kept[p, me, :, at : at + value.shape[1]] = value
            at += value.shape[1]
        advance_kept(p, 0, 0)
        for owner in range(parts):
            split[p, 0, owner] = hid1[:, owner * span : (owner + 1) * span]
            split[p, 1, owner] = hid2[:, owner * span : (owner + 1) * span]
        for mask in range(1, parts):
            hand(p, mask).start()
    for p in range(2):
        pltpu.make_async_copy(own.at[p], rows(p, level, 0), own_sem.at[p]).wait()

    def each_side(d, do):
        @pl.when(level >= d)
        def _():
            do(level - d, True)

        @pl.when(level + d < images)
        def _():
            do(level + d, False)

    def enter(d):
        def do(image, up):
            for p in range(2):
                came(p, d, up)

                @pl.when((level < images - 1) if up else (level > 0))
                def _():
                    hop(p, d, up).start()

                advance(p, image, 0)

        each_side(d, do)

    def go_on(d, at):
        if d == 0:
            for p in range(2):
                advance(p, level, at)
                advance_kept(p, 0, at)
        else:

            def do(image, up):
                for p in range(2):
                    advance(p, image, at)

            each_side(d, do)

    for tick in range(1, images + bits - 1):
        for d in range(images):
            at = tick - d
            if at == 0:
                enter(d)
            elif 0 < at < bits:
                go_on(d, at)

    loss = jnp.zeros((1, 1), jnp.float32)
    for p in range(2):
        arrive_kept(p, 0, bits - 1)
        for mask in range(1, parts):
            handed(p, mask)
        for k in range(2):
            cols[p, k, me] = split[p, k, me]
        slopes = kept[p].reshape(parts * mine, kept.shape[3])
        down = (((0,), (0,)), ((), ()))
        for k, (start, stop) in enumerate(((0, hidden), (hidden, grad_ref.shape[2]))):
            left = cols[p, k].reshape(parts * mine, span)
            grad_ref[p, :, start:stop] = lax.dot_general(
                left, slopes[:, start:stop], down, preferred_element_type=jnp.float32
            )
        loss += jnp.sum(slopes[:, grad_ref.shape[2] :].astype(jnp.float32), keepdims=True)
    corner = grad_ref[0, 0:8, grad_ref.shape[2] - LANES :]
    place = [lax.broadcasted_iota(jnp.int32, corner.shape, k) for k in range(2)]
    corner = jnp.where((place[0] == 0) & (place[1] == LANES - 1), loss, corner)
    grad_ref[0, 0:8, grad_ref.shape[2] - LANES :] = corner

    for p in range(2):
        finish(p, level)
        sent_kept(p, 0)
        for mask in range(1, parts):
            hand(p, mask).wait_send()

        @pl.when(level < images - 1)
        def _():
            hop(p, 0, True).wait_send()

        @pl.when(level > 0)
        def _():
            hop(p, 0, False).wait_send()

    for d in range(1, images):

        def do(image, up):
            for p in range(2):
                finish(p, image)

                @pl.when((level < images - 1) if up else (level > 0))
                def _():
                    hop(p, d, up).wait_send()

        each_side(d, do)
    for p in range(2):
        for mask in range(1, parts):
            copies[p, mask].wait_send()
    for copy in counting:
        copy.wait_send()


def head_step(part, weight, box, count, images, parts):
    passes, boxes, hidden = part.shape
    mine = boxes // parts
    outs = weight.shape[2] - hidden
    span = hidden // parts
    low = jnp.bfloat16
    vmem = pl.BlockSpec(memory_space=pltpu.VMEM)
    dma = pltpu.SemaphoreType.DMA
    return pl.pallas_call(
        partial(head_kernel, images, parts, mine),
        out_shape=[
            jax.ShapeDtypeStruct((passes, images * boxes, hidden), low),
            jax.ShapeDtypeStruct((passes, span, hidden + outs), jnp.float32),
        ],
        in_specs=[vmem] * 4,
        out_specs=[pl.BlockSpec(memory_space=pl.ANY), vmem],
        scratch_shapes=[
            pltpu.VMEM((passes, parts, mine, hidden), jnp.float32),
            pltpu.VMEM((passes, parts, mine, hidden), jnp.float32),
            pltpu.VMEM((passes, mine, hidden), low),
            pltpu.VMEM((images, 8, LANES), jnp.float32),
            pltpu.VMEM((passes, 2, parts, mine, span), low),
            pltpu.VMEM((passes, 2, parts, mine, span), low),
            pltpu.VMEM((passes, parts, mine, hidden + outs + LANES), low),
            dma((passes, parts)),
            dma((passes, parts)),
            dma((passes, images, parts)),
            dma((passes, images, parts)),
            dma((passes, images)),
            dma((passes, images)),
            dma((passes, images)),
            dma((passes, images)),
            dma((passes,)),
            dma((images,)),
            dma((images,)),
            dma((passes, parts)),
            dma((passes, parts)),
            dma((passes, 1, parts)),
            dma((passes, 1, parts)),
        ],
        compiler_params=pltpu.CompilerParams(
            vmem_limit_bytes=48 * MIB, collective_id=0, has_side_effects=True
        ),
        cost_estimate=pl.CostEstimate(
            flops=8 * passes * mine * hidden * (hidden + outs),
            bytes_accessed=100 * MIB,
            transcendentals=4 * passes * mine * hidden,
        ),
        name="head_step",
    )(part, weight, box, count)


def small_kernel(grad_ref, count_ref, *refs):
    hidden = refs[0].shape[2]
    outs = refs[3].shape[0]
    new = adamw(*(r[...] for r in refs[:3]), grad_ref[:, :, :hidden])
    for ref, value in zip(refs[6:9], new):
        ref[...] = value
    for p in range(grad_ref.shape[0]):
        grad = grad_ref[p, :, hidden:].T[:outs]
        new = adamw(*(r[:, p, :] for r in refs[3:6]), grad)
        for ref, value in zip(refs[9:12], new):
            ref[:, p, :] = value
    total = grad_ref[0, 0:1, grad_ref.shape[2] - 1 :]
    lane = lax.broadcasted_iota(jnp.int32, (8, LANES), 1)
    refs[12][...] = jnp.where(lane == 0, total, count_ref[...])


def update_small(grad, count, two, head):
    arrays = tuple(two) + tuple(x.transpose(2, 0, 1) for x in head)
    shapes = [jax.ShapeDtypeStruct(x.shape, jnp.float32) for x in arrays]
    out = pl.pallas_call(
        small_kernel,
        out_shape=shapes + [jax.ShapeDtypeStruct((8, LANES), jnp.float32)],
        compiler_params=pltpu.CompilerParams(vmem_limit_bytes=30 * MIB),
        name="update_small",
    )(grad, jnp.full((8, LANES), count), *arrays)
    return (out[6][0, :2],), out[:3], tuple(x.transpose(1, 2, 0) for x in out[3:6])


def per_device(
    feat_p2, feat_p3, feat_p4, feat_p5, rois, levels, labels, sampled, targets,
    fc1_w, fc1_m, fc1_v, fc2_w, fc2_m, fc2_v, head_w, head_m, head_v,
):
    side = feat_p2.shape[-1]
    channels = feat_p2.shape[1]
    boxes = rois.shape[2]
    images = lax.axis_size("wide")
    mine = boxes // lax.axis_size("narrow")
    first = lax.axis_index("narrow") * mine
    level = lax.axis_index("wide").astype(jnp.int32)
    parts = lax.axis_size("narrow")
    hidden = fc2_w.shape[2]
    outs = head_w.shape[2]
    zero = jnp.zeros((), jnp.int32)
    rank = box_order(rois[:, 0], levels[:, 0], side)
    ordered = sort_boxes(rois[:, 0], levels[:, 0], rank)
    feat = feature_rows((feat_p2, feat_p3, feat_p4, feat_p5))
    height = feat.shape[0]
    flags = sampled[:, 0].astype(jnp.bfloat16).reshape(1, 2, boxes)
    both = jnp.concatenate([feat, jnp.concatenate([ordered, flags]).reshape(-1, LANES)])
    weight = jnp.concatenate([fc2_w, jnp.pad(head_w, ((0, 0), (0, 0), (0, -outs % LANES)))], axis=2)
    weight = lax.all_gather(weight.astype(jnp.bfloat16), "narrow", axis=1, tiled=True)
    counted = jnp.sum(sampled).astype(jnp.float32)
    table, spans = box_table(ordered[None], side)
    pooled, own = pool(feat[None], table, spans, zero, level, images, channels)
    w1 = fc1_w.astype(jnp.bfloat16)
    part = lax.dot_general(own, w1, (((1,), (1,)), ((0,), (0,))), preferred_element_type=jnp.float32)
    both, weight, part = lax.optimization_barrier((both, weight, part))
    feats = lax.all_gather(both, "wide", axis=0)
    hot = rank[:, None, :] == first + jnp.arange(mine, dtype=jnp.int32)[:, None]

    def pick(values):
        return jnp.sum(jnp.where(hot, values[:, 0].astype(jnp.float32)[:, None, :], 0), axis=-1)

    box = [pick(labels), pick(sampled)] + [pick(targets[..., k]) for k in range(4)]
    box = jnp.pad(jnp.stack(box, axis=-1), ((0, 0), (0, 0), (0, LANES - 6)))
    back, grad = head_step(part, weight, box, jnp.full((8, LANES), counted), images, parts)
    grad = lax.psum_scatter(grad, "wide", scatter_dimension=1, tiled=True)

    tails = feats[:, height:].reshape(images, 6, 2, boxes)
    count = jnp.sum(tails[:, 5].astype(jnp.float32))
    tables, all_spans = box_table(tails[:, :5], side)
    turn = [lax.rem(level + k, images) for k in range(1, images)]
    for k in range(images - 1):
        pooled = pool(feats, tables, all_spans, turn[k], turn[k], images, channels, pooled)[0]
        if k == max(images - 3, 0):
            grad, pooled = lax.optimization_barrier((grad, pooled))
            grad = lax.all_gather(grad, "wide", axis=1, tiled=True)
    new1 = update_first(pooled, back, fc1_w, fc1_m, fc1_v)
    grad, new1 = lax.optimization_barrier((grad, new1))
    losses, new2, newh = update_small(grad, count, (fc2_w, fc2_m, fc2_v), (head_w, head_m, head_v))
    return losses + tuple(new1) + tuple(new2) + tuple(newh)


def solution(mesh):
    maps = P("wide", "narrow", None, None)
    rows = P(None, "narrow", None)
    box = P(None, "wide", None)
    coords = P(None, "wide", None, None)
    return jax.shard_map(
        per_device,
        mesh=mesh,
        in_specs=(maps,) * 4 + (coords, box, box, box, coords) + (rows,) * 9,
        out_specs=(P(),) + (rows,) * 9,
        check_vma=False,
    )
```

```python
from functools import partial

import jax
import jax.numpy as jnp
from jax import lax
from jax.experimental import pallas as pl
from jax.experimental.pallas import tpu as pltpu
from jax.sharding import PartitionSpec as P

CLASSES = 81
STEP = 5
BETA_ONE = 0.5
BETA_TWO = 0.5
RATE = 0.02
DECAY = 0.01
EPSILON = 1e-08
BINS = 7
CHUNK = 8
STATIC = 5
WINDOW = 24
MORE = 4
SPANS = 17
LANES = 128
MIB = 2**20


def tent(where, cells):
    return 0.5 * sum(jnp.maximum(0.0, 1.0 - jnp.abs(w - cells)) for w in where)


def pool_kernel(channels, side, groups, copies, pick_ref, span_ref, feat_ref, table_ref, *refs):
    out_refs = refs[-7 - copies : -7]
    cols, rows, parts = refs[-7:-5], refs[-5:-3], refs[-3:-1]
    line_ref = refs[-1]
    image = pick_ref[0]
    half = LANES // 2
    offsets = (0.25, 0.75)
    cells = lax.broadcasted_iota(jnp.int32, (side, LANES), 0).astype(jnp.float32)
    bins = lax.broadcasted_iota(jnp.int32, (8, LANES), 0).astype(jnp.float32)

    def at(group):
        return (image * groups + group) * SPANS

    def param(group, k):
        return table_ref[group, k : k + 1, :]

    def weights(group, slot):
        top, x_start, x_step = param(group, 2), param(group, 4), param(group, 5)
        for j in range(BINS):
            where = [jnp.clip(x_start + (j + off) * x_step, 0.0, top) for off in offsets]
            weight = tent(where, cells)
            high = weight.astype(jnp.bfloat16)
            low = (weight - high.astype(jnp.float32)).astype(jnp.bfloat16)
            lanes = pl.ds(j * LANES, LANES)
            cols[slot][0:side, lanes] = high
            cols[slot][side : 2 * side, lanes] = high
            cols[slot][2 * side : 3 * side, lanes] = low
            cols[slot][3 * side : 4 * side, lanes] = low

    def fill(group, slot, row):
        y_start, y_step, top, base = (param(group, k) for k in range(4))
        where = [jnp.clip(y_start + (bins + off) * y_step, 0.0, top) for off in offsets]
        for h in range(CHUNK):
            rows[slot][row + h] = tent(where, (row + h).astype(jnp.float32) - base)
        place = pl.ds(pl.multiple_of(row * channels, channels), CHUNK * channels)
        left = feat_ref[place, :]
        left = jnp.concatenate([left, left], axis=1)
        parts[slot][place, :] = jnp.dot(left, cols[slot][...], preferred_element_type=jnp.float32)

    def rest(group, slot):
        first = span_ref[at(group)] + STATIC * CHUNK

        @pl.loop(0, span_ref[at(group) + 1])
        def _(t):
            fill(group, slot, first + t * CHUNK)

    def block(slot, i, low_row, count):
        accs = None
        for h in range(count):
            start = pl.multiple_of((low_row + h) * channels, channels)
            weight = jnp.broadcast_to(rows[slot][low_row + h, i : i + 1, :], (channels, LANES))
            new = [
                weight * parts[slot][pl.ds(start, channels), j * LANES : (j + 1) * LANES] for j in range(BINS)
            ]
            accs = new if accs is None else [x + y for x, y in zip(accs, new)]
        return accs

    def spot(i, j):
        return pl.ds(i * BINS + j, channels, stride=BINS * BINS)

    def work(group, slot, following):
        for i in range(BINS):
            accs = block(slot, i, span_ref[at(group) + 3 + i], WINDOW)
            for j in range(BINS):
                line_ref[slot, spot(i, j), :] = accs[j]
            if i < STATIC:
                fill(following, 1 - slot, span_ref[at(following)] + i * CHUNK)

        @pl.when(span_ref[at(group) + 2] > 0)
        def _():
            for i in range(BINS):
                low_row = span_ref[at(group) + 3 + i] + WINDOW

                @pl.loop(0, span_ref[at(group) + 3 + BINS + i])
                def _(t):
                    more = block(slot, i, low_row + t * MORE, MORE)
                    for j in range(BINS):
                        line_ref[slot, spot(i, j), :] = line_ref[slot, spot(i, j), :] + more[j]

    step = pl.program_id(0)

    @pl.when(step == 0)
    def _():
        weights(0, 0)
        for i in range(STATIC):
            fill(0, 0, span_ref[at(0)] + i * CHUNK)
        rest(0, 0)

    group = 2 * step
    weights(group + 1, 1)
    work(group, 0, group + 1)
    rest(group + 1, 1)
    following = jnp.minimum(group + 2, groups - 1)
    weights(following, 0)
    work(group + 1, 1, following)
    rest(following, 0)
    a, b = line_ref[0], line_ref[1]
    lanes = lax.broadcasted_iota(jnp.int32, a.shape, 1)
    new = [jnp.where(lanes < half, a, pltpu.roll(b, half, 1)), jnp.where(lanes < half, pltpu.roll(a, half, 1), b)]
    for out_ref in out_refs:
        for p in range(2):
            out_ref[p] = new[p].astype(jnp.bfloat16)


def pool(feat, table, spans, source, image, images, channels, buffer=None):
    depth = feat.shape[2]
    groups = table.shape[1]
    wide = channels * BINS * BINS
    side = depth // 2
    rows = sum(side >> k for k in range(4))
    boxes = groups * LANES // 2
    blocks = groups // 2
    pick = jnp.stack([source, image])
    out_shape = [jax.ShapeDtypeStruct((2, wide, images * boxes), jnp.bfloat16)]
    out_specs = [pl.BlockSpec((2, wide, LANES), lambda s, pick, spans: (0, 0, pick[1] * blocks + s))]
    in_specs = [
        pl.BlockSpec((None, rows * channels, depth), lambda s, pick, spans: (pick[0], 0, 0)),
        pl.BlockSpec((None, groups, 8, LANES), lambda s, pick, spans: (pick[0], 0, 0, 0)),
    ]
    operands = (pick, spans, feat, table)
    aliases = {}
    if buffer is None:
        out_shape.append(jax.ShapeDtypeStruct((2, wide, boxes), jnp.bfloat16))
        out_specs.append(pl.BlockSpec((2, wide, LANES), lambda s, pick, spans: (0, 0, s)))
    else:
        in_specs.append(pl.BlockSpec(memory_space=pl.ANY))
        operands += (buffer,)
        aliases = {4: 0}
    return pl.pallas_call(
        partial(pool_kernel, channels, side, groups, len(out_shape)),
        out_shape=out_shape,
        grid_spec=pltpu.PrefetchScalarGridSpec(
            num_scalar_prefetch=2,
            grid=(blocks,),
            in_specs=in_specs,
            out_specs=out_specs,
            scratch_shapes=[
                pltpu.VMEM((4 * side, BINS * LANES), jnp.bfloat16),
                pltpu.VMEM((4 * side, BINS * LANES), jnp.bfloat16),
                pltpu.VMEM((rows, 8, LANES), jnp.float32),
                pltpu.VMEM((rows, 8, LANES), jnp.float32),
                pltpu.VMEM((rows * channels, BINS * LANES), jnp.float32),
                pltpu.VMEM((rows * channels, BINS * LANES), jnp.float32),
                pltpu.VMEM((2, wide, LANES), jnp.float32),
            ],
        ),
        input_output_aliases=aliases,
        compiler_params=pltpu.CompilerParams(vmem_limit_bytes=60 * MIB),
        cost_estimate=pl.CostEstimate(
            flops=groups * 40 * channels * BINS * LANES * 8 * depth,
            bytes_accessed=80 * MIB,
            transcendentals=0,
        ),
        name="pool_rois",
    )(*operands)


def feature_rows(maps):
    side = maps[0].shape[-1]
    parts = [
        jnp.pad(m.transpose(0, 2, 1, 3), ((0, 0), (0, 0), (0, 0), (0, side - m.shape[-1])))
        for m in maps
    ]
    full = jnp.concatenate(parts, axis=1)
    high = lax.reduce_precision(full, 8, 7)
    low = (full - high).astype(jnp.bfloat16)
    full = jnp.concatenate([high.astype(jnp.bfloat16), low], axis=-1)
    return full.reshape(-1, 2 * side)


def box_order(boxes, levels, side):
    base = 2 * side - 2 * (side >> levels)
    key = ((boxes[..., 1] + boxes[..., 3]) >> levels) + base * 8
    key = key * key.shape[-1] + jnp.arange(key.shape[-1], dtype=jnp.int32)
    return jnp.sum((key[..., :, None] > key[..., None, :]).astype(jnp.int32), axis=-1)


def sort_boxes(boxes, levels, rank):
    count = boxes.shape[1]
    hot = (rank[:, None, :] == jnp.arange(count, dtype=jnp.int32)[:, None]).astype(jnp.bfloat16)
    both = jnp.concatenate([boxes, levels[..., None]], axis=-1).astype(jnp.bfloat16)
    return jnp.einsum("psr,prk->kps", hot, both, preferred_element_type=jnp.float32).astype(jnp.bfloat16)


def box_table(boxes, side):
    images, _, _, count = boxes.shape
    x0, y0, x1, y1, level = (boxes[:, k].astype(jnp.float32) for k in range(5))
    rows = sum(side >> k for k in range(4))
    scale = jnp.where(level < 0.5, 0.25, jnp.where(level < 1.5, 0.125, jnp.where(level < 2.5, 0.0625, 0.03125)))
    height = scale * (4 * side)
    base = 2.0 * side - 2.0 * height
    top = height - 1.0

    def axis(low, high):
        return low * scale - 0.5, ((high - low) * scale) / 7.0

    x_start, x_step = axis(x0, x1)
    y_start, y_step = axis(y0, y1)
    half = LANES // 2
    groups = count // half

    def split(v):
        return v.reshape(v.shape[:-1] + (groups, half))

    lows, highs = [], []
    for i in range(BINS):
        low = base + jnp.floor(jnp.clip(y_start + (i + 0.25) * y_step, 0.0, top))
        high = base + jnp.floor(jnp.clip(y_start + (i + 0.75) * y_step, 0.0, top)) + 1.0
        lows.append(jnp.min(split(low), axis=(1, 3)))
        highs.append(jnp.max(split(jnp.minimum(high, rows - 1.0)), axis=(1, 3)))
    low = jnp.stack(lows, axis=-1).astype(jnp.int32)
    high = jnp.stack(highs, axis=-1).astype(jnp.int32)
    least = jnp.min(low, axis=-1)
    chunks = jnp.maximum((jnp.max(high, axis=-1) - least + CHUNK) // CHUNK, STATIC)
    first = jnp.clip(rows - chunks * CHUNK, 0, least)
    extra = jnp.maximum(high - low + MORE - WINDOW, 0) // MORE
    low = jnp.minimum(low, (first + chunks * CHUNK)[..., None] - WINDOW - MORE * extra)
    heads = jnp.stack([first, chunks - STATIC, jnp.max(extra, axis=-1)], axis=-1)
    spans = jnp.concatenate([heads, low, extra], axis=-1).reshape(-1)
    zero = jnp.zeros_like(base)
    table = jnp.stack([split(v) for v in (y_start, y_step, top, base, x_start, x_step, zero, zero)])
    return table.transpose(1, 3, 0, 2, 4).reshape(images, groups, 8, LANES), spans


def adamw(weight, moment, second, grad):
    moment = BETA_ONE * moment + (1.0 - BETA_ONE) * grad
    second = BETA_TWO * second + (1.0 - BETA_TWO) * grad * grad
    fixed_m = moment / (1.0 - BETA_ONE**STEP)
    fixed_v = second / (1.0 - BETA_TWO**STEP)
    weight = weight - RATE * (fixed_m / (jnp.sqrt(fixed_v) + EPSILON) + DECAY * weight)
    return (weight, moment, second)


def update_kernel(pooled_ref, back_ref, w_ref, m_ref, v_ref, *outs):
    grad = jnp.dot(pooled_ref[...], back_ref[...], preferred_element_type=jnp.float32)
    new = adamw(w_ref[...], m_ref[...], v_ref[...], grad)
    for ref, value in zip(outs, new):
        ref[...] = value


def update_first(pooled, back, weight, moment, second):
    passes, wide, hidden = weight.shape
    boxes = pooled.shape[2]
    block = wide // BINS
    big = pl.BlockSpec((None, block, hidden), lambda p, b: (p, b, 0))
    return pl.pallas_call(
        update_kernel,
        out_shape=[jax.ShapeDtypeStruct(weight.shape, jnp.float32)] * 3,
        grid=(passes, BINS),
        in_specs=[
            pl.BlockSpec((None, block, boxes), lambda p, b: (p, b, 0)),
            pl.BlockSpec((None, boxes, hidden), lambda p, b: (p, 0, 0)),
            big,
            big,
            big,
        ],
        out_specs=[big] * 3,
        compiler_params=pltpu.CompilerParams(vmem_limit_bytes=60 * MIB),
        cost_estimate=pl.CostEstimate(
            flops=2 * passes * wide * hidden * boxes,
            bytes_accessed=passes * wide * hidden * 24 + passes * boxes * (wide + hidden) * 2,
            transcendentals=passes * wide * hidden,
        ),
        name="update_first",
    )(pooled, back, weight, moment, second)


def loss_and_slope(logits, box, count):
    place = lax.broadcasted_iota(jnp.int32, logits.shape, 1)
    is_class = place < CLASSES
    label = box[:, 0:1].astype(jnp.int32)
    weight = box[:, 1:2]
    top = jnp.max(jnp.where(is_class, logits, -jnp.inf), axis=1, keepdims=True)
    grown = jnp.where(is_class, jnp.exp(jnp.where(is_class, logits - top, 0.0)), 0.0)
    norm = jnp.sum(grown, axis=1, keepdims=True)
    hot = place == label
    picked = jnp.sum(jnp.where(hot, logits, 0.0), axis=1, keepdims=True)
    fore = jnp.where(label > 0, weight, 0.0)
    rows = weight * (top + jnp.log(norm) - picked)
    slope = weight * (grown / norm - jnp.where(hot, 1.0, 0.0))
    offset = place - (CLASSES + 4 * (label - 1))
    for k in range(4):
        mask = (offset == k) & (place >= CLASSES)
        chosen = jnp.sum(jnp.where(mask, logits, 0.0), axis=1, keepdims=True)
        differ = fore * (chosen - box[:, 2 + k : 3 + k])
        near = jnp.abs(differ)
        rows += jnp.where(near < 1.0, 0.5 * differ * differ, near - 0.5) * fore
        slope = jnp.where(mask, fore * jnp.clip(differ, -1.0, 1.0), slope)
    return rows, slope / count


def sigmoid(value):
    return 1.0 / (1.0 + jnp.exp(-value))


def head_kernel(
    images, parts, mine,
    part_ref, weight_ref, box_ref, count_ref,
    back_ref, grad_ref,
    sums, landed, own, counts, split, cols, kept,
    rs_send, rs_recv, ag_send, ag_recv, up_send, up_recv, down_send, down_recv, own_sem,
    count_send, count_recv, col_send, col_recv, kept_send, kept_recv,
):
    me = lax.axis_index("narrow")
    level = lax.axis_index("wide")
    bits = parts.bit_length() - 1
    turn = [(1 - 2 * ((me // 2**k) % 2)) * 2**k for k in range(bits)]

    def peer(mask):
        return me + sum((turn[k] for k in range(bits) if mask >> k & 1), 0)

    links = list(range(1, bits))
    orders = [links, links[::-1]]

    barrier = pltpu.get_barrier_semaphore()
    for mask in range(1, parts):
        pl.semaphore_signal(barrier, inc=1, device_id={"narrow": peer(mask)})
    for k in range(1, images):
        pl.semaphore_signal(barrier, inc=1, device_id={"wide": lax.rem(level + k, images)})
    pl.semaphore_wait(barrier, parts + images - 2)

    counting = []
    for k in range(1, images):
        counting.append(
            pltpu.make_async_remote_copy(
                src_ref=count_ref,
                dst_ref=counts.at[k],
                send_sem=count_send.at[k],
                recv_sem=count_recv.at[k],
                device_id={"wide": lax.rem(level + k, images)},
            )
        )

    part = mine // 2

    def scatter(q, mask, bit, source):
        return pltpu.make_async_remote_copy(
            src_ref=source,
            dst_ref=landed.at[q, mask],
            send_sem=rs_send.at[q, mask],
            recv_sem=rs_recv.at[q, mask],
            device_id={"narrow": peer(1 << bit)},
        )

    def part_at(q, mask):
        start = peer(mask) * mine + q % 2 * part
        return part_ref.at[q // 2, pl.ds(pl.multiple_of(start, part), part), :]

    copies = {}
    for q in range(4):
        for mask in range(1, parts, 2):
            copies[q, mask] = scatter(q, mask, 0, part_at(q, mask))
            copies[q, mask].start()

    def stage(p, at):
        for q in (2 * p, 2 * p + 1):
            order = [0] + orders[q % 2]
            bit = order[at - 1]
            seen = sum(1 << b for b in order[:at])
            masks = [m for m in range(parts) if not m & seen]
            if at < bits:
                masks.sort(key=lambda m: not m >> order[at] & 1)
            for mask in masks:
                copies[q, mask | 1 << bit].wait_recv()
                have = part_at(q, mask)[...] if at == 1 else sums[q, mask]
                sums[q, mask] = have + landed[q, mask | 1 << bit]
                if at < bits and mask >> order[at] & 1:
                    copies[q, mask] = scatter(q, mask, order[at], sums.at[q, mask])
                    copies[q, mask].start()

    for copy in counting:
        copy.start()
    for at in range(1, bits):
        stage(0, at)
    stage(1, 1)

    def rows(p, image, mask):
        place = (image * parts + peer(mask)) * mine
        return back_ref.at[p, pl.ds(pl.multiple_of(place, mine), mine), :]

    def hop(p, d, up, source=None):
        image = level - d if up else level + d
        spot = rows(p, image, 0)
        return pltpu.make_async_remote_copy(
            src_ref=spot if source is None else source,
            dst_ref=spot,
            send_sem=(up_send if up else down_send).at[p, d],
            recv_sem=(up_recv if up else down_recv).at[p, d],
            device_id={"wide": level + 1 if up else level - 1},
        )

    def came(p, d, up):
        image = level - d if up else level + d
        spot = rows(p, image, 0)
        pltpu.make_async_remote_copy(
            src_ref=spot, dst_ref=spot, send_sem=(up_send if up else down_send).at[p, d],
            recv_sem=(up_recv if up else down_recv).at[p, d - 1],
            device_id={"wide": level - 1 if up else level + 1},
        ).wait_recv()

    steps = [orders[p] + [0] for p in range(2)]

    def masks_before(p, at):
        seen = sum(1 << b for b in steps[p][:at])
        return [m for m in range(parts) if not m & ~seen]

    def doubling(spot, send, recv):
        def spread(p, key, mask, bit, source=None):
            there = mask | 1 << bit
            return pltpu.make_async_remote_copy(
                src_ref=spot(p, key, mask) if source is None else source,
                dst_ref=spot(p, key, mask),
                send_sem=send.at[p, key, there],
                recv_sem=recv.at[p, key, there],
                device_id={"narrow": peer(1 << bit)},
            )

        def arrive(p, key, at):
            for m in masks_before(p, at):
                there = m | 1 << steps[p][at]
                pltpu.make_async_remote_copy(
                    src_ref=spot(p, key, there),
                    dst_ref=spot(p, key, there),
                    send_sem=send.at[p, key, there],
                    recv_sem=recv.at[p, key, there],
                    device_id={"narrow": peer(1)},
                ).wait_recv()

        def advance(p, key, at, source=None):
            if at:
                arrive(p, key, at - 1)
            for m in masks_before(p, at):
                spread(p, key, m, steps[p][at], source if m == 0 else None).start()

        def sent(p, key):
            for at in range(bits):
                for m in masks_before(p, at):
                    spread(p, key, m, steps[p][at]).wait_send()

        return advance, arrive, sent

    advance, arrive, sent = doubling(rows, ag_send, ag_recv)
    advance_kept, arrive_kept, sent_kept = doubling(
        lambda p, key, mask: kept.at[p, peer(mask)], kept_send, kept_recv
    )

    def finish(p, image):
        arrive(p, image, bits - 1)
        sent(p, image)

    span = grad_ref.shape[1]

    def hand(p, mask):
        return pltpu.make_async_remote_copy(
            src_ref=split.at[p, :, peer(mask)],
            dst_ref=cols.at[p, :, me],
            send_sem=col_send.at[p, mask],
            recv_sem=col_recv.at[p, mask],
            device_id={"narrow": peer(mask)},
        )

    def handed(p, mask):
        spot = cols.at[p, :, peer(mask)]
        pltpu.make_async_remote_copy(
            src_ref=spot, dst_ref=spot, send_sem=col_send.at[p, mask], recv_sem=col_recv.at[p, mask],
            device_id={"narrow": peer(mask)},
        ).wait_recv()

    for copy in counting:
        copy.wait_recv()
    count = count_ref[0:1, 0:1] + sum(counts[k, 0:1, 0:1] for k in range(1, images))
    hidden = part_ref.shape[2]
    for p in range(2):
        for at in range(2 if p else bits, bits + 1):
            stage(p, at)
        pre1 = jnp.concatenate([sums[2 * p, 0], sums[2 * p + 1, 0]], axis=0)
        sig1 = sigmoid(pre1)
        hid1 = (pre1 * sig1).astype(jnp.bfloat16)
        pre2 = jnp.dot(hid1, weight_ref[p, :, :hidden], preferred_element_type=jnp.float32)
        sig2 = sigmoid(pre2)
        hid2 = (pre2 * sig2).astype(jnp.bfloat16)
        logits = jnp.dot(hid2, weight_ref[p, :, hidden:], preferred_element_type=jnp.float32)
        loss, slope = loss_and_slope(logits, box_ref[p], count)
        back_z = slope.astype(jnp.bfloat16)
        across = (((1,), (1,)), ((), ()))
        back_h2 = lax.dot_general(back_z, weight_ref[p, :, hidden:], across, preferred_element_type=jnp.float32)
        back_p2 = (back_h2 * (sig2 * (1.0 + pre2 * (1.0 - sig2)))).astype(jnp.bfloat16)
        back_h1 = lax.dot_general(back_p2, weight_ref[p, :, :hidden], across, preferred_element_type=jnp.float32)
        own[p] = (back_h1 * (sig1 * (1.0 + pre1 * (1.0 - sig1)))).astype(jnp.bfloat16)

        @pl.when(level < images - 1)
        def _():
            hop(p, 0, True, own.at[p]).start()

        @pl.when(level > 0)
        def _():
            hop(p, 0, False, own.at[p]).start()

        advance(p, level, 0, own.at[p])
        pltpu.make_async_copy(own.at[p], rows(p, level, 0), own_sem.at[p]).start()
        place = lax.broadcasted_iota(jnp.int32, (mine, LANES), 1)
        losses = jnp.zeros((mine, LANES), jnp.float32)
        for k in range(3):
            near = loss.astype(jnp.bfloat16).astype(jnp.float32)
            losses = jnp.where(place == k, near, losses)
            loss = loss - near
        at = 0
        for value in (back_p2, back_z, losses.astype(jnp.bfloat16)):
            kept[p, me, :, at : at + value.shape[1]] = value
            at += value.shape[1]
        advance_kept(p, 0, 0)
        for owner in range(parts):
            split[p, 0, owner] = hid1[:, owner * span : (owner + 1) * span]
            split[p, 1, owner] = hid2[:, owner * span : (owner + 1) * span]
        for mask in range(1, parts):
            hand(p, mask).start()
    for p in range(2):
        pltpu.make_async_copy(own.at[p], rows(p, level, 0), own_sem.at[p]).wait()

    def each_side(d, do):
        @pl.when(level >= d)
        def _():
            do(level - d, True)

        @pl.when(level + d < images)
        def _():
            do(level + d, False)

    def enter(d):
        def do(image, up):
            for p in range(2):
                came(p, d, up)

                @pl.when((level < images - 1) if up else (level > 0))
                def _():
                    hop(p, d, up).start()

                advance(p, image, 0)

        each_side(d, do)

    def go_on(d, at):
        if d == 0:
            for p in range(2):
                advance(p, level, at)
                advance_kept(p, 0, at)
        else:

            def do(image, up):
                for p in range(2):
                    advance(p, image, at)

            each_side(d, do)

    for tick in range(1, images + bits - 1):
        for d in range(images):
            at = tick - d
            if at == 0:
                enter(d)
            elif 0 < at < bits:
                go_on(d, at)

    loss = jnp.zeros((1, 1), jnp.float32)
    for p in range(2):
        arrive_kept(p, 0, bits - 1)
        for mask in range(1, parts):
            handed(p, mask)
        for k in range(2):
            cols[p, k, me] = split[p, k, me]
        slopes = kept[p].reshape(parts * mine, kept.shape[3])
        down = (((0,), (0,)), ((), ()))
        for k, (start, stop) in enumerate(((0, hidden), (hidden, grad_ref.shape[2]))):
            left = cols[p, k].reshape(parts * mine, span)
            grad_ref[p, :, start:stop] = lax.dot_general(
                left, slopes[:, start:stop], down, preferred_element_type=jnp.float32
            )
        loss += jnp.sum(slopes[:, grad_ref.shape[2] :].astype(jnp.float32), keepdims=True)
    corner = grad_ref[0, 0:8, grad_ref.shape[2] - LANES :]
    place = [lax.broadcasted_iota(jnp.int32, corner.shape, k) for k in range(2)]
    corner = jnp.where((place[0] == 0) & (place[1] == LANES - 1), loss, corner)
    grad_ref[0, 0:8, grad_ref.shape[2] - LANES :] = corner

    for p in range(2):
        finish(p, level)
        sent_kept(p, 0)
        for mask in range(1, parts):
            hand(p, mask).wait_send()

        @pl.when(level < images - 1)
        def _():
            hop(p, 0, True).wait_send()

        @pl.when(level > 0)
        def _():
            hop(p, 0, False).wait_send()

    for d in range(1, images):

        def do(image, up):
            for p in range(2):
                finish(p, image)

                @pl.when((level < images - 1) if up else (level > 0))
                def _():
                    hop(p, d, up).wait_send()

        each_side(d, do)
    for q in range(4):
        for mask in range(1, parts):
            copies[q, mask].wait_send()
    for copy in counting:
        copy.wait_send()


def head_step(part, weight, box, count, images, parts):
    passes, boxes, hidden = part.shape
    mine = boxes // parts
    outs = weight.shape[2] - hidden
    span = hidden // parts
    low = jnp.bfloat16
    vmem = pl.BlockSpec(memory_space=pltpu.VMEM)
    dma = pltpu.SemaphoreType.DMA
    return pl.pallas_call(
        partial(head_kernel, images, parts, mine),
        out_shape=[
            jax.ShapeDtypeStruct((passes, images * boxes, hidden), low),
            jax.ShapeDtypeStruct((passes, span, hidden + outs), jnp.float32),
        ],
        in_specs=[vmem] * 4,
        out_specs=[pl.BlockSpec(memory_space=pl.ANY), vmem],
        scratch_shapes=[
            pltpu.VMEM((2 * passes, parts, mine // 2, hidden), jnp.float32),
            pltpu.VMEM((2 * passes, parts, mine // 2, hidden), jnp.float32),
            pltpu.VMEM((passes, mine, hidden), low),
            pltpu.VMEM((images, 8, LANES), jnp.float32),
            pltpu.VMEM((passes, 2, parts, mine, span), low),
            pltpu.VMEM((passes, 2, parts, mine, span), low),
            pltpu.VMEM((passes, parts, mine, hidden + outs + LANES), low),
            dma((2 * passes, parts)),
            dma((2 * passes, parts)),
            dma((passes, images, parts)),
            dma((passes, images, parts)),
            dma((passes, images)),
            dma((passes, images)),
            dma((passes, images)),
            dma((passes, images)),
            dma((passes,)),
            dma((images,)),
            dma((images,)),
            dma((passes, parts)),
            dma((passes, parts)),
            dma((passes, 1, parts)),
            dma((passes, 1, parts)),
        ],
        compiler_params=pltpu.CompilerParams(
            vmem_limit_bytes=48 * MIB, collective_id=0, has_side_effects=True
        ),
        cost_estimate=pl.CostEstimate(
            flops=8 * passes * mine * hidden * (hidden + outs),
            bytes_accessed=100 * MIB,
            transcendentals=4 * passes * mine * hidden,
        ),
        name="head_step",
    )(part, weight, box, count)


def small_kernel(grad_ref, count_ref, *refs):
    hidden = refs[0].shape[2]
    outs = refs[3].shape[0]
    new = adamw(*(r[...] for r in refs[:3]), grad_ref[:, :, :hidden])
    for ref, value in zip(refs[6:9], new):
        ref[...] = value
    for p in range(grad_ref.shape[0]):
        grad = grad_ref[p, :, hidden:].T[:outs]
        new = adamw(*(r[:, p, :] for r in refs[3:6]), grad)
        for ref, value in zip(refs[9:12], new):
            ref[:, p, :] = value
    total = grad_ref[0, 0:1, grad_ref.shape[2] - 1 :]
    lane = lax.broadcasted_iota(jnp.int32, (8, LANES), 1)
    refs[12][...] = jnp.where(lane == 0, total, count_ref[...])


def update_small(grad, count, two, head):
    arrays = tuple(two) + tuple(x.transpose(2, 0, 1) for x in head)
    shapes = [jax.ShapeDtypeStruct(x.shape, jnp.float32) for x in arrays]
    out = pl.pallas_call(
        small_kernel,
        out_shape=shapes + [jax.ShapeDtypeStruct((8, LANES), jnp.float32)],
        compiler_params=pltpu.CompilerParams(vmem_limit_bytes=30 * MIB),
        name="update_small",
    )(grad, jnp.full((8, LANES), count), *arrays)
    return (out[6][0, :2],), out[:3], tuple(x.transpose(1, 2, 0) for x in out[3:6])


def per_device(
    feat_p2, feat_p3, feat_p4, feat_p5, rois, levels, labels, sampled, targets,
    fc1_w, fc1_m, fc1_v, fc2_w, fc2_m, fc2_v, head_w, head_m, head_v,
):
    side = feat_p2.shape[-1]
    channels = feat_p2.shape[1]
    boxes = rois.shape[2]
    images = lax.axis_size("wide")
    mine = boxes // lax.axis_size("narrow")
    first = lax.axis_index("narrow") * mine
    level = lax.axis_index("wide").astype(jnp.int32)
    parts = lax.axis_size("narrow")
    hidden = fc2_w.shape[2]
    outs = head_w.shape[2]
    zero = jnp.zeros((), jnp.int32)
    rank = box_order(rois[:, 0], levels[:, 0], side)
    ordered = sort_boxes(rois[:, 0], levels[:, 0], rank)
    feat = feature_rows((feat_p2, feat_p3, feat_p4, feat_p5))
    height = feat.shape[0]
    flags = sampled[:, 0].astype(jnp.bfloat16).reshape(1, 2, boxes)
    both = jnp.concatenate([feat, jnp.concatenate([ordered, flags]).reshape(-1, LANES)])
    weight = jnp.concatenate([fc2_w, jnp.pad(head_w, ((0, 0), (0, 0), (0, -outs % LANES)))], axis=2)
    weight = lax.all_gather(weight.astype(jnp.bfloat16), "narrow", axis=1, tiled=True)
    counted = jnp.sum(sampled).astype(jnp.float32)
    table, spans = box_table(ordered[None], side)
    pooled, own = pool(feat[None], table, spans, zero, level, images, channels)
    w1 = fc1_w.astype(jnp.bfloat16)
    part = lax.dot_general(own, w1, (((1,), (1,)), ((0,), (0,))), preferred_element_type=jnp.float32)
    both, weight, part = lax.optimization_barrier((both, weight, part))
    feats = lax.all_gather(both, "wide", axis=0)
    hot = rank[:, None, :] == first + jnp.arange(mine, dtype=jnp.int32)[:, None]

    def pick(values):
        return jnp.sum(jnp.where(hot, values[:, 0].astype(jnp.float32)[:, None, :], 0), axis=-1)

    box = [pick(labels), pick(sampled)] + [pick(targets[..., k]) for k in range(4)]
    box = jnp.pad(jnp.stack(box, axis=-1), ((0, 0), (0, 0), (0, LANES - 6)))
    back, grad = head_step(part, weight, box, jnp.full((8, LANES), counted), images, parts)
    grad = lax.psum_scatter(grad, "wide", scatter_dimension=1, tiled=True)

    tails = feats[:, height:].reshape(images, 6, 2, boxes)
    count = jnp.sum(tails[:, 5].astype(jnp.float32))
    tables, all_spans = box_table(tails[:, :5], side)
    turn = [lax.rem(level + k, images) for k in range(1, images)]
    for k in range(images - 1):
        pooled = pool(feats, tables, all_spans, turn[k], turn[k], images, channels, pooled)[0]
        if k == max(images - 3, 0):
            grad, pooled = lax.optimization_barrier((grad, pooled))
            grad = lax.all_gather(grad, "wide", axis=1, tiled=True)
    new1 = update_first(pooled, back, fc1_w, fc1_m, fc1_v)
    grad, new1 = lax.optimization_barrier((grad, new1))
    losses, new2, newh = update_small(grad, count, (fc2_w, fc2_m, fc2_v), (head_w, head_m, head_v))
    return losses + tuple(new1) + tuple(new2) + tuple(newh)


def solution(mesh):
    maps = P("wide", "narrow", None, None)
    rows = P(None, "narrow", None)
    box = P(None, "wide", None)
    coords = P(None, "wide", None, None)
    return jax.shard_map(
        per_device,
        mesh=mesh,
        in_specs=(maps,) * 4 + (coords, box, box, box, coords) + (rows,) * 9,
        out_specs=(P(),) + (rows,) * 9,
        check_vma=False,
    )
```

```python
from functools import partial

import jax
import jax.numpy as jnp
from jax import lax
from jax.experimental import pallas as pl
from jax.experimental.pallas import tpu as pltpu
from jax.sharding import PartitionSpec as P

CLASSES = 81
STEP = 5
BETA_ONE = 0.5
BETA_TWO = 0.5
RATE = 0.02
DECAY = 0.01
EPSILON = 1e-08
BINS = 7
CHUNK = 8
STATIC = 4
WINDOW = 20
MORE = 4
SPANS = 17
LANES = 128
MIB = 2**20


def tent(where, cells):
    return 0.5 * sum(jnp.maximum(0.0, 1.0 - jnp.abs(w - cells)) for w in where)


def pool_kernel(channels, side, groups, copies, pick_ref, span_ref, feat_ref, table_ref, *refs):
    out_refs = refs[-7 - copies : -7]
    cols, rows, parts = refs[-7:-5], refs[-5:-3], refs[-3:-1]
    line_ref = refs[-1]
    image = pick_ref[0]
    half = LANES // 2
    offsets = (0.25, 0.75)
    cells = lax.broadcasted_iota(jnp.int32, (side, LANES), 0).astype(jnp.float32)
    bins = lax.broadcasted_iota(jnp.int32, (8, LANES), 0).astype(jnp.float32)

    def at(group):
        return (image * groups + group) * SPANS

    def param(group, k):
        return table_ref[group, k : k + 1, :]

    def weights(group, slot):
        top, x_start, x_step = param(group, 2), param(group, 4), param(group, 5)
        for j in range(BINS):
            where = [jnp.clip(x_start + (j + off) * x_step, 0.0, top) for off in offsets]
            weight = tent(where, cells)
            high = weight.astype(jnp.bfloat16)
            low = (weight - high.astype(jnp.float32)).astype(jnp.bfloat16)
            lanes = pl.ds(j * LANES, LANES)
            cols[slot][0:side, lanes] = high
            cols[slot][side : 2 * side, lanes] = high
            cols[slot][2 * side : 3 * side, lanes] = low
            cols[slot][3 * side : 4 * side, lanes] = low

    def fill(group, slot, row):
        y_start, y_step, top, base = (param(group, k) for k in range(4))
        where = [jnp.clip(y_start + (bins + off) * y_step, 0.0, top) for off in offsets]
        for h in range(CHUNK):
            rows[slot][row + h] = tent(where, (row + h).astype(jnp.float32) - base)
        place = pl.ds(pl.multiple_of(row * channels, channels), CHUNK * channels)
        left = feat_ref[place, :]
        left = jnp.concatenate([left, left], axis=1)
        parts[slot][place, :] = jnp.dot(left, cols[slot][...], preferred_element_type=jnp.float32)

    def rest(group, slot):
        first = span_ref[at(group)] + STATIC * CHUNK

        @pl.loop(0, span_ref[at(group) + 1])
        def _(t):
            fill(group, slot, first + t * CHUNK)

    def block(slot, i, low_row, count):
        accs = None
        for h in range(count):
            start = pl.multiple_of((low_row + h) * channels, channels)
            weight = jnp.broadcast_to(rows[slot][low_row + h, i : i + 1, :], (channels, LANES))
            new = [
                weight * parts[slot][pl.ds(start, channels), j * LANES : (j + 1) * LANES] for j in range(BINS)
            ]
            accs = new if accs is None else [x + y for x, y in zip(accs, new)]
        return accs

    def spot(i, j):
        return pl.ds(i * BINS + j, channels, stride=BINS * BINS)

    def work(group, slot, following, beside):
        for i in range(BINS):
            accs = block(slot, i, span_ref[at(group) + 3 + i], WINDOW)
            for j in range(BINS):
                line_ref[slot, spot(i, j), :] = accs[j]
            if beside and i < STATIC:
                fill(following, 1 - slot, span_ref[at(following)] + i * CHUNK)

        @pl.when(span_ref[at(group) + 2] > 0)
        def _():
            for i in range(BINS):
                low_row = span_ref[at(group) + 3 + i] + WINDOW

                @pl.loop(0, span_ref[at(group) + 3 + BINS + i])
                def _(t):
                    more = block(slot, i, low_row + t * MORE, MORE)
                    for j in range(BINS):
                        line_ref[slot, spot(i, j), :] = line_ref[slot, spot(i, j), :] + more[j]

    step = pl.program_id(0)

    @pl.when(step == 0)
    def _():
        weights(0, 0)
        for i in range(STATIC):
            fill(0, 0, span_ref[at(0)] + i * CHUNK)
        rest(0, 0)

    group = 2 * step
    weights(group + 1, 1)
    work(group, 0, group + 1, True)
    rest(group + 1, 1)

    @pl.when(group + 2 < groups)
    def _():
        weights(group + 2, 0)
        work(group + 1, 1, group + 2, True)
        rest(group + 2, 0)

    @pl.when(group + 2 >= groups)
    def _():
        work(group + 1, 1, group + 1, False)

    a, b = line_ref[0], line_ref[1]
    lanes = lax.broadcasted_iota(jnp.int32, a.shape, 1)
    new = [jnp.where(lanes < half, a, pltpu.roll(b, half, 1)), jnp.where(lanes < half, pltpu.roll(a, half, 1), b)]
    for out_ref in out_refs:
        for p in range(2):
            out_ref[p] = new[p].astype(jnp.bfloat16)


def pool(feat, table, spans, source, image, images, channels, buffer=None):
    depth = feat.shape[2]
    groups = table.shape[1]
    wide = channels * BINS * BINS
    side = depth // 2
    rows = sum(side >> k for k in range(4))
    boxes = groups * LANES // 2
    blocks = groups // 2
    pick = jnp.stack([source, image])
    out_shape = [jax.ShapeDtypeStruct((2, wide, images * boxes), jnp.bfloat16)]
    out_specs = [pl.BlockSpec((2, wide, LANES), lambda s, pick, spans: (0, 0, pick[1] * blocks + s))]
    in_specs = [
        pl.BlockSpec((None, rows * channels, depth), lambda s, pick, spans: (pick[0], 0, 0)),
        pl.BlockSpec((None, groups, 8, LANES), lambda s, pick, spans: (pick[0], 0, 0, 0)),
    ]
    operands = (pick, spans, feat, table)
    aliases = {}
    if buffer is None:
        out_shape.append(jax.ShapeDtypeStruct((2, wide, boxes), jnp.bfloat16))
        out_specs.append(pl.BlockSpec((2, wide, LANES), lambda s, pick, spans: (0, 0, s)))
    else:
        in_specs.append(pl.BlockSpec(memory_space=pl.ANY))
        operands += (buffer,)
        aliases = {4: 0}
    return pl.pallas_call(
        partial(pool_kernel, channels, side, groups, len(out_shape)),
        out_shape=out_shape,
        grid_spec=pltpu.PrefetchScalarGridSpec(
            num_scalar_prefetch=2,
            grid=(blocks,),
            in_specs=in_specs,
            out_specs=out_specs,
            scratch_shapes=[
                pltpu.VMEM((4 * side, BINS * LANES), jnp.bfloat16),
                pltpu.VMEM((4 * side, BINS * LANES), jnp.bfloat16),
                pltpu.VMEM((rows, 8, LANES), jnp.float32),
                pltpu.VMEM((rows, 8, LANES), jnp.float32),
                pltpu.VMEM((rows * channels, BINS * LANES), jnp.float32),
                pltpu.VMEM((rows * channels, BINS * LANES), jnp.float32),
                pltpu.VMEM((2, wide, LANES), jnp.float32),
            ],
        ),
        input_output_aliases=aliases,
        compiler_params=pltpu.CompilerParams(vmem_limit_bytes=60 * MIB),
        cost_estimate=pl.CostEstimate(
            flops=groups * 40 * channels * BINS * LANES * 8 * depth,
            bytes_accessed=80 * MIB,
            transcendentals=0,
        ),
        name="pool_rois",
    )(*operands)


def feature_rows(maps):
    side = maps[0].shape[-1]
    parts = [
        jnp.pad(m.transpose(0, 2, 1, 3), ((0, 0), (0, 0), (0, 0), (0, side - m.shape[-1])))
        for m in maps
    ]
    full = jnp.concatenate(parts, axis=1)
    high = lax.reduce_precision(full, 8, 7)
    low = (full - high).astype(jnp.bfloat16)
    full = jnp.concatenate([high.astype(jnp.bfloat16), low], axis=-1)
    return full.reshape(-1, 2 * side)


def box_order(boxes, levels, side):
    base = 2 * side - 2 * (side >> levels)
    key = ((boxes[..., 1] + boxes[..., 3]) >> levels) + base * 8
    key = key * key.shape[-1] + jnp.arange(key.shape[-1], dtype=jnp.int32)
    return jnp.sum((key[..., :, None] > key[..., None, :]).astype(jnp.int32), axis=-1)


def sort_boxes(boxes, levels, rank):
    count = boxes.shape[1]
    hot = (rank[:, None, :] == jnp.arange(count, dtype=jnp.int32)[:, None]).astype(jnp.bfloat16)
    both = jnp.concatenate([boxes, levels[..., None]], axis=-1).astype(jnp.bfloat16)
    return jnp.einsum("psr,prk->kps", hot, both, preferred_element_type=jnp.float32).astype(jnp.bfloat16)


def box_table(boxes, side):
    images, _, _, count = boxes.shape
    x0, y0, x1, y1, level = (boxes[:, k].astype(jnp.float32) for k in range(5))
    rows = sum(side >> k for k in range(4))
    scale = jnp.where(level < 0.5, 0.25, jnp.where(level < 1.5, 0.125, jnp.where(level < 2.5, 0.0625, 0.03125)))
    height = scale * (4 * side)
    base = 2.0 * side - 2.0 * height
    top = height - 1.0

    def axis(low, high):
        return low * scale - 0.5, ((high - low) * scale) / 7.0

    x_start, x_step = axis(x0, x1)
    y_start, y_step = axis(y0, y1)
    half = LANES // 2
    groups = count // half

    def split(v):
        return v.reshape(v.shape[:-1] + (groups, half))

    lows, highs = [], []
    for i in range(BINS):
        low = base + jnp.floor(jnp.clip(y_start + (i + 0.25) * y_step, 0.0, top))
        high = base + jnp.floor(jnp.clip(y_start + (i + 0.75) * y_step, 0.0, top)) + 1.0
        lows.append(jnp.min(split(low), axis=(1, 3)))
        highs.append(jnp.max(split(jnp.minimum(high, rows - 1.0)), axis=(1, 3)))
    low = jnp.stack(lows, axis=-1).astype(jnp.int32)
    high = jnp.stack(highs, axis=-1).astype(jnp.int32)
    least = jnp.min(low, axis=-1)
    chunks = jnp.maximum((jnp.max(high, axis=-1) - least + CHUNK) // CHUNK, STATIC)
    first = jnp.clip(rows - chunks * CHUNK, 0, least)
    extra = jnp.maximum(high - low + MORE - WINDOW, 0) // MORE
    low = jnp.minimum(low, (first + chunks * CHUNK)[..., None] - WINDOW - MORE * extra)
    heads = jnp.stack([first, chunks - STATIC, jnp.max(extra, axis=-1)], axis=-1)
    spans = jnp.concatenate([heads, low, extra], axis=-1).reshape(-1)
    zero = jnp.zeros_like(base)
    table = jnp.stack([split(v) for v in (y_start, y_step, top, base, x_start, x_step, zero, zero)])
    return table.transpose(1, 3, 0, 2, 4).reshape(images, groups, 8, LANES), spans


def adamw(weight, moment, second, grad):
    moment = BETA_ONE * moment + (1.0 - BETA_ONE) * grad
    second = BETA_TWO * second + (1.0 - BETA_TWO) * grad * grad
    fixed_m = moment / (1.0 - BETA_ONE**STEP)
    fixed_v = second / (1.0 - BETA_TWO**STEP)
    weight = weight - RATE * (fixed_m / (jnp.sqrt(fixed_v) + EPSILON) + DECAY * weight)
    return (weight, moment, second)


def update_kernel(pooled_ref, back_ref, w_ref, m_ref, v_ref, *outs):
    grad = jnp.dot(pooled_ref[...], back_ref[...], preferred_element_type=jnp.float32)
    new = adamw(w_ref[...], m_ref[...], v_ref[...], grad)
    for ref, value in zip(outs, new):
        ref[...] = value


def update_first(pooled, back, weight, moment, second):
    passes, wide, hidden = weight.shape
    boxes = pooled.shape[2]
    block = wide // BINS
    big = pl.BlockSpec((None, block, hidden), lambda p, b: (p, b, 0))
    return pl.pallas_call(
        update_kernel,
        out_shape=[jax.ShapeDtypeStruct(weight.shape, jnp.float32)] * 3,
        grid=(passes, BINS),
        in_specs=[
            pl.BlockSpec((None, block, boxes), lambda p, b: (p, b, 0)),
            pl.BlockSpec((None, boxes, hidden), lambda p, b: (p, 0, 0)),
            big,
            big,
            big,
        ],
        out_specs=[big] * 3,
        compiler_params=pltpu.CompilerParams(vmem_limit_bytes=60 * MIB),
        cost_estimate=pl.CostEstimate(
            flops=2 * passes * wide * hidden * boxes,
            bytes_accessed=passes * wide * hidden * 24 + passes * boxes * (wide + hidden) * 2,
            transcendentals=passes * wide * hidden,
        ),
        name="update_first",
    )(pooled, back, weight, moment, second)


def loss_and_slope(logits, box, count):
    place = lax.broadcasted_iota(jnp.int32, logits.shape, 1)
    is_class = place < CLASSES
    label = box[:, 0:1].astype(jnp.int32)
    weight = box[:, 1:2]
    top = jnp.max(jnp.where(is_class, logits, -jnp.inf), axis=1, keepdims=True)
    grown = jnp.where(is_class, jnp.exp(jnp.where(is_class, logits - top, 0.0)), 0.0)
    norm = jnp.sum(grown, axis=1, keepdims=True)
    hot = place == label
    picked = jnp.sum(jnp.where(hot, logits, 0.0), axis=1, keepdims=True)
    fore = jnp.where(label > 0, weight, 0.0)
    rows = weight * (top + jnp.log(norm) - picked)
    slope = weight * (grown / norm - jnp.where(hot, 1.0, 0.0))
    offset = place - (CLASSES + 4 * (label - 1))
    for k in range(4):
        mask = (offset == k) & (place >= CLASSES)
        chosen = jnp.sum(jnp.where(mask, logits, 0.0), axis=1, keepdims=True)
        differ = fore * (chosen - box[:, 2 + k : 3 + k])
        near = jnp.abs(differ)
        rows += jnp.where(near < 1.0, 0.5 * differ * differ, near - 0.5) * fore
        slope = jnp.where(mask, fore * jnp.clip(differ, -1.0, 1.0), slope)
    return rows, slope / count


def sigmoid(value):
    return 1.0 / (1.0 + jnp.exp(-value))


def head_kernel(
    images, parts, mine,
    part_ref, weight_ref, box_ref, count_ref,
    back_ref, grad_ref,
    sums, landed, own, counts, split, cols, kept,
    rs_send, rs_recv, ag_send, ag_recv, up_send, up_recv, down_send, down_recv, own_sem,
    count_send, count_recv, col_send, col_recv, kept_send, kept_recv,
):
    me = lax.axis_index("narrow")
    level = lax.axis_index("wide")
    bits = parts.bit_length() - 1
    turn = [(1 - 2 * ((me // 2**k) % 2)) * 2**k for k in range(bits)]

    def peer(mask):
        return me + sum((turn[k] for k in range(bits) if mask >> k & 1), 0)

    links = list(range(1, bits))
    orders = [links, links[::-1]]

    barrier = pltpu.get_barrier_semaphore()
    for mask in range(1, parts):
        pl.semaphore_signal(barrier, inc=1, device_id={"narrow": peer(mask)})
    for k in range(1, images):
        pl.semaphore_signal(barrier, inc=1, device_id={"wide": lax.rem(level + k, images)})
    pl.semaphore_wait(barrier, parts + images - 2)

    counting = []
    for k in range(1, images):
        counting.append(
            pltpu.make_async_remote_copy(
                src_ref=count_ref,
                dst_ref=counts.at[k],
                send_sem=count_send.at[k],
                recv_sem=count_recv.at[k],
                device_id={"wide": lax.rem(level + k, images)},
            )
        )

    def scatter(p, mask, bit, source):
        return pltpu.make_async_remote_copy(
            src_ref=source,
            dst_ref=landed.at[p, mask],
            send_sem=rs_send.at[p, mask],
            recv_sem=rs_recv.at[p, mask],
            device_id={"narrow": peer(1 << bit)},
        )

    def part_at(p, mask):
        return part_ref.at[p, pl.ds(pl.multiple_of(peer(mask) * mine, mine), mine), :]

    copies = {}
    for p in range(2):
        for mask in range(1, parts, 2):
            copies[p, mask] = scatter(p, mask, 0, part_at(p, mask))
            copies[p, mask].start()

    def stage(p, at):
        order = [0] + orders[p]
        bit = order[at - 1]
        seen = sum(1 << b for b in order[:at])
        for mask in range(parts):
            if mask & seen:
                continue
            copies[p, mask | 1 << bit].wait_recv()
            if at == 1:
                have = part_ref[p, pl.ds(pl.multiple_of(peer(mask) * mine, mine), mine), :]
            else:
                have = sums[p, mask]
            sums[p, mask] = have + landed[p, mask | 1 << bit]
            if at < bits and mask >> order[at] & 1:
                copies[p, mask] = scatter(p, mask, order[at], sums.at[p, mask])
                copies[p, mask].start()

    for copy in counting:
        copy.start()
    for at in range(1, bits):
        for p in range(2):
            stage(p, at)

    def rows(p, image, mask):
        place = (image * parts + peer(mask)) * mine
        return back_ref.at[p, pl.ds(pl.multiple_of(place, mine), mine), :]

    def hop(p, d, up, source=None):
        image = level - d if up else level + d
        spot = rows(p, image, 0)
        return pltpu.make_async_remote_copy(
            src_ref=spot if source is None else source,
            dst_ref=spot,
            send_sem=(up_send if up else down_send).at[p, d],
            recv_sem=(up_recv if up else down_recv).at[p, d],
            device_id={"wide": level + 1 if up else level - 1},
        )

    def came(p, d, up):
        image = level - d if up else level + d
        spot = rows(p, image, 0)
        pltpu.make_async_remote_copy(
            src_ref=spot, dst_ref=spot, send_sem=(up_send if up else down_send).at[p, d],
            recv_sem=(up_recv if up else down_recv).at[p, d - 1],
            device_id={"wide": level - 1 if up else level + 1},
        ).wait_recv()

    steps = [orders[p] + [0] for p in range(2)]

    def masks_before(p, at):
        seen = sum(1 << b for b in steps[p][:at])
        return [m for m in range(parts) if not m & ~seen]

    def doubling(spot, send, recv):
        def spread(p, key, mask, bit, source=None):
            there = mask | 1 << bit
            return pltpu.make_async_remote_copy(
                src_ref=spot(p, key, mask) if source is None else source,
                dst_ref=spot(p, key, mask),
                send_sem=send.at[p, key, there],
                recv_sem=recv.at[p, key, there],
                device_id={"narrow": peer(1 << bit)},
            )

        def arrive(p, key, at):
            for m in masks_before(p, at):
                there = m | 1 << steps[p][at]
                pltpu.make_async_remote_copy(
                    src_ref=spot(p, key, there),
                    dst_ref=spot(p, key, there),
                    send_sem=send.at[p, key, there],
                    recv_sem=recv.at[p, key, there],
                    device_id={"narrow": peer(1)},
                ).wait_recv()

        def advance(p, key, at, source=None):
            if at:
                arrive(p, key, at - 1)
            for m in masks_before(p, at):
                spread(p, key, m, steps[p][at], source if m == 0 else None).start()

        def sent(p, key):
            for at in range(bits):
                for m in masks_before(p, at):
                    spread(p, key, m, steps[p][at]).wait_send()

        return advance, arrive, sent

    advance, arrive, sent = doubling(rows, ag_send, ag_recv)
    advance_kept, arrive_kept, sent_kept = doubling(
        lambda p, key, mask: kept.at[p, peer(mask)], kept_send, kept_recv
    )

    def finish(p, image):
        arrive(p, image, bits - 1)
        sent(p, image)

    span = grad_ref.shape[1]

    def hand(p, mask):
        return pltpu.make_async_remote_copy(
            src_ref=split.at[p, :, peer(mask)],
            dst_ref=cols.at[p, :, me],
            send_sem=col_send.at[p, mask],
            recv_sem=col_recv.at[p, mask],
            device_id={"narrow": peer(mask)},
        )

    def handed(p, mask):
        spot = cols.at[p, :, peer(mask)]
        pltpu.make_async_remote_copy(
            src_ref=spot, dst_ref=spot, send_sem=col_send.at[p, mask], recv_sem=col_recv.at[p, mask],
            device_id={"narrow": peer(mask)},
        ).wait_recv()

    for copy in counting:
        copy.wait_recv()
    count = count_ref[0:1, 0:1] + sum(counts[k, 0:1, 0:1] for k in range(1, images))
    hidden = part_ref.shape[2]
    for p in range(2):
        stage(p, bits)
        pre1 = sums[p, 0]
        sig1 = sigmoid(pre1)
        hid1 = (pre1 * sig1).astype(jnp.bfloat16)
        pre2 = jnp.dot(hid1, weight_ref[p, :, :hidden], preferred_element_type=jnp.float32)
        sig2 = sigmoid(pre2)
        hid2 = (pre2 * sig2).astype(jnp.bfloat16)
        logits = jnp.dot(hid2, weight_ref[p, :, hidden:], preferred_element_type=jnp.float32)
        loss, slope = loss_and_slope(logits, box_ref[p], count)
        back_z = slope.astype(jnp.bfloat16)
        across = (((1,), (1,)), ((), ()))
        back_h2 = lax.dot_general(back_z, weight_ref[p, :, hidden:], across, preferred_element_type=jnp.float32)
        back_p2 = (back_h2 * (sig2 * (1.0 + pre2 * (1.0 - sig2)))).astype(jnp.bfloat16)
        back_h1 = lax.dot_general(back_p2, weight_ref[p, :, :hidden], across, preferred_element_type=jnp.float32)
        own[p] = (back_h1 * (sig1 * (1.0 + pre1 * (1.0 - sig1)))).astype(jnp.bfloat16)

        @pl.when(level < images - 1)
        def _():
            hop(p, 0, True, own.at[p]).start()

        @pl.when(level > 0)
        def _():
            hop(p, 0, False, own.at[p]).start()

        advance(p, level, 0, own.at[p])
        pltpu.make_async_copy(own.at[p], rows(p, level, 0), own_sem.at[p]).start()
        place = lax.broadcasted_iota(jnp.int32, (mine, LANES), 1)
        losses = jnp.zeros((mine, LANES), jnp.float32)
        for k in range(3):
            near = loss.astype(jnp.bfloat16).astype(jnp.float32)
            losses = jnp.where(place == k, near, losses)
            loss = loss - near
        at = 0
        for value in (back_p2, back_z, losses.astype(jnp.bfloat16)):
            kept[p, me, :, at : at + value.shape[1]] = value
            at += value.shape[1]
        for owner in range(parts):
            split[p, 0, owner] = hid1[:, owner * span : (owner + 1) * span]
            split[p, 1, owner] = hid2[:, owner * span : (owner + 1) * span]
        for mask in range(1, parts):
            hand(p, mask).start()
    for p in range(2):
        pltpu.make_async_copy(own.at[p], rows(p, level, 0), own_sem.at[p]).wait()

    def each_side(d, do):
        @pl.when(level >= d)
        def _():
            do(level - d, True)

        @pl.when(level + d < images)
        def _():
            do(level + d, False)

    def enter(d):
        def do(image, up):
            for p in range(2):
                came(p, d, up)

                @pl.when((level < images - 1) if up else (level > 0))
                def _():
                    hop(p, d, up).start()

                advance(p, image, 0)

        each_side(d, do)

    def go_on(d, at):
        if d == 0:
            for p in range(2):
                advance(p, level, at)
        else:

            def do(image, up):
                for p in range(2):
                    advance(p, image, at)

            each_side(d, do)

    for tick in range(1, images + bits - 1):
        for d in range(images):
            at = tick - d
            if at == 0:
                enter(d)
            elif 0 < at < bits:
                go_on(d, at)
        if tick % 2 and tick // 2 < bits:
            for p in range(2):
                advance_kept(p, 0, tick // 2)
    for at in range((images + bits - 1) // 2, bits):
        for p in range(2):
            advance_kept(p, 0, at)

    loss = jnp.zeros((1, 1), jnp.float32)
    for p in range(2):
        arrive_kept(p, 0, bits - 1)
        for mask in range(1, parts):
            handed(p, mask)
        for k in range(2):
            cols[p, k, me] = split[p, k, me]
        slopes = kept[p].reshape(parts * mine, kept.shape[3])
        down = (((0,), (0,)), ((), ()))
        for k, (start, stop) in enumerate(((0, hidden), (hidden, grad_ref.shape[2]))):
            left = cols[p, k].reshape(parts * mine, span)
            grad_ref[p, :, start:stop] = lax.dot_general(
                left, slopes[:, start:stop], down, preferred_element_type=jnp.float32
            )
        loss += jnp.sum(slopes[:, grad_ref.shape[2] :].astype(jnp.float32), keepdims=True)
    corner = grad_ref[0, 0:8, grad_ref.shape[2] - LANES :]
    place = [lax.broadcasted_iota(jnp.int32, corner.shape, k) for k in range(2)]
    corner = jnp.where((place[0] == 0) & (place[1] == LANES - 1), loss, corner)
    grad_ref[0, 0:8, grad_ref.shape[2] - LANES :] = corner

    for p in range(2):
        finish(p, level)
        sent_kept(p, 0)
        for mask in range(1, parts):
            hand(p, mask).wait_send()

        @pl.when(level < images - 1)
        def _():
            hop(p, 0, True).wait_send()

        @pl.when(level > 0)
        def _():
            hop(p, 0, False).wait_send()

    for d in range(1, images):

        def do(image, up):
            for p in range(2):
                finish(p, image)

                @pl.when((level < images - 1) if up else (level > 0))
                def _():
                    hop(p, d, up).wait_send()

        each_side(d, do)
    for p in range(2):
        for mask in range(1, parts):
            copies[p, mask].wait_send()
    for copy in counting:
        copy.wait_send()


def head_step(part, weight, box, count, images, parts):
    passes, boxes, hidden = part.shape
    mine = boxes // parts
    outs = weight.shape[2] - hidden
    span = hidden // parts
    low = jnp.bfloat16
    vmem = pl.BlockSpec(memory_space=pltpu.VMEM)
    dma = pltpu.SemaphoreType.DMA
    return pl.pallas_call(
        partial(head_kernel, images, parts, mine),
        out_shape=[
            jax.ShapeDtypeStruct((passes, images * boxes, hidden), low),
            jax.ShapeDtypeStruct((passes, span, hidden + outs), jnp.float32),
        ],
        in_specs=[vmem] * 4,
        out_specs=[pl.BlockSpec(memory_space=pl.ANY), vmem],
        scratch_shapes=[
            pltpu.VMEM((passes, parts, mine, hidden), jnp.float32),
            pltpu.VMEM((passes, parts, mine, hidden), jnp.float32),
            pltpu.VMEM((passes, mine, hidden), low),
            pltpu.VMEM((images, 8, LANES), jnp.float32),
            pltpu.VMEM((passes, 2, parts, mine, span), low),
            pltpu.VMEM((passes, 2, parts, mine, span), low),
            pltpu.VMEM((passes, parts, mine, hidden + outs + LANES), low),
            dma((passes, parts)),
            dma((passes, parts)),
            dma((passes, images, parts)),
            dma((passes, images, parts)),
            dma((passes, images)),
            dma((passes, images)),
            dma((passes, images)),
            dma((passes, images)),
            dma((passes,)),
            dma((images,)),
            dma((images,)),
            dma((passes, parts)),
            dma((passes, parts)),
            dma((passes, 1, parts)),
            dma((passes, 1, parts)),
        ],
        compiler_params=pltpu.CompilerParams(
            vmem_limit_bytes=48 * MIB, collective_id=0, has_side_effects=True
        ),
        cost_estimate=pl.CostEstimate(
            flops=8 * passes * mine * hidden * (hidden + outs),
            bytes_accessed=100 * MIB,
            transcendentals=4 * passes * mine * hidden,
        ),
        name="head_step",
    )(part, weight, box, count)


def small_kernel(grad_ref, count_ref, *refs):
    hidden = refs[0].shape[2]
    outs = refs[3].shape[0]
    new = adamw(*(r[...] for r in refs[:3]), grad_ref[:, :, :hidden])
    for ref, value in zip(refs[6:9], new):
        ref[...] = value
    for p in range(grad_ref.shape[0]):
        grad = grad_ref[p, :, hidden:].T[:outs]
        new = adamw(*(r[:, p, :] for r in refs[3:6]), grad)
        for ref, value in zip(refs[9:12], new):
            ref[:, p, :] = value
    total = grad_ref[0, 0:1, grad_ref.shape[2] - 1 :]
    lane = lax.broadcasted_iota(jnp.int32, (8, LANES), 1)
    refs[12][...] = jnp.where(lane == 0, total, count_ref[...])


def update_small(grad, count, two, head):
    arrays = tuple(two) + tuple(x.transpose(2, 0, 1) for x in head)
    shapes = [jax.ShapeDtypeStruct(x.shape, jnp.float32) for x in arrays]
    out = pl.pallas_call(
        small_kernel,
        out_shape=shapes + [jax.ShapeDtypeStruct((8, LANES), jnp.float32)],
        compiler_params=pltpu.CompilerParams(vmem_limit_bytes=30 * MIB),
        name="update_small",
    )(grad, jnp.full((8, LANES), count), *arrays)
    return (out[6][0, :2],), out[:3], tuple(x.transpose(1, 2, 0) for x in out[3:6])


def per_device(
    feat_p2, feat_p3, feat_p4, feat_p5, rois, levels, labels, sampled, targets,
    fc1_w, fc1_m, fc1_v, fc2_w, fc2_m, fc2_v, head_w, head_m, head_v,
):
    side = feat_p2.shape[-1]
    channels = feat_p2.shape[1]
    boxes = rois.shape[2]
    images = lax.axis_size("wide")
    mine = boxes // lax.axis_size("narrow")
    first = lax.axis_index("narrow") * mine
    level = lax.axis_index("wide").astype(jnp.int32)
    parts = lax.axis_size("narrow")
    hidden = fc2_w.shape[2]
    outs = head_w.shape[2]
    zero = jnp.zeros((), jnp.int32)
    rank = box_order(rois[:, 0], levels[:, 0], side)
    ordered = sort_boxes(rois[:, 0], levels[:, 0], rank)
    feat = feature_rows((feat_p2, feat_p3, feat_p4, feat_p5))
    height = feat.shape[0]
    flags = sampled[:, 0].astype(jnp.bfloat16).reshape(1, 2, boxes)
    both = jnp.concatenate([feat, jnp.concatenate([ordered, flags]).reshape(-1, LANES)])
    weight = jnp.concatenate([fc2_w, jnp.pad(head_w, ((0, 0), (0, 0), (0, -outs % LANES)))], axis=2)
    weight = lax.all_gather(weight.astype(jnp.bfloat16), "narrow", axis=1, tiled=True)
    counted = jnp.sum(sampled).astype(jnp.float32)
    table, spans = box_table(ordered[None], side)
    pooled, own = pool(feat[None], table, spans, zero, level, images, channels)
    w1 = fc1_w.astype(jnp.bfloat16)
    part = lax.dot_general(own, w1, (((1,), (1,)), ((0,), (0,))), preferred_element_type=jnp.float32)
    both, weight, part = lax.optimization_barrier((both, weight, part))
    feats = lax.all_gather(both, "wide", axis=0)
    hot = rank[:, None, :] == first + jnp.arange(mine, dtype=jnp.int32)[:, None]

    def pick(values):
        return jnp.sum(jnp.where(hot, values[:, 0].astype(jnp.float32)[:, None, :], 0), axis=-1)

    box = [pick(labels), pick(sampled)] + [pick(targets[..., k]) for k in range(4)]
    box = jnp.pad(jnp.stack(box, axis=-1), ((0, 0), (0, 0), (0, LANES - 6)))
    back, grad = head_step(part, weight, box, jnp.full((8, LANES), counted), images, parts)
    grad = lax.psum_scatter(grad, "wide", scatter_dimension=1, tiled=True)

    tails = feats[:, height:].reshape(images, 6, 2, boxes)
    count = jnp.sum(tails[:, 5].astype(jnp.float32))
    tables, all_spans = box_table(tails[:, :5], side)
    turn = [lax.rem(level + k, images) for k in range(1, images)]
    for k in range(images - 1):
        pooled = pool(feats, tables, all_spans, turn[k], turn[k], images, channels, pooled)[0]
        if k == max(images - 3, 0):
            grad, pooled = lax.optimization_barrier((grad, pooled))
            grad = lax.all_gather(grad, "wide", axis=1, tiled=True)
    new1 = update_first(pooled, back, fc1_w, fc1_m, fc1_v)
    grad, new1 = lax.optimization_barrier((grad, new1))
    losses, new2, newh = update_small(grad, count, (fc2_w, fc2_m, fc2_v), (head_w, head_m, head_v))
    return losses + tuple(new1) + tuple(new2) + tuple(newh)


def solution(mesh):
    maps = P("wide", "narrow", None, None)
    rows = P(None, "narrow", None)
    box = P(None, "wide", None)
    coords = P(None, "wide", None, None)
    return jax.shard_map(
        per_device,
        mesh=mesh,
        in_specs=(maps,) * 4 + (coords, box, box, box, coords) + (rows,) * 9,
        out_specs=(P(),) + (rows,) * 9,
        check_vma=False,
    )
```

```python
from functools import partial

import jax
import jax.numpy as jnp
from jax import lax
from jax.experimental import pallas as pl
from jax.experimental.pallas import tpu as pltpu
from jax.sharding import PartitionSpec as P

CLASSES = 81
STEP = 5
BETA_ONE = 0.5
BETA_TWO = 0.5
RATE = 0.02
DECAY = 0.01
EPSILON = 1e-08
BINS = 7
CHUNK = 8
STATIC = 4
WINDOW = 20
MORE = 4
SPANS = 17
LANES = 128
MIB = 2**20


def tent(where, cells):
    return 0.5 * sum(jnp.maximum(0.0, 1.0 - jnp.abs(w - cells)) for w in where)


def pool_kernel(channels, side, groups, copies, pick_ref, span_ref, feat_ref, table_ref, *refs):
    out_refs = refs[-7 - copies : -7]
    cols, rows, parts = refs[-7:-5], refs[-5:-3], refs[-3:-1]
    line_ref = refs[-1]
    image = pick_ref[0]
    half = LANES // 2
    offsets = (0.25, 0.75)
    cells = lax.broadcasted_iota(jnp.int32, (side, LANES), 0).astype(jnp.float32)
    bins = lax.broadcasted_iota(jnp.int32, (8, LANES), 0).astype(jnp.float32)

    def at(group):
        return (image * groups + group) * SPANS

    def param(group, k):
        return table_ref[group, k : k + 1, :]

    def weights(group, slot):
        top, x_start, x_step = param(group, 2), param(group, 4), param(group, 5)
        for j in range(BINS):
            where = [jnp.clip(x_start + (j + off) * x_step, 0.0, top) for off in offsets]
            weight = tent(where, cells)
            high = weight.astype(jnp.bfloat16)
            low = (weight - high.astype(jnp.float32)).astype(jnp.bfloat16)
            lanes = pl.ds(j * LANES, LANES)
            cols[slot][0:side, lanes] = high
            cols[slot][side : 2 * side, lanes] = high
            cols[slot][2 * side : 3 * side, lanes] = low
            cols[slot][3 * side : 4 * side, lanes] = low

    def fill(group, slot, row):
        y_start, y_step, top, base = (param(group, k) for k in range(4))
        where = [jnp.clip(y_start + (bins + off) * y_step, 0.0, top) for off in offsets]
        for h in range(CHUNK):
            rows[slot][row + h] = tent(where, (row + h).astype(jnp.float32) - base)
        place = pl.ds(pl.multiple_of(row * channels, channels), CHUNK * channels)
        left = feat_ref[place, :]
        left = jnp.concatenate([left, left], axis=1)
        parts[slot][place, :] = jnp.dot(left, cols[slot][...], preferred_element_type=jnp.float32)

    def rest(group, slot):
        first = span_ref[at(group)] + STATIC * CHUNK

        @pl.loop(0, span_ref[at(group) + 1])
        def _(t):
            fill(group, slot, first + t * CHUNK)

    def block(slot, i, low_row, count):
        accs = None
        for h in range(count):
            start = pl.multiple_of((low_row + h) * channels, channels)
            weight = jnp.broadcast_to(rows[slot][low_row + h, i : i + 1, :], (channels, LANES))
            new = [
                weight * parts[slot][pl.ds(start, channels), j * LANES : (j + 1) * LANES] for j in range(BINS)
            ]
            accs = new if accs is None else [x + y for x, y in zip(accs, new)]
        return accs

    def spot(i, j):
        return pl.ds(i * BINS + j, channels, stride=BINS * BINS)

    def work(group, slot, following, beside):
        for i in range(BINS):
            accs = block(slot, i, span_ref[at(group) + 3 + i], WINDOW)
            for j in range(BINS):
                line_ref[slot, spot(i, j), :] = accs[j]
            if beside and i < STATIC:
                fill(following, 1 - slot, span_ref[at(following)] + i * CHUNK)

        @pl.when(span_ref[at(group) + 2] > 0)
        def _():
            for i in range(BINS):
                low_row = span_ref[at(group) + 3 + i] + WINDOW

                @pl.loop(0, span_ref[at(group) + 3 + BINS + i])
                def _(t):
                    more = block(slot, i, low_row + t * MORE, MORE)
                    for j in range(BINS):
                        line_ref[slot, spot(i, j), :] = line_ref[slot, spot(i, j), :] + more[j]

    step = pl.program_id(0)

    @pl.when(step == 0)
    def _():
        weights(0, 0)
        for i in range(STATIC):
            fill(0, 0, span_ref[at(0)] + i * CHUNK)
        rest(0, 0)

    group = 2 * step
    weights(group + 1, 1)
    work(group, 0, group + 1, True)
    rest(group + 1, 1)

    @pl.when(group + 2 < groups)
    def _():
        weights(group + 2, 0)
        work(group + 1, 1, group + 2, True)
        rest(group + 2, 0)

    @pl.when(group + 2 >= groups)
    def _():
        work(group + 1, 1, group + 1, False)

    a, b = line_ref[0], line_ref[1]
    lanes = lax.broadcasted_iota(jnp.int32, a.shape, 1)
    new = [jnp.where(lanes < half, a, pltpu.roll(b, half, 1)), jnp.where(lanes < half, pltpu.roll(a, half, 1), b)]
    for out_ref in out_refs:
        for p in range(2):
            out_ref[p] = new[p].astype(jnp.bfloat16)


def pool(feat, table, spans, source, image, images, channels, buffer=None):
    depth = feat.shape[2]
    groups = table.shape[1]
    wide = channels * BINS * BINS
    side = depth // 2
    rows = sum(side >> k for k in range(4))
    boxes = groups * LANES // 2
    blocks = groups // 2
    pick = jnp.stack([source, image])
    out_shape = [jax.ShapeDtypeStruct((2, wide, images * boxes), jnp.bfloat16)]
    out_specs = [pl.BlockSpec((2, wide, LANES), lambda s, pick, spans: (0, 0, pick[1] * blocks + s))]
    in_specs = [
        pl.BlockSpec((None, rows * channels, depth), lambda s, pick, spans: (pick[0], 0, 0)),
        pl.BlockSpec((None, groups, 8, LANES), lambda s, pick, spans: (pick[0], 0, 0, 0)),
    ]
    operands = (pick, spans, feat, table)
    aliases = {}
    if buffer is None:
        out_shape.append(jax.ShapeDtypeStruct((2, wide, boxes), jnp.bfloat16))
        out_specs.append(pl.BlockSpec((2, wide, LANES), lambda s, pick, spans: (0, 0, s)))
    else:
        in_specs.append(pl.BlockSpec(memory_space=pl.ANY))
        operands += (buffer,)
        aliases = {4: 0}
    return pl.pallas_call(
        partial(pool_kernel, channels, side, groups, len(out_shape)),
        out_shape=out_shape,
        grid_spec=pltpu.PrefetchScalarGridSpec(
            num_scalar_prefetch=2,
            grid=(blocks,),
            in_specs=in_specs,
            out_specs=out_specs,
            scratch_shapes=[
                pltpu.VMEM((4 * side, BINS * LANES), jnp.bfloat16),
                pltpu.VMEM((4 * side, BINS * LANES), jnp.bfloat16),
                pltpu.VMEM((rows, 8, LANES), jnp.float32),
                pltpu.VMEM((rows, 8, LANES), jnp.float32),
                pltpu.VMEM((rows * channels, BINS * LANES), jnp.float32),
                pltpu.VMEM((rows * channels, BINS * LANES), jnp.float32),
                pltpu.VMEM((2, wide, LANES), jnp.float32),
            ],
        ),
        input_output_aliases=aliases,
        compiler_params=pltpu.CompilerParams(vmem_limit_bytes=60 * MIB),
        cost_estimate=pl.CostEstimate(
            flops=groups * 40 * channels * BINS * LANES * 8 * depth,
            bytes_accessed=80 * MIB,
            transcendentals=0,
        ),
        name="pool_rois",
    )(*operands)


def feature_rows(maps):
    side = maps[0].shape[-1]
    parts = [
        jnp.pad(m.transpose(0, 2, 1, 3), ((0, 0), (0, 0), (0, 0), (0, side - m.shape[-1])))
        for m in maps
    ]
    full = jnp.concatenate(parts, axis=1)
    high = lax.reduce_precision(full, 8, 7)
    low = (full - high).astype(jnp.bfloat16)
    full = jnp.concatenate([high.astype(jnp.bfloat16), low], axis=-1)
    return full.reshape(-1, 2 * side)


def box_order(boxes, levels, side):
    base = 2 * side - 2 * (side >> levels)
    key = ((boxes[..., 1] + boxes[..., 3]) >> levels) + base * 8
    key = key * key.shape[-1] + jnp.arange(key.shape[-1], dtype=jnp.int32)
    return jnp.sum((key[..., :, None] > key[..., None, :]).astype(jnp.int32), axis=-1)


def sort_boxes(boxes, levels, rank):
    count = boxes.shape[1]
    hot = (rank[:, None, :] == jnp.arange(count, dtype=jnp.int32)[:, None]).astype(jnp.bfloat16)
    both = jnp.concatenate([boxes, levels[..., None]], axis=-1).astype(jnp.bfloat16)
    return jnp.einsum("psr,prk->kps", hot, both, preferred_element_type=jnp.float32).astype(jnp.bfloat16)


def box_table(boxes, side):
    images, _, _, count = boxes.shape
    x0, y0, x1, y1, level = (boxes[:, k].astype(jnp.float32) for k in range(5))
    rows = sum(side >> k for k in range(4))
    scale = jnp.where(level < 0.5, 0.25, jnp.where(level < 1.5, 0.125, jnp.where(level < 2.5, 0.0625, 0.03125)))
    height = scale * (4 * side)
    base = 2.0 * side - 2.0 * height
    top = height - 1.0

    def axis(low, high):
        return low * scale - 0.5, ((high - low) * scale) / 7.0

    x_start, x_step = axis(x0, x1)
    y_start, y_step = axis(y0, y1)
    half = LANES // 2
    groups = count // half

    def split(v):
        return v.reshape(v.shape[:-1] + (groups, half))

    lows, highs = [], []
    for i in range(BINS):
        low = base + jnp.floor(jnp.clip(y_start + (i + 0.25) * y_step, 0.0, top))
        high = base + jnp.floor(jnp.clip(y_start + (i + 0.75) * y_step, 0.0, top)) + 1.0
        lows.append(jnp.min(split(low), axis=(1, 3)))
        highs.append(jnp.max(split(jnp.minimum(high, rows - 1.0)), axis=(1, 3)))
    low = jnp.stack(lows, axis=-1).astype(jnp.int32)
    high = jnp.stack(highs, axis=-1).astype(jnp.int32)
    least = jnp.min(low, axis=-1)
    chunks = jnp.maximum((jnp.max(high, axis=-1) - least + CHUNK) // CHUNK, STATIC)
    first = jnp.clip(rows - chunks * CHUNK, 0, least)
    extra = jnp.maximum(high - low + MORE - WINDOW, 0) // MORE
    low = jnp.minimum(low, (first + chunks * CHUNK)[..., None] - WINDOW - MORE * extra)
    heads = jnp.stack([first, chunks - STATIC, jnp.max(extra, axis=-1)], axis=-1)
    spans = jnp.concatenate([heads, low, extra], axis=-1).reshape(-1)
    zero = jnp.zeros_like(base)
    table = jnp.stack([split(v) for v in (y_start, y_step, top, base, x_start, x_step, zero, zero)])
    return table.transpose(1, 3, 0, 2, 4).reshape(images, groups, 8, LANES), spans


def adamw(weight, moment, second, grad):
    moment = BETA_ONE * moment + (1.0 - BETA_ONE) * grad
    second = BETA_TWO * second + (1.0 - BETA_TWO) * grad * grad
    fixed_m = moment / (1.0 - BETA_ONE**STEP)
    fixed_v = second / (1.0 - BETA_TWO**STEP)
    weight = weight - RATE * (fixed_m / (jnp.sqrt(fixed_v) + EPSILON) + DECAY * weight)
    return (weight, moment, second)


def update_kernel(pooled_ref, back_ref, w_ref, m_ref, v_ref, *outs):
    grad = jnp.dot(pooled_ref[...], back_ref[...], preferred_element_type=jnp.float32)
    new = adamw(w_ref[...], m_ref[...], v_ref[...], grad)
    for ref, value in zip(outs, new):
        ref[...] = value


def update_first(pooled, back, weight, moment, second):
    passes, wide, hidden = weight.shape
    boxes = pooled.shape[2]
    block = wide // BINS
    big = pl.BlockSpec((None, block, hidden), lambda p, b: (p, b, 0))
    return pl.pallas_call(
        update_kernel,
        out_shape=[jax.ShapeDtypeStruct(weight.shape, jnp.float32)] * 3,
        grid=(passes, BINS),
        in_specs=[
            pl.BlockSpec((None, block, boxes), lambda p, b: (p, b, 0)),
            pl.BlockSpec((None, boxes, hidden), lambda p, b: (p, 0, 0)),
            big,
            big,
            big,
        ],
        out_specs=[big] * 3,
        compiler_params=pltpu.CompilerParams(vmem_limit_bytes=60 * MIB),
        cost_estimate=pl.CostEstimate(
            flops=2 * passes * wide * hidden * boxes,
            bytes_accessed=passes * wide * hidden * 24 + passes * boxes * (wide + hidden) * 2,
            transcendentals=passes * wide * hidden,
        ),
        name="update_first",
    )(pooled, back, weight, moment, second)


def loss_and_slope(logits, box, count):
    place = lax.broadcasted_iota(jnp.int32, logits.shape, 1)
    is_class = place < CLASSES
    label = box[:, 0:1].astype(jnp.int32)
    weight = box[:, 1:2]
    top = jnp.max(jnp.where(is_class, logits, -jnp.inf), axis=1, keepdims=True)
    grown = jnp.where(is_class, jnp.exp(jnp.where(is_class, logits - top, 0.0)), 0.0)
    norm = jnp.sum(grown, axis=1, keepdims=True)
    hot = place == label
    picked = jnp.sum(jnp.where(hot, logits, 0.0), axis=1, keepdims=True)
    fore = jnp.where(label > 0, weight, 0.0)
    rows = weight * (top + jnp.log(norm) - picked)
    slope = weight * (grown / norm - jnp.where(hot, 1.0, 0.0))
    offset = place - (CLASSES + 4 * (label - 1))
    for k in range(4):
        mask = (offset == k) & (place >= CLASSES)
        chosen = jnp.sum(jnp.where(mask, logits, 0.0), axis=1, keepdims=True)
        differ = fore * (chosen - box[:, 2 + k : 3 + k])
        near = jnp.abs(differ)
        rows += jnp.where(near < 1.0, 0.5 * differ * differ, near - 0.5) * fore
        slope = jnp.where(mask, fore * jnp.clip(differ, -1.0, 1.0), slope)
    return rows, slope / count


def sigmoid(value):
    return 1.0 / (1.0 + jnp.exp(-value))


def head_kernel(
    images, parts, mine,
    part_ref, weight_ref, box_ref, count_ref,
    back_ref, grad_ref,
    sums, landed, own, counts, split, cols, kept,
    rs_send, rs_recv, ag_send, ag_recv, up_send, up_recv, down_send, down_recv, own_sem,
    count_send, count_recv, col_send, col_recv, kept_send, kept_recv,
):
    me = lax.axis_index("narrow")
    level = lax.axis_index("wide")
    bits = parts.bit_length() - 1
    turn = [(1 - 2 * ((me // 2**k) % 2)) * 2**k for k in range(bits)]

    def peer(mask):
        return me + sum((turn[k] for k in range(bits) if mask >> k & 1), 0)

    links = list(range(1, bits))
    orders = [links, links[::-1]]

    barrier = pltpu.get_barrier_semaphore()
    for mask in range(1, parts):
        pl.semaphore_signal(barrier, inc=1, device_id={"narrow": peer(mask)})
    for k in range(1, images):
        pl.semaphore_signal(barrier, inc=1, device_id={"wide": lax.rem(level + k, images)})
    pl.semaphore_wait(barrier, parts + images - 2)

    counting = []
    for k in range(1, images):
        counting.append(
            pltpu.make_async_remote_copy(
                src_ref=count_ref,
                dst_ref=counts.at[k],
                send_sem=count_send.at[k],
                recv_sem=count_recv.at[k],
                device_id={"wide": lax.rem(level + k, images)},
            )
        )

    def scatter(p, mask, bit, source):
        return pltpu.make_async_remote_copy(
            src_ref=source,
            dst_ref=landed.at[p, mask],
            send_sem=rs_send.at[p, mask],
            recv_sem=rs_recv.at[p, mask],
            device_id={"narrow": peer(1 << bit)},
        )

    def part_at(p, mask):
        return part_ref.at[p, pl.ds(pl.multiple_of(peer(mask) * mine, mine), mine), :]

    copies = {}
    for p in range(2):
        for mask in range(1, parts, 2):
            copies[p, mask] = scatter(p, mask, 0, part_at(p, mask))
            copies[p, mask].start()

    def stage(p, at):
        order = [0] + orders[p]
        bit = order[at - 1]
        seen = sum(1 << b for b in order[:at])
        for mask in range(parts):
            if mask & seen:
                continue
            copies[p, mask | 1 << bit].wait_recv()
            if at == 1:
                have = part_ref[p, pl.ds(pl.multiple_of(peer(mask) * mine, mine), mine), :]
            else:
                have = sums[p, mask]
            sums[p, mask] = have + landed[p, mask | 1 << bit]
            if at < bits and mask >> order[at] & 1:
                copies[p, mask] = scatter(p, mask, order[at], sums.at[p, mask])
                copies[p, mask].start()

    for copy in counting:
        copy.start()
    for at in range(1, bits):
        for p in range(2):
            stage(p, at)

    def rows(p, image, mask):
        place = (image * parts + peer(mask)) * mine
        return back_ref.at[p, pl.ds(pl.multiple_of(place, mine), mine), :]

    def hop(p, d, up, source=None):
        image = level - d if up else level + d
        spot = rows(p, image, 0)
        return pltpu.make_async_remote_copy(
            src_ref=spot if source is None else source,
            dst_ref=spot,
            send_sem=(up_send if up else down_send).at[p, d],
            recv_sem=(up_recv if up else down_recv).at[p, d],
            device_id={"wide": level + 1 if up else level - 1},
        )

    def came(p, d, up):
        image = level - d if up else level + d
        spot = rows(p, image, 0)
        pltpu.make_async_remote_copy(
            src_ref=spot, dst_ref=spot, send_sem=(up_send if up else down_send).at[p, d],
            recv_sem=(up_recv if up else down_recv).at[p, d - 1],
            device_id={"wide": level - 1 if up else level + 1},
        ).wait_recv()

    steps = [orders[p] + [0] for p in range(2)]

    def masks_before(p, at):
        seen = sum(1 << b for b in steps[p][:at])
        return [m for m in range(parts) if not m & ~seen]

    def doubling(spot, send, recv):
        def spread(p, key, mask, bit, source=None):
            there = mask | 1 << bit
            return pltpu.make_async_remote_copy(
                src_ref=spot(p, key, mask) if source is None else source,
                dst_ref=spot(p, key, mask),
                send_sem=send.at[p, key, there],
                recv_sem=recv.at[p, key, there],
                device_id={"narrow": peer(1 << bit)},
            )

        def arrive(p, key, at):
            for m in masks_before(p, at):
                there = m | 1 << steps[p][at]
                pltpu.make_async_remote_copy(
                    src_ref=spot(p, key, there),
                    dst_ref=spot(p, key, there),
                    send_sem=send.at[p, key, there],
                    recv_sem=recv.at[p, key, there],
                    device_id={"narrow": peer(1)},
                ).wait_recv()

        def advance(p, key, at, source=None):
            if at:
                arrive(p, key, at - 1)
            for m in masks_before(p, at):
                spread(p, key, m, steps[p][at], source if m == 0 else None).start()

        def sent(p, key):
            for at in range(bits):
                for m in masks_before(p, at):
                    spread(p, key, m, steps[p][at]).wait_send()

        return advance, arrive, sent

    advance, arrive, sent = doubling(rows, ag_send, ag_recv)
    advance_kept, arrive_kept, sent_kept = doubling(
        lambda p, key, mask: kept.at[p, peer(mask)], kept_send, kept_recv
    )

    def finish(p, image):
        arrive(p, image, bits - 1)
        sent(p, image)

    span = grad_ref.shape[1]

    def hand(p, mask):
        return pltpu.make_async_remote_copy(
            src_ref=split.at[p, :, peer(mask)],
            dst_ref=cols.at[p, :, me],
            send_sem=col_send.at[p, mask],
            recv_sem=col_recv.at[p, mask],
            device_id={"narrow": peer(mask)},
        )

    def handed(p, mask):
        spot = cols.at[p, :, peer(mask)]
        pltpu.make_async_remote_copy(
            src_ref=spot, dst_ref=spot, send_sem=col_send.at[p, mask], recv_sem=col_recv.at[p, mask],
            device_id={"narrow": peer(mask)},
        ).wait_recv()

    for copy in counting:
        copy.wait_recv()
    count = count_ref[0:1, 0:1] + sum(counts[k, 0:1, 0:1] for k in range(1, images))
    hidden = part_ref.shape[2]
    for p in range(2):
        stage(p, bits)
        pre1 = sums[p, 0]
        sig1 = sigmoid(pre1)
        hid1 = (pre1 * sig1).astype(jnp.bfloat16)
        pre2 = jnp.dot(hid1, weight_ref[p, :, :hidden], preferred_element_type=jnp.float32)
        sig2 = sigmoid(pre2)
        hid2 = (pre2 * sig2).astype(jnp.bfloat16)
        logits = jnp.dot(hid2, weight_ref[p, :, hidden:], preferred_element_type=jnp.float32)
        loss, slope = loss_and_slope(logits, box_ref[p], count)
        back_z = slope.astype(jnp.bfloat16)
        across = (((1,), (1,)), ((), ()))
        back_h2 = lax.dot_general(back_z, weight_ref[p, :, hidden:], across, preferred_element_type=jnp.float32)
        back_p2 = (back_h2 * (sig2 * (1.0 + pre2 * (1.0 - sig2)))).astype(jnp.bfloat16)
        back_h1 = lax.dot_general(back_p2, weight_ref[p, :, :hidden], across, preferred_element_type=jnp.float32)
        own[p] = (back_h1 * (sig1 * (1.0 + pre1 * (1.0 - sig1)))).astype(jnp.bfloat16)

        @pl.when(level < images - 1)
        def _():
            hop(p, 0, True, own.at[p]).start()

        @pl.when(level > 0)
        def _():
            hop(p, 0, False, own.at[p]).start()

        advance(p, level, 0, own.at[p])
        pltpu.make_async_copy(own.at[p], rows(p, level, 0), own_sem.at[p]).start()
        place = lax.broadcasted_iota(jnp.int32, (mine, LANES), 1)
        losses = jnp.zeros((mine, LANES), jnp.float32)
        for k in range(3):
            near = loss.astype(jnp.bfloat16).astype(jnp.float32)
            losses = jnp.where(place == k, near, losses)
            loss = loss - near
        at = 0
        for value in (back_p2, back_z, losses.astype(jnp.bfloat16)):
            kept[p, me, :, at : at + value.shape[1]] = value
            at += value.shape[1]
        advance_kept(p, 0, 0)
        for owner in range(parts):
            split[p, 0, owner] = hid1[:, owner * span : (owner + 1) * span]
            split[p, 1, owner] = hid2[:, owner * span : (owner + 1) * span]
        for mask in range(1, parts):
            hand(p, mask).start()
    for p in range(2):
        pltpu.make_async_copy(own.at[p], rows(p, level, 0), own_sem.at[p]).wait()

    def each_side(d, do):
        @pl.when(level >= d)
        def _():
            do(level - d, True)

        @pl.when(level + d < images)
        def _():
            do(level + d, False)

    def enter(d):
        def do(image, up):
            for p in range(2):
                came(p, d, up)

                @pl.when((level < images - 1) if up else (level > 0))
                def _():
                    hop(p, d, up).start()

                advance(p, image, 0)

        each_side(d, do)

    def go_on(d, at):
        if d == 0:
            for p in range(2):
                advance(p, level, at)
                advance_kept(p, 0, at)
        else:

            def do(image, up):
                for p in range(2):
                    advance(p, image, at)

            each_side(d, do)

    for tick in range(1, images + bits - 1):
        for d in range(images):
            at = tick - d
            if at == 0:
                enter(d)
            elif 0 < at < bits:
                go_on(d, at)

    loss = jnp.zeros((1, 1), jnp.float32)
    for p in range(2):
        arrive_kept(p, 0, bits - 1)
        for mask in range(1, parts):
            handed(p, mask)
        for k in range(2):
            cols[p, k, me] = split[p, k, me]
        slopes = kept[p].reshape(parts * mine, kept.shape[3])
        down = (((0,), (0,)), ((), ()))
        for k, (start, stop) in enumerate(((0, hidden), (hidden, grad_ref.shape[2]))):
            left = cols[p, k].reshape(parts * mine, span)
            grad_ref[p, :, start:stop] = lax.dot_general(
                left, slopes[:, start:stop], down, preferred_element_type=jnp.float32
            )
        loss += jnp.sum(slopes[:, grad_ref.shape[2] :].astype(jnp.float32), keepdims=True)
    corner = grad_ref[0, 0:8, grad_ref.shape[2] - LANES :]
    place = [lax.broadcasted_iota(jnp.int32, corner.shape, k) for k in range(2)]
    corner = jnp.where((place[0] == 0) & (place[1] == LANES - 1), loss, corner)
    grad_ref[0, 0:8, grad_ref.shape[2] - LANES :] = corner

    for p in range(2):
        finish(p, level)
        sent_kept(p, 0)
        for mask in range(1, parts):
            hand(p, mask).wait_send()

        @pl.when(level < images - 1)
        def _():
            hop(p, 0, True).wait_send()

        @pl.when(level > 0)
        def _():
            hop(p, 0, False).wait_send()

    for d in range(1, images):

        def do(image, up):
            for p in range(2):
                finish(p, image)

                @pl.when((level < images - 1) if up else (level > 0))
                def _():
                    hop(p, d, up).wait_send()

        each_side(d, do)
    for p in range(2):
        for mask in range(1, parts):
            copies[p, mask].wait_send()
    for copy in counting:
        copy.wait_send()


def head_step(part, weight, box, count, images, parts):
    passes, boxes, hidden = part.shape
    mine = boxes // parts
    outs = weight.shape[2] - hidden
    span = hidden // parts
    low = jnp.bfloat16
    vmem = pl.BlockSpec(memory_space=pltpu.VMEM)
    dma = pltpu.SemaphoreType.DMA
    return pl.pallas_call(
        partial(head_kernel, images, parts, mine),
        out_shape=[
            jax.ShapeDtypeStruct((passes, images * boxes, hidden), low),
            jax.ShapeDtypeStruct((passes, span, hidden + outs), jnp.float32),
        ],
        in_specs=[vmem] * 4,
        out_specs=[pl.BlockSpec(memory_space=pl.ANY), vmem],
        scratch_shapes=[
            pltpu.VMEM((passes, parts, mine, hidden), jnp.float32),
            pltpu.VMEM((passes, parts, mine, hidden), jnp.float32),
            pltpu.VMEM((passes, mine, hidden), low),
            pltpu.VMEM((images, 8, LANES), jnp.float32),
            pltpu.VMEM((passes, 2, parts, mine, span), low),
            pltpu.VMEM((passes, 2, parts, mine, span), low),
            pltpu.VMEM((passes, parts, mine, hidden + outs + LANES), low),
            dma((passes, parts)),
            dma((passes, parts)),
            dma((passes, images, parts)),
            dma((passes, images, parts)),
            dma((passes, images)),
            dma((passes, images)),
            dma((passes, images)),
            dma((passes, images)),
            dma((passes,)),
            dma((images,)),
            dma((images,)),
            dma((passes, parts)),
            dma((passes, parts)),
            dma((passes, 1, parts)),
            dma((passes, 1, parts)),
        ],
        compiler_params=pltpu.CompilerParams(
            vmem_limit_bytes=48 * MIB, collective_id=0, has_side_effects=True
        ),
        cost_estimate=pl.CostEstimate(
            flops=8 * passes * mine * hidden * (hidden + outs),
            bytes_accessed=100 * MIB,
            transcendentals=4 * passes * mine * hidden,
        ),
        name="head_step",
    )(part, weight, box, count)


def small_kernel(grad_ref, count_ref, *refs):
    hidden = refs[0].shape[2]
    outs = refs[3].shape[0]
    new = adamw(*(r[...] for r in refs[:3]), grad_ref[:, :, :hidden])
    for ref, value in zip(refs[6:9], new):
        ref[...] = value
    for p in range(grad_ref.shape[0]):
        grad = grad_ref[p, :, hidden:].T[:outs]
        new = adamw(*(r[:, p, :] for r in refs[3:6]), grad)
        for ref, value in zip(refs[9:12], new):
            ref[:, p, :] = value
    total = grad_ref[0, 0:1, grad_ref.shape[2] - 1 :]
    lane = lax.broadcasted_iota(jnp.int32, (8, LANES), 1)
    refs[12][...] = jnp.where(lane == 0, total, count_ref[...])


def update_small(grad, count, two, head):
    arrays = tuple(two) + tuple(x.transpose(2, 0, 1) for x in head)
    shapes = [jax.ShapeDtypeStruct(x.shape, jnp.float32) for x in arrays]
    out = pl.pallas_call(
        small_kernel,
        out_shape=shapes + [jax.ShapeDtypeStruct((8, LANES), jnp.float32)],
        compiler_params=pltpu.CompilerParams(vmem_limit_bytes=30 * MIB),
        name="update_small",
    )(grad, jnp.full((8, LANES), count), *arrays)
    return (out[6][0, :2],), out[:3], tuple(x.transpose(1, 2, 0) for x in out[3:6])


def per_device(
    feat_p2, feat_p3, feat_p4, feat_p5, rois, levels, labels, sampled, targets,
    fc1_w, fc1_m, fc1_v, fc2_w, fc2_m, fc2_v, head_w, head_m, head_v,
):
    side = feat_p2.shape[-1]
    channels = feat_p2.shape[1]
    boxes = rois.shape[2]
    images = lax.axis_size("wide")
    mine = boxes // lax.axis_size("narrow")
    first = lax.axis_index("narrow") * mine
    level = lax.axis_index("wide").astype(jnp.int32)
    parts = lax.axis_size("narrow")
    hidden = fc2_w.shape[2]
    outs = head_w.shape[2]
    zero = jnp.zeros((), jnp.int32)
    rank = box_order(rois[:, 0], levels[:, 0], side)
    ordered = sort_boxes(rois[:, 0], levels[:, 0], rank)
    feat = feature_rows((feat_p2, feat_p3, feat_p4, feat_p5))
    height = feat.shape[0]
    flags = sampled[:, 0].astype(jnp.bfloat16).reshape(1, 2, boxes)
    both = jnp.concatenate([feat, jnp.concatenate([ordered, flags]).reshape(-1, LANES)])
    weight = jnp.concatenate([fc2_w, jnp.pad(head_w, ((0, 0), (0, 0), (0, -outs % LANES)))], axis=2)
    weight = lax.all_gather(weight.astype(jnp.bfloat16), "narrow", axis=1, tiled=True)
    counted = jnp.sum(sampled).astype(jnp.float32)
    table, spans = box_table(ordered[None], side)
    pooled, own = pool(feat[None], table, spans, zero, level, images, channels)
    w1 = fc1_w.astype(jnp.bfloat16)
    part = lax.dot_general(own, w1, (((1,), (1,)), ((0,), (0,))), preferred_element_type=jnp.float32)
    both, weight, part = lax.optimization_barrier((both, weight, part))
    feats = lax.all_gather(both, "wide", axis=0)
    hot = rank[:, None, :] == first + jnp.arange(mine, dtype=jnp.int32)[:, None]

    def pick(values):
        return jnp.sum(jnp.where(hot, values[:, 0].astype(jnp.float32)[:, None, :], 0), axis=-1)

    box = [pick(labels), pick(sampled)] + [pick(targets[..., k]) for k in range(4)]
    box = jnp.pad(jnp.stack(box, axis=-1), ((0, 0), (0, 0), (0, LANES - 6)))
    back, grad = head_step(part, weight, box, jnp.full((8, LANES), counted), images, parts)
    grad = lax.psum_scatter(grad, "wide", scatter_dimension=1, tiled=True)

    tails = feats[:, height:].reshape(images, 6, 2, boxes)
    count = jnp.sum(tails[:, 5].astype(jnp.float32))
    tables, all_spans = box_table(tails[:, :5], side)
    turn = [lax.rem(level + k, images) for k in range(1, images)]
    for k in range(images - 1):
        pooled = pool(feats, tables, all_spans, turn[k], turn[k], images, channels, pooled)[0]
        if k == max(images - 3, 0):
            grad, pooled = lax.optimization_barrier((grad, pooled))
            grad = lax.all_gather(grad, "wide", axis=1, tiled=True)
    new1 = update_first(pooled, back, fc1_w, fc1_m, fc1_v)
    grad, new1 = lax.optimization_barrier((grad, new1))
    losses, new2, newh = update_small(grad, count, (fc2_w, fc2_m, fc2_v), (head_w, head_m, head_v))
    return losses + tuple(new1) + tuple(new2) + tuple(newh)


def solution(mesh):
    maps = P("wide", "narrow", None, None)
    rows = P(None, "narrow", None)
    box = P(None, "wide", None)
    coords = P(None, "wide", None, None)
    return jax.shard_map(
        per_device,
        mesh=mesh,
        in_specs=(maps,) * 4 + (coords, box, box, box, coords) + (rows,) * 9,
        out_specs=(P(),) + (rows,) * 9,
        check_vma=False,
    )
```

```python
from functools import partial

import jax
import jax.numpy as jnp
from jax import lax
from jax.experimental import pallas as pl
from jax.experimental.pallas import tpu as pltpu
from jax.sharding import PartitionSpec as P

CLASSES = 81
STEP = 5
BETA_ONE = 0.5
BETA_TWO = 0.5
RATE = 0.02
DECAY = 0.01
EPSILON = 1e-08
BINS = 7
CHUNK = 8
STATIC = 4
WINDOW = 20
MORE = 4
SPANS = 17
LANES = 128
MIB = 2**20


def tent(where, cells):
    return 0.5 * sum(jnp.maximum(0.0, 1.0 - jnp.abs(w - cells)) for w in where)


def pool_kernel(channels, side, groups, copies, pick_ref, span_ref, feat_ref, table_ref, *refs):
    out_refs = refs[-7 - copies : -7]
    cols, rows, parts = refs[-7:-5], refs[-5:-3], refs[-3:-1]
    line_ref = refs[-1]
    image = pick_ref[0]
    half = LANES // 2
    offsets = (0.25, 0.75)
    cells = lax.broadcasted_iota(jnp.int32, (side, LANES), 0).astype(jnp.float32)
    bins = lax.broadcasted_iota(jnp.int32, (8, LANES), 0).astype(jnp.float32)

    def at(group):
        return (image * groups + group) * SPANS

    def param(group, k):
        return table_ref[group, k : k + 1, :]

    def weights(group, slot):
        top, x_start, x_step = param(group, 2), param(group, 4), param(group, 5)
        for j in range(BINS):
            where = [jnp.clip(x_start + (j + off) * x_step, 0.0, top) for off in offsets]
            weight = tent(where, cells)
            high = weight.astype(jnp.bfloat16)
            low = (weight - high.astype(jnp.float32)).astype(jnp.bfloat16)
            lanes = pl.ds(j * LANES, LANES)
            cols[slot][0:side, lanes] = high
            cols[slot][side : 2 * side, lanes] = high
            cols[slot][2 * side : 3 * side, lanes] = low
            cols[slot][3 * side : 4 * side, lanes] = low

    def fill(group, slot, row):
        y_start, y_step, top, base = (param(group, k) for k in range(4))
        where = [jnp.clip(y_start + (bins + off) * y_step, 0.0, top) for off in offsets]
        for h in range(CHUNK):
            rows[slot][row + h] = tent(where, (row + h).astype(jnp.float32) - base)
        place = pl.ds(pl.multiple_of(row * channels, channels), CHUNK * channels)
        left = feat_ref[place, :]
        left = jnp.concatenate([left, left], axis=1)
        parts[slot][place, :] = jnp.dot(left, cols[slot][...], preferred_element_type=jnp.float32)

    def rest(group, slot):
        first = span_ref[at(group)] + STATIC * CHUNK

        @pl.loop(0, span_ref[at(group) + 1])
        def _(t):
            fill(group, slot, first + t * CHUNK)

    def block(slot, i, low_row, count):
        accs = None
        for h in range(count):
            start = pl.multiple_of((low_row + h) * channels, channels)
            weight = jnp.broadcast_to(rows[slot][low_row + h, i : i + 1, :], (channels, LANES))
            new = [
                weight * parts[slot][pl.ds(start, channels), j * LANES : (j + 1) * LANES] for j in range(BINS)
            ]
            accs = new if accs is None else [x + y for x, y in zip(accs, new)]
        return accs

    def spot(i, j):
        return pl.ds(i * BINS + j, channels, stride=BINS * BINS)

    def work(group, slot, following, beside):
        for i in range(BINS):
            accs = block(slot, i, span_ref[at(group) + 3 + i], WINDOW)
            for j in range(BINS):
                line_ref[slot, spot(i, j), :] = accs[j]
            if beside and i < STATIC:
                fill(following, 1 - slot, span_ref[at(following)] + i * CHUNK)

        @pl.when(span_ref[at(group) + 2] > 0)
        def _():
            for i in range(BINS):
                low_row = span_ref[at(group) + 3 + i] + WINDOW

                @pl.loop(0, span_ref[at(group) + 3 + BINS + i])
                def _(t):
                    more = block(slot, i, low_row + t * MORE, MORE)
                    for j in range(BINS):
                        line_ref[slot, spot(i, j), :] = line_ref[slot, spot(i, j), :] + more[j]

    step = pl.program_id(0)

    @pl.when(step == 0)
    def _():
        weights(0, 0)
        for i in range(STATIC):
            fill(0, 0, span_ref[at(0)] + i * CHUNK)
        rest(0, 0)

    group = 2 * step
    weights(group + 1, 1)
    work(group, 0, group + 1, True)
    rest(group + 1, 1)

    @pl.when(group + 2 < groups)
    def _():
        weights(group + 2, 0)
        work(group + 1, 1, group + 2, True)
        rest(group + 2, 0)

    @pl.when(group + 2 >= groups)
    def _():
        work(group + 1, 1, group + 1, False)

    a, b = line_ref[0], line_ref[1]
    lanes = lax.broadcasted_iota(jnp.int32, a.shape, 1)
    new = [jnp.where(lanes < half, a, pltpu.roll(b, half, 1)), jnp.where(lanes < half, pltpu.roll(a, half, 1), b)]
    for out_ref in out_refs:
        for p in range(2):
            out_ref[p] = new[p].astype(jnp.bfloat16)


def pool(feat, table, spans, source, image, images, channels, buffer=None):
    depth = feat.shape[2]
    groups = table.shape[1]
    wide = channels * BINS * BINS
    side = depth // 2
    rows = sum(side >> k for k in range(4))
    boxes = groups * LANES // 2
    blocks = groups // 2
    pick = jnp.stack([source, image])
    out_shape = [jax.ShapeDtypeStruct((2, wide, images * boxes), jnp.bfloat16)]
    out_specs = [pl.BlockSpec((2, wide, LANES), lambda s, pick, spans: (0, 0, pick[1] * blocks + s))]
    in_specs = [
        pl.BlockSpec((None, rows * channels, depth), lambda s, pick, spans: (pick[0], 0, 0)),
        pl.BlockSpec((None, groups, 8, LANES), lambda s, pick, spans: (pick[0], 0, 0, 0)),
    ]
    operands = (pick, spans, feat, table)
    aliases = {}
    if buffer is None:
        out_shape.append(jax.ShapeDtypeStruct((2, wide, boxes), jnp.bfloat16))
        out_specs.append(pl.BlockSpec((2, wide, LANES), lambda s, pick, spans: (0, 0, s)))
    else:
        in_specs.append(pl.BlockSpec(memory_space=pl.ANY))
        operands += (buffer,)
        aliases = {4: 0}
    return pl.pallas_call(
        partial(pool_kernel, channels, side, groups, len(out_shape)),
        out_shape=out_shape,
        grid_spec=pltpu.PrefetchScalarGridSpec(
            num_scalar_prefetch=2,
            grid=(blocks,),
            in_specs=in_specs,
            out_specs=out_specs,
            scratch_shapes=[
                pltpu.VMEM((4 * side, BINS * LANES), jnp.bfloat16),
                pltpu.VMEM((4 * side, BINS * LANES), jnp.bfloat16),
                pltpu.VMEM((rows, 8, LANES), jnp.float32),
                pltpu.VMEM((rows, 8, LANES), jnp.float32),
                pltpu.VMEM((rows * channels, BINS * LANES), jnp.float32),
                pltpu.VMEM((rows * channels, BINS * LANES), jnp.float32),
                pltpu.VMEM((2, wide, LANES), jnp.float32),
            ],
        ),
        input_output_aliases=aliases,
        compiler_params=pltpu.CompilerParams(vmem_limit_bytes=60 * MIB),
        cost_estimate=pl.CostEstimate(
            flops=groups * 40 * channels * BINS * LANES * 8 * depth,
            bytes_accessed=80 * MIB,
            transcendentals=0,
        ),
        name="pool_rois",
    )(*operands)


def feature_rows(maps):
    side = maps[0].shape[-1]
    parts = [
        jnp.pad(m.transpose(0, 2, 1, 3), ((0, 0), (0, 0), (0, 0), (0, side - m.shape[-1])))
        for m in maps
    ]
    full = jnp.concatenate(parts, axis=1)
    high = lax.reduce_precision(full, 8, 7)
    low = (full - high).astype(jnp.bfloat16)
    full = jnp.concatenate([high.astype(jnp.bfloat16), low], axis=-1)
    return full.reshape(-1, 2 * side)


def box_order(boxes, levels, side):
    base = 2 * side - 2 * (side >> levels)
    key = ((boxes[..., 1] + boxes[..., 3]) >> levels) + base * 8
    key = key * key.shape[-1] + jnp.arange(key.shape[-1], dtype=jnp.int32)
    return jnp.sum((key[..., :, None] > key[..., None, :]).astype(jnp.int32), axis=-1)


def sort_boxes(boxes, levels, rank):
    count = boxes.shape[1]
    hot = (rank[:, None, :] == jnp.arange(count, dtype=jnp.int32)[:, None]).astype(jnp.bfloat16)
    both = jnp.concatenate([boxes, levels[..., None]], axis=-1).astype(jnp.bfloat16)
    return jnp.einsum("psr,prk->kps", hot, both, preferred_element_type=jnp.float32).astype(jnp.bfloat16)


def box_table(boxes, side):
    images, _, _, count = boxes.shape
    x0, y0, x1, y1, level = (boxes[:, k].astype(jnp.float32) for k in range(5))
    rows = sum(side >> k for k in range(4))
    scale = jnp.where(level < 0.5, 0.25, jnp.where(level < 1.5, 0.125, jnp.where(level < 2.5, 0.0625, 0.03125)))
    height = scale * (4 * side)
    base = 2.0 * side - 2.0 * height
    top = height - 1.0

    def axis(low, high):
        return low * scale - 0.5, ((high - low) * scale) / 7.0

    x_start, x_step = axis(x0, x1)
    y_start, y_step = axis(y0, y1)
    half = LANES // 2
    groups = count // half

    def split(v):
        return v.reshape(v.shape[:-1] + (groups, half))

    lows, highs = [], []
    for i in range(BINS):
        low = base + jnp.floor(jnp.clip(y_start + (i + 0.25) * y_step, 0.0, top))
        high = base + jnp.floor(jnp.clip(y_start + (i + 0.75) * y_step, 0.0, top)) + 1.0
        lows.append(jnp.min(split(low), axis=(1, 3)))
        highs.append(jnp.max(split(jnp.minimum(high, rows - 1.0)), axis=(1, 3)))
    low = jnp.stack(lows, axis=-1).astype(jnp.int32)
    high = jnp.stack(highs, axis=-1).astype(jnp.int32)
    least = jnp.min(low, axis=-1)
    chunks = jnp.maximum((jnp.max(high, axis=-1) - least + CHUNK) // CHUNK, STATIC)
    first = jnp.clip(rows - chunks * CHUNK, 0, least)
    extra = jnp.maximum(high - low + MORE - WINDOW, 0) // MORE
    low = jnp.minimum(low, (first + chunks * CHUNK)[..., None] - WINDOW - MORE * extra)
    heads = jnp.stack([first, chunks - STATIC, jnp.max(extra, axis=-1)], axis=-1)
    spans = jnp.concatenate([heads, low, extra], axis=-1).reshape(-1)
    zero = jnp.zeros_like(base)
    table = jnp.stack([split(v) for v in (y_start, y_step, top, base, x_start, x_step, zero, zero)])
    return table.transpose(1, 3, 0, 2, 4).reshape(images, groups, 8, LANES), spans


def adamw(weight, moment, second, grad):
    moment = BETA_ONE * moment + (1.0 - BETA_ONE) * grad
    second = BETA_TWO * second + (1.0 - BETA_TWO) * grad * grad
    fixed_m = moment / (1.0 - BETA_ONE**STEP)
    fixed_v = second / (1.0 - BETA_TWO**STEP)
    weight = weight - RATE * (fixed_m / (jnp.sqrt(fixed_v) + EPSILON) + DECAY * weight)
    return (weight, moment, second)


def update_kernel(pooled_ref, back_ref, w_ref, m_ref, v_ref, *outs):
    grad = jnp.dot(pooled_ref[...], back_ref[...], preferred_element_type=jnp.float32)
    new = adamw(w_ref[...], m_ref[...], v_ref[...], grad)
    for ref, value in zip(outs, new):
        ref[...] = value


def update_first(pooled, back, weight, moment, second):
    passes, wide, hidden = weight.shape
    boxes = pooled.shape[2]
    block = wide // BINS
    big = pl.BlockSpec((None, block, hidden), lambda p, b: (p, b, 0))
    return pl.pallas_call(
        update_kernel,
        out_shape=[jax.ShapeDtypeStruct(weight.shape, jnp.float32)] * 3,
        grid=(passes, BINS),
        in_specs=[
            pl.BlockSpec((None, block, boxes), lambda p, b: (p, b, 0)),
            pl.BlockSpec((None, boxes, hidden), lambda p, b: (p, 0, 0)),
            big,
            big,
            big,
        ],
        out_specs=[big] * 3,
        compiler_params=pltpu.CompilerParams(vmem_limit_bytes=60 * MIB),
        cost_estimate=pl.CostEstimate(
            flops=2 * passes * wide * hidden * boxes,
            bytes_accessed=passes * wide * hidden * 24 + passes * boxes * (wide + hidden) * 2,
            transcendentals=passes * wide * hidden,
        ),
        name="update_first",
    )(pooled, back, weight, moment, second)


def loss_and_slope(logits, box, count):
    place = lax.broadcasted_iota(jnp.int32, logits.shape, 1)
    is_class = place < CLASSES
    label = box[:, 0:1].astype(jnp.int32)
    weight = box[:, 1:2]
    top = jnp.max(jnp.where(is_class, logits, -jnp.inf), axis=1, keepdims=True)
    grown = jnp.where(is_class, jnp.exp(jnp.where(is_class, logits - top, 0.0)), 0.0)
    norm = jnp.sum(grown, axis=1, keepdims=True)
    hot = place == label
    picked = jnp.sum(jnp.where(hot, logits, 0.0), axis=1, keepdims=True)
    fore = jnp.where(label > 0, weight, 0.0)
    rows = weight * (top + jnp.log(norm) - picked)
    slope = weight * (grown / norm - jnp.where(hot, 1.0, 0.0))
    offset = place - (CLASSES + 4 * (label - 1))
    for k in range(4):
        mask = (offset == k) & (place >= CLASSES)
        chosen = jnp.sum(jnp.where(mask, logits, 0.0), axis=1, keepdims=True)
        differ = fore * (chosen - box[:, 2 + k : 3 + k])
        near = jnp.abs(differ)
        rows += jnp.where(near < 1.0, 0.5 * differ * differ, near - 0.5) * fore
        slope = jnp.where(mask, fore * jnp.clip(differ, -1.0, 1.0), slope)
    return rows, slope / count


def sigmoid(value):
    return 1.0 / (1.0 + jnp.exp(-value))


def head_kernel(
    images, parts, mine,
    part_ref, weight_ref, box_ref, count_ref,
    back_ref, grad_ref,
    sums, landed, own, counts, split, cols, kept,
    rs_send, rs_recv, ag_send, ag_recv, up_send, up_recv, down_send, down_recv, own_sem,
    count_send, count_recv, col_send, col_recv, kept_send, kept_recv,
):
    me = lax.axis_index("narrow")
    level = lax.axis_index("wide")
    bits = parts.bit_length() - 1
    turn = [(1 - 2 * ((me // 2**k) % 2)) * 2**k for k in range(bits)]

    def peer(mask):
        return me + sum((turn[k] for k in range(bits) if mask >> k & 1), 0)

    links = list(range(1, bits))
    orders = [links, links[::-1]]

    barrier = pltpu.get_barrier_semaphore()
    for mask in range(1, parts):
        pl.semaphore_signal(barrier, inc=1, device_id={"narrow": peer(mask)})
    for k in range(1, images):
        pl.semaphore_signal(barrier, inc=1, device_id={"wide": lax.rem(level + k, images)})
    pl.semaphore_wait(barrier, parts + images - 2)

    counting = []
    for k in range(1, images):
        counting.append(
            pltpu.make_async_remote_copy(
                src_ref=count_ref,
                dst_ref=counts.at[k],
                send_sem=count_send.at[k],
                recv_sem=count_recv.at[k],
                device_id={"wide": lax.rem(level + k, images)},
            )
        )

    def scatter(p, mask, bit, source):
        return pltpu.make_async_remote_copy(
            src_ref=source,
            dst_ref=landed.at[p, mask],
            send_sem=rs_send.at[p, mask],
            recv_sem=rs_recv.at[p, mask],
            device_id={"narrow": peer(1 << bit)},
        )

    def part_at(p, mask):
        return part_ref.at[p, pl.ds(pl.multiple_of(peer(mask) * mine, mine), mine), :]

    copies = {}
    for p in range(2):
        for mask in range(1, parts, 2):
            copies[p, mask] = scatter(p, mask, 0, part_at(p, mask))
            copies[p, mask].start()

    def stage(p, at):
        order = [0] + orders[p]
        bit = order[at - 1]
        seen = sum(1 << b for b in order[:at])
        for mask in range(parts):
            if mask & seen:
                continue
            copies[p, mask | 1 << bit].wait_recv()
            if at == 1:
                have = part_ref[p, pl.ds(pl.multiple_of(peer(mask) * mine, mine), mine), :]
            else:
                have = sums[p, mask]
            sums[p, mask] = have + landed[p, mask | 1 << bit]
            if at < bits and mask >> order[at] & 1:
                copies[p, mask] = scatter(p, mask, order[at], sums.at[p, mask])
                copies[p, mask].start()

    for copy in counting:
        copy.start()
    for at in range(1, bits):
        for p in range(2):
            stage(p, at)

    def rows(p, image, mask):
        place = (image * parts + peer(mask)) * mine
        return back_ref.at[p, pl.ds(pl.multiple_of(place, mine), mine), :]

    def hop(p, d, up, source=None):
        image = level - d if up else level + d
        spot = rows(p, image, 0)
        return pltpu.make_async_remote_copy(
            src_ref=spot if source is None else source,
            dst_ref=spot,
            send_sem=(up_send if up else down_send).at[p, d],
            recv_sem=(up_recv if up else down_recv).at[p, d],
            device_id={"wide": level + 1 if up else level - 1},
        )

    def came(p, d, up):
        image = level - d if up else level + d
        spot = rows(p, image, 0)
        pltpu.make_async_remote_copy(
            src_ref=spot, dst_ref=spot, send_sem=(up_send if up else down_send).at[p, d],
            recv_sem=(up_recv if up else down_recv).at[p, d - 1],
            device_id={"wide": level - 1 if up else level + 1},
        ).wait_recv()

    steps = [orders[p] + [0] for p in range(2)]

    def masks_before(p, at):
        seen = sum(1 << b for b in steps[p][:at])
        return [m for m in range(parts) if not m & ~seen]

    def doubling(spot, send, recv):
        def spread(p, key, mask, bit, source=None):
            there = mask | 1 << bit
            return pltpu.make_async_remote_copy(
                src_ref=spot(p, key, mask) if source is None else source,
                dst_ref=spot(p, key, mask),
                send_sem=send.at[p, key, there],
                recv_sem=recv.at[p, key, there],
                device_id={"narrow": peer(1 << bit)},
            )

        def arrive(p, key, at):
            for m in masks_before(p, at):
                there = m | 1 << steps[p][at]
                pltpu.make_async_remote_copy(
                    src_ref=spot(p, key, there),
                    dst_ref=spot(p, key, there),
                    send_sem=send.at[p, key, there],
                    recv_sem=recv.at[p, key, there],
                    device_id={"narrow": peer(1)},
                ).wait_recv()

        def advance(p, key, at, source=None):
            if at:
                arrive(p, key, at - 1)
            for m in masks_before(p, at):
                spread(p, key, m, steps[p][at], source if m == 0 else None).start()

        def sent(p, key):
            for at in range(bits):
                for m in masks_before(p, at):
                    spread(p, key, m, steps[p][at]).wait_send()

        return advance, arrive, sent

    advance, arrive, sent = doubling(rows, ag_send, ag_recv)
    advance_kept, arrive_kept, sent_kept = doubling(
        lambda p, key, mask: kept.at[p, peer(mask)], kept_send, kept_recv
    )

    def finish(p, image):
        arrive(p, image, bits - 1)
        sent(p, image)

    span = grad_ref.shape[1]

    def hand(p, mask):
        return pltpu.make_async_remote_copy(
            src_ref=split.at[p, :, peer(mask)],
            dst_ref=cols.at[p, :, me],
            send_sem=col_send.at[p, mask],
            recv_sem=col_recv.at[p, mask],
            device_id={"narrow": peer(mask)},
        )

    def handed(p, mask):
        spot = cols.at[p, :, peer(mask)]
        pltpu.make_async_remote_copy(
            src_ref=spot, dst_ref=spot, send_sem=col_send.at[p, mask], recv_sem=col_recv.at[p, mask],
            device_id={"narrow": peer(mask)},
        ).wait_recv()

    for copy in counting:
        copy.wait_recv()
    count = count_ref[0:1, 0:1] + sum(counts[k, 0:1, 0:1] for k in range(1, images))
    hidden = part_ref.shape[2]
    for p in range(2):
        stage(p, bits)
        pre1 = sums[p, 0]
        sig1 = sigmoid(pre1)
        hid1 = (pre1 * sig1).astype(jnp.bfloat16)
        pre2 = jnp.dot(hid1, weight_ref[p, :, :hidden], preferred_element_type=jnp.float32)
        sig2 = sigmoid(pre2)
        hid2 = (pre2 * sig2).astype(jnp.bfloat16)
        logits = jnp.dot(hid2, weight_ref[p, :, hidden:], preferred_element_type=jnp.float32)
        loss, slope = loss_and_slope(logits, box_ref[p], count)
        back_z = slope.astype(jnp.bfloat16)
        across = (((1,), (1,)), ((), ()))
        back_h2 = lax.dot_general(back_z, weight_ref[p, :, hidden:], across, preferred_element_type=jnp.float32)
        back_p2 = (back_h2 * (sig2 * (1.0 + pre2 * (1.0 - sig2)))).astype(jnp.bfloat16)
        back_h1 = lax.dot_general(back_p2, weight_ref[p, :, :hidden], across, preferred_element_type=jnp.float32)
        own[p] = (back_h1 * (sig1 * (1.0 + pre1 * (1.0 - sig1)))).astype(jnp.bfloat16)

        @pl.when(level < images - 1)
        def _():
            hop(p, 0, True, own.at[p]).start()

        @pl.when(level > 0)
        def _():
            hop(p, 0, False, own.at[p]).start()

        advance(p, level, 0, own.at[p])
        pltpu.make_async_copy(own.at[p], rows(p, level, 0), own_sem.at[p]).start()
        place = lax.broadcasted_iota(jnp.int32, back_z.shape, 1)
        shown = back_z.astype(jnp.float32)
        for k in range(3):
            near = loss.astype(jnp.bfloat16).astype(jnp.float32)
            shown = jnp.where(place == back_z.shape[1] - 1 - k, near, shown)
            loss = loss - near
        kept[p, me, :, :hidden] = back_p2
        kept[p, me, :, hidden:] = shown.astype(jnp.bfloat16)
        advance_kept(p, 0, 0)
        for owner in range(parts):
            split[p, 0, owner] = hid1[:, owner * span : (owner + 1) * span]
            split[p, 1, owner] = hid2[:, owner * span : (owner + 1) * span]
        for mask in range(1, parts):
            hand(p, mask).start()
    for p in range(2):
        pltpu.make_async_copy(own.at[p], rows(p, level, 0), own_sem.at[p]).wait()

    def each_side(d, do):
        @pl.when(level >= d)
        def _():
            do(level - d, True)

        @pl.when(level + d < images)
        def _():
            do(level + d, False)

    def enter(d):
        def do(image, up):
            for p in range(2):
                came(p, d, up)

                @pl.when((level < images - 1) if up else (level > 0))
                def _():
                    hop(p, d, up).start()

                advance(p, image, 0)

        each_side(d, do)

    def go_on(d, at):
        if d == 0:
            for p in range(2):
                advance(p, level, at)
                advance_kept(p, 0, at)
        else:

            def do(image, up):
                for p in range(2):
                    advance(p, image, at)

            each_side(d, do)

    for tick in range(1, images + bits - 1):
        for d in range(images):
            at = tick - d
            if at == 0:
                enter(d)
            elif 0 < at < bits:
                go_on(d, at)

    loss = jnp.zeros((1, 1), jnp.float32)
    for p in range(2):
        arrive_kept(p, 0, bits - 1)
        for mask in range(1, parts):
            handed(p, mask)
        for k in range(2):
            cols[p, k, me] = split[p, k, me]
        slopes = kept[p].reshape(parts * mine, kept.shape[3])
        down = (((0,), (0,)), ((), ()))
        for k, (start, stop) in enumerate(((0, hidden), (hidden, grad_ref.shape[2]))):
            left = cols[p, k].reshape(parts * mine, span)
            grad_ref[p, :, start:stop] = lax.dot_general(
                left, slopes[:, start:stop], down, preferred_element_type=jnp.float32
            )
        ends = slopes[:, grad_ref.shape[2] - LANES :].astype(jnp.float32)
        place = lax.broadcasted_iota(jnp.int32, ends.shape, 1)
        loss += jnp.sum(jnp.where(place >= LANES - 3, ends, 0.0), keepdims=True)
    corner = grad_ref[0, 0:8, grad_ref.shape[2] - LANES :]
    place = [lax.broadcasted_iota(jnp.int32, corner.shape, k) for k in range(2)]
    corner = jnp.where((place[0] == 0) & (place[1] == LANES - 1), loss, corner)
    grad_ref[0, 0:8, grad_ref.shape[2] - LANES :] = corner

    for p in range(2):
        finish(p, level)
        sent_kept(p, 0)
        for mask in range(1, parts):
            hand(p, mask).wait_send()

        @pl.when(level < images - 1)
        def _():
            hop(p, 0, True).wait_send()

        @pl.when(level > 0)
        def _():
            hop(p, 0, False).wait_send()

    for d in range(1, images):

        def do(image, up):
            for p in range(2):
                finish(p, image)

                @pl.when((level < images - 1) if up else (level > 0))
                def _():
                    hop(p, d, up).wait_send()

        each_side(d, do)
    for p in range(2):
        for mask in range(1, parts):
            copies[p, mask].wait_send()
    for copy in counting:
        copy.wait_send()


def head_step(part, weight, box, count, images, parts):
    passes, boxes, hidden = part.shape
    mine = boxes // parts
    outs = weight.shape[2] - hidden
    span = hidden // parts
    low = jnp.bfloat16
    vmem = pl.BlockSpec(memory_space=pltpu.VMEM)
    dma = pltpu.SemaphoreType.DMA
    return pl.pallas_call(
        partial(head_kernel, images, parts, mine),
        out_shape=[
            jax.ShapeDtypeStruct((passes, images * boxes, hidden), low),
            jax.ShapeDtypeStruct((passes, span, hidden + outs), jnp.float32),
        ],
        in_specs=[vmem] * 4,
        out_specs=[pl.BlockSpec(memory_space=pl.ANY), vmem],
        scratch_shapes=[
            pltpu.VMEM((passes, parts, mine, hidden), jnp.float32),
            pltpu.VMEM((passes, parts, mine, hidden), jnp.float32),
            pltpu.VMEM((passes, mine, hidden), low),
            pltpu.VMEM((images, 8, LANES), jnp.float32),
            pltpu.VMEM((passes, 2, parts, mine, span), low),
            pltpu.VMEM((passes, 2, parts, mine, span), low),
            pltpu.VMEM((passes, parts, mine, hidden + outs), low),
            dma((passes, parts)),
            dma((passes, parts)),
            dma((passes, images, parts)),
            dma((passes, images, parts)),
            dma((passes, images)),
            dma((passes, images)),
            dma((passes, images)),
            dma((passes, images)),
            dma((passes,)),
            dma((images,)),
            dma((images,)),
            dma((passes, parts)),
            dma((passes, parts)),
            dma((passes, 1, parts)),
            dma((passes, 1, parts)),
        ],
        compiler_params=pltpu.CompilerParams(
            vmem_limit_bytes=48 * MIB, collective_id=0, has_side_effects=True
        ),
        cost_estimate=pl.CostEstimate(
            flops=8 * passes * mine * hidden * (hidden + outs),
            bytes_accessed=100 * MIB,
            transcendentals=4 * passes * mine * hidden,
        ),
        name="head_step",
    )(part, weight, box, count)


def small_kernel(grad_ref, count_ref, *refs):
    hidden = refs[0].shape[2]
    outs = refs[3].shape[0]
    new = adamw(*(r[...] for r in refs[:3]), grad_ref[:, :, :hidden])
    for ref, value in zip(refs[6:9], new):
        ref[...] = value
    for p in range(grad_ref.shape[0]):
        grad = grad_ref[p, :, hidden:].T[:outs]
        new = adamw(*(r[:, p, :] for r in refs[3:6]), grad)
        for ref, value in zip(refs[9:12], new):
            ref[:, p, :] = value
    total = grad_ref[0, 0:1, grad_ref.shape[2] - 1 :]
    lane = lax.broadcasted_iota(jnp.int32, (8, LANES), 1)
    refs[12][...] = jnp.where(lane == 0, total, count_ref[...])


def update_small(grad, count, two, head):
    arrays = tuple(two) + tuple(x.transpose(2, 0, 1) for x in head)
    shapes = [jax.ShapeDtypeStruct(x.shape, jnp.float32) for x in arrays]
    out = pl.pallas_call(
        small_kernel,
        out_shape=shapes + [jax.ShapeDtypeStruct((8, LANES), jnp.float32)],
        compiler_params=pltpu.CompilerParams(vmem_limit_bytes=30 * MIB),
        name="update_small",
    )(grad, jnp.full((8, LANES), count), *arrays)
    return (out[6][0, :2],), out[:3], tuple(x.transpose(1, 2, 0) for x in out[3:6])


def per_device(
    feat_p2, feat_p3, feat_p4, feat_p5, rois, levels, labels, sampled, targets,
    fc1_w, fc1_m, fc1_v, fc2_w, fc2_m, fc2_v, head_w, head_m, head_v,
):
    side = feat_p2.shape[-1]
    channels = feat_p2.shape[1]
    boxes = rois.shape[2]
    images = lax.axis_size("wide")
    mine = boxes // lax.axis_size("narrow")
    first = lax.axis_index("narrow") * mine
    level = lax.axis_index("wide").astype(jnp.int32)
    parts = lax.axis_size("narrow")
    hidden = fc2_w.shape[2]
    outs = head_w.shape[2]
    zero = jnp.zeros((), jnp.int32)
    rank = box_order(rois[:, 0], levels[:, 0], side)
    ordered = sort_boxes(rois[:, 0], levels[:, 0], rank)
    feat = feature_rows((feat_p2, feat_p3, feat_p4, feat_p5))
    height = feat.shape[0]
    flags = sampled[:, 0].astype(jnp.bfloat16).reshape(1, 2, boxes)
    both = jnp.concatenate([feat, jnp.concatenate([ordered, flags]).reshape(-1, LANES)])
    weight = jnp.concatenate([fc2_w, jnp.pad(head_w, ((0, 0), (0, 0), (0, -outs % LANES)))], axis=2)
    weight = lax.all_gather(weight.astype(jnp.bfloat16), "narrow", axis=1, tiled=True)
    counted = jnp.sum(sampled).astype(jnp.float32)
    table, spans = box_table(ordered[None], side)
    pooled, own = pool(feat[None], table, spans, zero, level, images, channels)
    w1 = fc1_w.astype(jnp.bfloat16)
    part = lax.dot_general(own, w1, (((1,), (1,)), ((0,), (0,))), preferred_element_type=jnp.float32)
    both, weight, part = lax.optimization_barrier((both, weight, part))
    feats = lax.all_gather(both, "wide", axis=0)
    hot = rank[:, None, :] == first + jnp.arange(mine, dtype=jnp.int32)[:, None]

    def pick(values):
        return jnp.sum(jnp.where(hot, values[:, 0].astype(jnp.float32)[:, None, :], 0), axis=-1)

    box = [pick(labels), pick(sampled)] + [pick(targets[..., k]) for k in range(4)]
    box = jnp.pad(jnp.stack(box, axis=-1), ((0, 0), (0, 0), (0, LANES - 6)))
    back, grad = head_step(part, weight, box, jnp.full((8, LANES), counted), images, parts)
    grad = lax.psum_scatter(grad, "wide", scatter_dimension=1, tiled=True)

    tails = feats[:, height:].reshape(images, 6, 2, boxes)
    count = jnp.sum(tails[:, 5].astype(jnp.float32))
    tables, all_spans = box_table(tails[:, :5], side)
    turn = [lax.rem(level + k, images) for k in range(1, images)]
    for k in range(images - 1):
        pooled = pool(feats, tables, all_spans, turn[k], turn[k], images, channels, pooled)[0]
        if k == max(images - 3, 0):
            grad, pooled = lax.optimization_barrier((grad, pooled))
            grad = lax.all_gather(grad, "wide", axis=1, tiled=True)
    new1 = update_first(pooled, back, fc1_w, fc1_m, fc1_v)
    grad, new1 = lax.optimization_barrier((grad, new1))
    losses, new2, newh = update_small(grad, count, (fc2_w, fc2_m, fc2_v), (head_w, head_m, head_v))
    return losses + tuple(new1) + tuple(new2) + tuple(newh)


def solution(mesh):
    maps = P("wide", "narrow", None, None)
    rows = P(None, "narrow", None)
    box = P(None, "wide", None)
    coords = P(None, "wide", None, None)
    return jax.shard_map(
        per_device,
        mesh=mesh,
        in_specs=(maps,) * 4 + (coords, box, box, box, coords) + (rows,) * 9,
        out_specs=(P(),) + (rows,) * 9,
        check_vma=False,
    )
```
